128 devices in a mesh: section: 4 (over y_lo, core), seq: 32 (over z, y_hi, x).
Axes of the slice: x: 4, y: 4 (y_hi: 2, y_lo: 2; y = y_hi * 2 + y_lo), z: 4, core: 2. Of those that a mesh axis runs over, the one named last changes fastest.
Arguments:
- hidden_in: bfloat16 [4, 4096, 8192], P('section', 'seq'), may hold values from -64 to 64
- saved_hidden: bfloat16 [4, 4096, 8192], P('section', 'seq'), may hold values from -64 to 64
- grad_in: bfloat16 [4, 4096, 8192], P('section', 'seq'), may hold values from -6 to 6
- norm_gain: float32 [4, 8192], P('section'), may hold values from 0.25 to 1.75
- w_query: bfloat16 [4, 8192, 512], P('section', 'seq'), may hold values from -1 to 1
- w_key: bfloat16 [4, 8192, 128], P('section', 'seq'), may hold values from -1 to 1
- w_value: bfloat16 [4, 8192, 128], P('section', 'seq'), may hold values from -0.0625 to 0.0625
- w_out: bfloat16 [4, 512, 8192], P('section', 'seq'), may hold values from -0.25 to 0.25
- head: float32 [8192], replicated, may hold values from -0.0625 to 0.0625
- block_table: int32 [16], replicated, may hold values from 0 to 15, each once
- resp_lengths: int32 [8], replicated, may hold values from 1 to 256, 1536 in all
- pairs: int32 [28, 2], replicated, may hold values from 0 to 7, as said below
Outputs:
- next_hidden: bfloat16 [4, 4096, 8192], P('section', 'seq')
- prev_grad: bfloat16 [4, 4096, 8192], P('section', 'seq')
The draws below stay inside these ranges and needn't reach their ends.
Inputs may be any that keep to these rules, and one draw needn't show every extreme that they name: `block_table`: each of the 16 prompt blocks appears once. `resp_lengths`: the longest response fills all 256 slots. `pairs`: each unordered pair of two different responses appears exactly once; the first entry is the preferred response.
All inputs are finite; a program needn't handle non-finite values.
Results may differ from the reference program's by a relative error of at most 0.04.
Values may be sent and summed in bfloat16 or wider, within the bound.
A program may use at most 128 MiB of HBM per device.

```python
import math
import jax
import jax.numpy as jnp
import numpy as np
from jax import lax

D = 8192
HD = 128
QH = 4
RESP = 8
BLK = 128
SECTIONS = 4
TOKENS = 4096
PROMPT = 2048
RLEN = 256
PBLK = 16
PAIRS = 28


def activation(key, salt):
    key = jax.random.fold_in(key, salt)
    key_rows, key_cols, key_vals = jax.random.split(key, 3)
    row_scale = jnp.exp(jax.random.uniform(key_rows, (SECTIONS, TOKENS, 1), minval=math.log(0.3), maxval=math.log(3.0)))
    col_scale = jnp.exp(jax.random.uniform(key_cols, (SECTIONS, 1, D), minval=math.log(0.5), maxval=math.log(2.0)))
    values = jnp.clip(jax.random.normal(key_vals, (SECTIONS, TOKENS, D)), -4.0, 4.0)
    result = values * row_scale * col_scale
    return result.astype(jnp.bfloat16)


def draw_hidden_in(key, part):
    return activation(key, 21)


def draw_saved_hidden(key, part):
    return activation(key, 22)


def projection(key, salt, width):
    key = jax.random.fold_in(key, salt)
    spread = math.sqrt(2.0 / D)
    values = jnp.clip(jax.random.normal(key, (SECTIONS, D, width)), -4.0, 4.0) * spread
    return values.astype(jnp.bfloat16)


def draw_w_query(key, part):
    return projection(key, 31, QH * HD)


def draw_w_key(key, part):
    return projection(key, 32, HD)


def draw_pairs(key, part):
    key = jax.random.fold_in(key, 41)
    key_flip, key_order = jax.random.split(key)
    lower, upper = jnp.triu_indices(RESP, 1)
    lower = lower.astype(jnp.int32)
    upper = upper.astype(jnp.int32)
    flip = jax.random.randint(key_flip, (PAIRS,), 0, 2)
    preferred = jnp.where(flip == 1, upper, lower)
    rejected = jnp.where(flip == 1, lower, upper)
    order = jax.random.permutation(key_order, PAIRS)
    return jnp.stack([preferred, rejected], axis=1)[order].astype(jnp.int32)


def block_scale(stream_key, shape, pieces, smallest, high):
    def one(axis_at, shards_of):
        heights = jax.random.uniform(jax.random.fold_in(jax.random.fold_in(stream_key, 6), axis_at), (shards_of,), jnp.float32, smallest / len(pieces), high / len(pieces))
        return jnp.repeat(jnp.exp(heights), shape[axis_at] // shards_of).reshape((-1,) + (1,) * (len(shape) - axis_at - 1))

    loudness = one(*pieces[0])
    for cut in pieces[1:]:
        loudness = loudness * one(*cut)
    return loudness


def split_up(number_of, total, limit, skew):
    loads = [(1 << 20) // math.isqrt(standing ** skew) + 1 for standing in range(2, number_of + 1)]
    rest, holding = total - limit - (number_of - 1), [1] * (number_of - 1)
    while rest > 0:
        movable = [i for i in range(number_of - 1) if holding[i] < limit]
        whole, left = sum([loads[i] for i in movable]), rest
        for i in movable:
            extra = min(limit - holding[i], max(1, left * loads[i] // whole), rest)
            holding[i] = holding[i] + extra
            rest = rest - extra
    return np.array([limit] + holding)


def ragged(rng, number_of, total, bound, skew):
    if number_of == 2:
        one = jax.random.randint(rng, (), max(1, total - bound), min(bound, total - 1) + 1)
        return jnp.stack([one, total - one])
    tallies = jnp.asarray(split_up(number_of, total, bound, skew), jnp.int32)
    pairs = (number_of - 1) // 2
    giver, sink = tallies[1:1 + 2 * pairs:2], tallies[2:2 + 2 * pairs:2]
    room = jnp.minimum(giver - 1, bound - sink)
    passed = jax.random.randint(jax.random.fold_in(rng, 1), (pairs,), 0, 1 << 20) % (room + 1)
    tallies = tallies.at[1:1 + 2 * pairs:2].set(giver - passed).at[2:2 + 2 * pairs:2].set(sink + passed)
    return tallies[jax.random.permutation(jax.random.fold_in(rng, 2), number_of)]


def gaussian(rng, extent, scale, reach, cuts=(), held_as=jnp.bfloat16):
    values = jax.random.normal(rng, extent, jnp.float32) * scale
    if len(cuts) > 0:
        values = block_scale(rng, extent, cuts, -0.22, 0.18) * values
    return jnp.clip(values, min=-reach, max=reach).astype(held_as)


def setup_inputs(seed: int = 0) -> dict:
    splits = jax.random.split(jax.random.key(seed), 13)
    hidden_in = draw_hidden_in(jax.random.fold_in(splits[12], 71), 0)
    saved_hidden = draw_saved_hidden(jax.random.fold_in(splits[12], 71), 0)
    grad_in = gaussian(splits[2], (SECTIONS, TOKENS, D), 1.0, 6.0, ((0, 4), (1, 32)))
    norm_gain = jnp.clip(1.0 + 0.15 * jax.random.normal(splits[3], (SECTIONS, D), jnp.float32), 0.25, 1.75)
    w_query = draw_w_query(jax.random.fold_in(splits[12], 71), 0)
    w_key = draw_w_key(jax.random.fold_in(splits[12], 71), 0)
    w_value = gaussian(splits[6], (SECTIONS, D, HD), D ** -0.5, 0.0625, ((0, 4), (1, 32)))
    w_out = gaussian(splits[7], (SECTIONS, QH * HD, D), (QH * HD) ** -0.5, 0.25, ((0, 4), (1, 32)))
    head = gaussian(splits[8], (D,), D ** -0.5, 0.0625, (), jnp.float32)
    block_table = jax.random.permutation(splits[9], PBLK).astype(jnp.int32)
    resp_lengths = ragged(splits[10], RESP, RESP * RLEN * 3 // 4, RLEN, 1).astype(jnp.int32)
    pairs = draw_pairs(jax.random.fold_in(splits[12], 71), 0)
    return {"hidden_in": hidden_in, "saved_hidden": saved_hidden, "grad_in": grad_in, "norm_gain": norm_gain, "w_query": w_query, "w_key": w_key, "w_value": w_value, "w_out": w_out, "head": head, "block_table": block_table, "resp_lengths": resp_lengths, "pairs": pairs}


EPSILON = 1e-05
ROPE_BASE = 500000.0
LOSS_SCALE = 1024.0
NEGATIVE = -1e+30

def rounded(value):
    return lax.optimization_barrier(value.astype(jnp.bfloat16))

def describe(indices, block_table, resp_lengths, prompt_len, answer_len):
    prompt_blocks = prompt_len // BLK
    in_prompt = indices < prompt_len
    block_of = jnp.clip(indices // BLK, 0, prompt_blocks - 1)
    table_hit = block_of[:, None] == jnp.arange(prompt_blocks, dtype=jnp.int32)[None, :]
    logical = lax.optimization_barrier(jnp.sum(jnp.where(table_hit, block_table[None, :], 0), axis=1))
    offset = jnp.maximum(indices - prompt_len, 0)
    answer = jnp.clip(offset // answer_len, 0, RESP - 1)
    within = offset % answer_len
    answer_hit = answer[:, None] == jnp.arange(RESP, dtype=jnp.int32)[None, :]
    length = lax.optimization_barrier(jnp.sum(jnp.where(answer_hit, resp_lengths[None, :], 0), axis=1))
    position = jnp.where(in_prompt, logical * BLK + indices % BLK, prompt_len + within)
    segment = jnp.where(in_prompt, -1, answer)
    usable = jnp.logical_or(in_prompt, within < length)
    return (position.astype(jnp.int32), segment.astype(jnp.int32), usable)

def visible(query_info, key_info):
    query_pos, query_seg, _ = query_info
    key_pos, key_seg, key_use = key_info
    causal = key_pos[None, :] <= query_pos[:, None]
    from_prompt = jnp.logical_and(key_seg[None, :] < 0, jnp.logical_or(query_seg[:, None] >= 0, causal))
    same_answer = jnp.logical_and(key_seg[None, :] == query_seg[:, None], causal)
    return jnp.logical_and(key_use[None, :], jnp.logical_or(from_prompt, same_answer))

def rotate(values, position, direction):
    half_width = values.shape[-1] // 2
    frequency = ROPE_BASE ** (-2.0 * jnp.arange(half_width, dtype=jnp.float32) / values.shape[-1])
    angles = position.astype(jnp.float32)[:, None] * frequency[None, :]
    cosine = jnp.cos(angles)[:, None, :]
    sine_part = direction * jnp.sin(angles)[:, None, :]
    lower_half = values[..., :half_width]
    upper_half = values[..., half_width:]
    return jnp.concatenate([lower_half * cosine - upper_half * sine_part, upper_half * cosine + lower_half * sine_part], axis=-1)

def normalize(hidden, gain_row):
    widened = hidden.astype(jnp.float32)
    inv_rms = lax.rsqrt(lax.optimization_barrier(jnp.mean(widened * widened, axis=1, keepdims=True)) + EPSILON)
    return (inv_rms, widened * inv_rms * gain_row[None, :])

def layer_forward(hidden, gain_row, w_q, w_k, w_v, info):
    position = info[0]
    inv_rms, scaled = normalize(hidden, gain_row)
    normed = rounded(scaled)
    head_count = w_q.shape[1] // HD
    queries = rounded(rotate(jnp.dot(normed, w_q, preferred_element_type=jnp.float32).reshape(TOKENS, head_count, HD), position, 1.0))
    key_part = rotate(jnp.dot(normed, w_k, preferred_element_type=jnp.float32)[:, None, :], position, 1.0)[:, 0, :]
    value_part = jnp.dot(normed, w_v, preferred_element_type=jnp.float32)
    pairs_kv = rounded(jnp.concatenate([key_part, value_part], axis=1))
    key_rows = pairs_kv[:, :HD].astype(jnp.float32)
    value_rows = pairs_kv[:, HD:].astype(jnp.float32)
    block_rows = min(512, TOKENS)

    def one_block(offset):
        query_block = lax.dynamic_slice_in_dim(queries, offset, block_rows, 0).astype(jnp.float32)
        query_info = tuple((lax.dynamic_slice_in_dim(element, offset, block_rows, 0) for element in info))
        allowed = visible(query_info, info)[None]
        scores = jnp.einsum('qhd,kd->hqk', query_block, key_rows) * HD ** (-0.5)
        scores = jnp.where(allowed, scores, NEGATIVE)
        row_max = lax.optimization_barrier(jnp.max(scores, axis=2))
        weights = jnp.where(allowed, jnp.exp(scores - row_max[:, :, None]), 0.0)
        denominator = lax.optimization_barrier(jnp.sum(weights, axis=2))
        weighted = jnp.einsum('hqk,kd->hqd', rounded(weights).astype(jnp.float32), value_rows)
        return (row_max, denominator, weighted / denominator[:, :, None])
    starts = jnp.arange(TOKENS // block_rows, dtype=jnp.int32) * block_rows
    row_max, denominator, mixed = lax.map(one_block, starts)
    row_max = jnp.transpose(row_max, (1, 0, 2)).reshape(head_count, TOKENS)
    denominator = jnp.transpose(denominator, (1, 0, 2)).reshape(head_count, TOKENS)
    mixed = rounded(jnp.transpose(mixed, (0, 2, 1, 3)).reshape(TOKENS, head_count * HD))
    return (inv_rms, queries, pairs_kv, mixed, row_max, denominator)

def layer_output(hidden, mixed, w_o):
    return rounded(jnp.dot(mixed, w_o, preferred_element_type=jnp.float32) + hidden.astype(jnp.float32))

def loss_cotangent(layer_out, head, resp_lengths, pairs):
    end_rows = PROMPT + jnp.arange(RESP, dtype=jnp.int32) * RLEN + resp_lengths - 1
    output_wide = layer_out[end_rows].astype(jnp.float32)
    inv_rms = lax.rsqrt(lax.optimization_barrier(jnp.mean(output_wide * output_wide, axis=1, keepdims=True)) + EPSILON)
    rewards = lax.optimization_barrier(jnp.sum(output_wide * inv_rms * head[None, :], axis=1))
    margin = rewards[pairs[:, 1]] - rewards[pairs[:, 0]]
    pressure = jax.nn.sigmoid(margin) * (LOSS_SCALE / PAIRS)
    reward_grad = jnp.zeros((RESP,), jnp.float32).at[pairs[:, 1]].add(pressure).at[pairs[:, 0]].add(-pressure)
    slope = inv_rms * head[None, :] - output_wide * inv_rms ** 3 * lax.optimization_barrier(jnp.mean(output_wide * head[None, :], axis=1, keepdims=True))
    return rounded(jnp.zeros((TOKENS, D), jnp.float32).at[end_rows].set(reward_grad[:, None] * slope))

def layer_backward(hidden, cotangent, gain_row, w_q, w_k, w_v, w_o, info):
    inv_rms, queries, pairs_kv, mixed, row_max, denominator = layer_forward(hidden, gain_row, w_q, w_k, w_v, info)
    position = info[0]
    head_count = queries.shape[1]
    key_rows = pairs_kv[:, :HD].astype(jnp.float32)
    value_rows = pairs_kv[:, HD:].astype(jnp.float32)
    d_mixed = rounded(jnp.dot(cotangent, w_o.T, preferred_element_type=jnp.float32))
    d_heads = d_mixed.reshape(TOKENS, head_count, HD).astype(jnp.float32)
    row_dots = lax.optimization_barrier(jnp.sum(d_heads * mixed.reshape(TOKENS, head_count, HD).astype(jnp.float32), axis=2)).T
    block_rows = min(512, TOKENS)

    def advance(running, offset):
        d_key, d_value = running
        query_block = lax.dynamic_slice_in_dim(queries, offset, block_rows, 0).astype(jnp.float32)
        grad_block = lax.dynamic_slice_in_dim(d_heads, offset, block_rows, 0)
        dots_block = lax.dynamic_slice_in_dim(row_dots, offset, block_rows, 1)
        max_block = lax.dynamic_slice_in_dim(row_max, offset, block_rows, 1)
        denom_block = lax.dynamic_slice_in_dim(denominator, offset, block_rows, 1)
        query_info = tuple((lax.dynamic_slice_in_dim(element, offset, block_rows, 0) for element in info))
        allowed = visible(query_info, info)[None]
        scores = jnp.where(allowed, jnp.einsum('qhd,kd->hqk', query_block, key_rows) * HD ** (-0.5), NEGATIVE)
        probs = jnp.where(allowed, jnp.exp(scores - max_block[:, :, None]) / denom_block[:, :, None], 0.0)
        d_probs = jnp.einsum('qhd,kd->hqk', grad_block, value_rows)
        d_scores = rounded(probs * (d_probs - dots_block[:, :, None])).astype(jnp.float32)
        d_query = jnp.einsum('hqk,kd->qhd', d_scores, key_rows) * HD ** (-0.5)
        d_key = d_key + jnp.einsum('hqk,qhd->kd', d_scores, query_block) * HD ** (-0.5)
        d_value = d_value + jnp.einsum('hqk,qhd->kd', rounded(probs).astype(jnp.float32), grad_block)
        return ((d_key, d_value), d_query)
    starts = jnp.arange(TOKENS // block_rows, dtype=jnp.int32) * block_rows
    empty = jnp.zeros((TOKENS, HD), jnp.float32)
    (d_key, d_value), d_query = lax.scan(advance, (empty, empty), starts)
    d_query = d_query.reshape(TOKENS, head_count, HD)
    back_query = rounded(rotate(d_query, position, -1.0).reshape(TOKENS, head_count * HD))
    back_key = rounded(rotate(d_key[:, None, :], position, -1.0)[:, 0, :])
    back_value = rounded(d_value)
    d_normed = jnp.dot(back_query, w_q.T, preferred_element_type=jnp.float32)
    d_normed = d_normed + jnp.dot(back_key, w_k.T, preferred_element_type=jnp.float32)
    d_normed = d_normed + jnp.dot(back_value, w_v.T, preferred_element_type=jnp.float32)
    scaled_grad = d_normed * gain_row[None, :]
    widened = hidden.astype(jnp.float32)
    result = cotangent.astype(jnp.float32) + inv_rms * scaled_grad - widened * inv_rms ** 3 * lax.optimization_barrier(jnp.mean(scaled_grad * widened, axis=1, keepdims=True))
    return result.astype(jnp.bfloat16)

def reference(hidden_in, saved_hidden, grad_in, norm_gain, w_query, w_key, w_value, w_out, head, block_table, resp_lengths, pairs):
    info = describe(jnp.arange(TOKENS, dtype=jnp.int32), block_table, resp_lengths, PROMPT, RLEN)
    empty = jnp.zeros((TOKENS, D), jnp.bfloat16)
    forwards = [empty]
    backwards = []
    for section in range(SECTIONS):
        parts = layer_forward(hidden_in[section], norm_gain[section], w_query[section], w_key[section], w_value[section], info)
        layer_out = layer_output(hidden_in[section], parts[3], w_out[section])
        if section < SECTIONS - 1:
            forwards.append(layer_out)
            source = saved_hidden[section]
            cotangent = grad_in[section]
        else:
            source = hidden_in[section]
            cotangent = loss_cotangent(layer_out, head, resp_lengths, pairs)
        backwards.append(layer_backward(source, cotangent, norm_gain[section], w_query[section], w_key[section], w_value[section], w_out[section], info))
    next_hidden = jnp.stack(forwards)
    prev_grad = jnp.stack(backwards[1:] + [empty])
    return (next_hidden, prev_grad)
```

```python
import functools
import math

import jax
import jax.numpy as jnp
from jax import lax
from jax.experimental import pallas as pl
from jax.experimental.pallas import tpu as pltpu
from jax.sharding import PartitionSpec as P

HD = 128
QH = 4
RESP = 8
BLK = 128
D = 8192
ROWS = 128
SEQ = 32
PBLK = 16
PROMPT = 2048
RLEN = 256
QKV = 768
EPSILON = 1e-05
ROPE_BASE = 500000.0
LOSS_SCALE = 1024.0
NEGATIVE = -1e30
FAR = 1 << 30
SCALE = HD**-0.5
LOG2 = SCALE / math.log(2.0)
OUT_COLS = 1024
OUT_STEPS = D // OUT_COLS
BACK_COLS = 512
BACK_STEPS = D // BACK_COLS

f32 = jnp.float32
bf16 = jnp.bfloat16

ORDER = ((0, 0), (1, 0), (0, 1), (0, 3), (1, 1), (1, 3), (0, 2), (1, 2))


def nt(a, b):
    return lax.dot_general(a, b, (((1,), (1,)), ((), ())), preferred_element_type=f32)


def tn(a, b):
    return lax.dot_general(a, b, (((0,), (0,)), ((), ())), preferred_element_type=f32)


def nn(a, b):
    return jnp.dot(a, b, preferred_element_type=f32)


class Place:
    def __init__(self):
        self.seq = lax.axis_index("seq")
        self.z = self.seq // 8
        self.y = (self.seq // 4) % 2
        self.x = self.seq % 4

    def at(self, dz=0, dy=0, dx=0):
        return ((self.z + dz) % 4) * 8 + ((self.y + dy) % 2) * 4 + (self.x + dx) % 4


class Gather:
    def __init__(self, place, view, send_sems, recv_sems, only=None):
        self.place, self.view, self.only = place, view, only
        self.send_sems, self.recv_sems = send_sems, recv_sems
        self.sent = []
        self.slots = {}
        for part in range(2):
            for dy, da in ORDER:
                for db in (0, 1, 3, 2):
                    for sub in (0, 1) if (da == 2 and db == 0) or db == 2 else (0,):
                        if (dy, da, db) != (0, 0, 0):
                            self.slots[(part, dy, da, db, sub)] = len(self.slots)

    def origin(self, part, dy, da, db):
        dx, dz = (da, db) if part == 0 else (db, da)
        return self.place.at(dz, dy, dx)

    def guard(self, part, da, db, action):
        if self.only is None:
            action()
        else:
            dz = db if part == 0 else da
            pl.when(self.only((self.place.z + dz) % 4))(action)

    def piece(self, part, dy, da, db, sub):
        return self.view(self.origin(part, dy, da, db), part, sub)

    def push(self, part, dy, da, db, axis, step, sub=None):
        if axis == "y":
            target, key = self.place.at(0, 1, 0), (part, 1 - dy, da, db, 0)
        else:
            along_x = (axis == "a") == (part == 0)
            target = self.place.at(0, 0, step) if along_x else self.place.at(step, 0, 0)
            if axis == "a":
                key = (part, dy, (da - step) % 4, db, sub or 0)
            else:
                key = (part, dy, da, (db - step) % 4, sub or 0)
        ref = self.piece(part, dy, da, db, sub)
        number = len(self.sent)
        copy = pltpu.make_async_remote_copy(
            src_ref=ref,
            dst_ref=ref,
            send_sem=self.send_sems.at[number] if self.only else self.send_sems.at[0],
            recv_sem=self.recv_sems.at[self.slots[key]],
            device_id={"seq": target},
            device_id_type=pl.DeviceIdType.MESH,
        )
        self.sent.append((part, da, db, copy))
        self.guard(part, da, db, copy.start)

    def take(self, part, dy, da, db, sub=None):
        ref = self.piece(part, dy, da, db, sub)
        copy = pltpu.make_async_remote_copy(
            src_ref=ref,
            dst_ref=ref,
            send_sem=self.send_sems.at[0],
            recv_sem=self.recv_sems.at[self.slots[(part, dy, da, db, sub or 0)]],
            device_id={"seq": self.place.at(0, 1, 0)},
            device_id_type=pl.DeviceIdType.MESH,
        )
        self.guard(part, da, db, copy.wait_recv)

    def begin(self):
        for part in range(2):
            self.push(part, 0, 0, 0, "y", 1)
        for part in range(2):
            for axis in ("a", "b"):
                for step in (1, -1):
                    self.push(part, 0, 0, 0, axis, step)

    def first(self, part, k):
        dy, da = ORDER[k]
        if (dy, da) == (0, 0):
            return
        if da == 2:
            self.take(part, dy, 2, 0, 0)
            self.take(part, dy, 2, 0, 1)
        else:
            self.take(part, dy, da, 0)
            if da == 0:
                self.push(part, dy, 0, 0, "a", 1)
                self.push(part, dy, 0, 0, "a", -1)
            elif da == 1:
                self.push(part, dy, 1, 0, "a", -1, 1)
            else:
                self.push(part, dy, 3, 0, "a", 1, 0)
        self.push(part, dy, da, 0, "b", 1)
        self.push(part, dy, da, 0, "b", -1)

    def second(self, part, k):
        dy, da = ORDER[k]
        self.take(part, dy, da, 1)
        self.push(part, dy, da, 1, "b", -1, 1)
        self.take(part, dy, da, 3)
        self.push(part, dy, da, 3, "b", 1, 0)

    def third(self, part, k):
        dy, da = ORDER[k]
        self.take(part, dy, da, 2, 0)
        self.take(part, dy, da, 2, 1)

    def steps(self):
        count = len(ORDER)
        for k in range(count + 2):
            here = []
            for part in range(2):
                if k < count:
                    self.first(part, k)
            for part in range(2):
                if 1 <= k <= count:
                    self.second(part, k - 1)
                    dy, da = ORDER[k - 1]
                    here += [(part, self.origin(part, dy, da, db)) for db in (0, 1, 3)]
                if k >= 2:
                    self.third(part, k - 2)
                    dy, da = ORDER[k - 2]
                    here.append((part, self.origin(part, dy, da, 2)))
            yield here

    def finish(self, whole=None):
        if self.only is None:
            pltpu.make_async_remote_copy(
                src_ref=whole,
                dst_ref=whole,
                send_sem=self.send_sems.at[0],
                recv_sem=self.recv_sems.at[0],
                device_id={"seq": self.place.at(0, 1, 0)},
                device_id_type=pl.DeviceIdType.MESH,
            ).wait_send()
        else:
            for part, da, db, copy in self.sent:
                self.guard(part, da, db, copy.wait_send)


def layer_kernel(
    scalars,
    hid_hbm,
    sav_hbm,
    gin_hbm,
    wq_hbm,
    wk_hbm,
    wv_hbm,
    wo_hbm,
    gain,
    head,
    cosine,
    sine,
    sign,
    nh_hbm,
    pg_hbm,
    hid,
    src,
    cot,
    xn,
    wqkv,
    wout,
    acc,
    queries,
    kv,
    mixed,
    layer_out,
    dheads,
    dkv,
    landed,
    tile,
    tiles,
    back,
    grad,
    zero,
    load_sems,
    wqkv_send,
    wqkv_recv,
    wout_send,
    wout_recv,
    kv_send,
    kv_recv,
    pair_sems,
    rs_send,
    rs_recv,
    tile_send,
    tile_recv,
    next_send,
    next_recv,
    prev_send,
    prev_recv,
    zero_sems,
):
    place = Place()
    seq = place.seq
    section = lax.axis_index("section")
    is_last = section == 3
    parity = seq % 2
    partner = seq + 1 - 2 * parity
    in_prompt = seq < PBLK

    def other(index):
        return {"seq": index}

    loads = [
        pltpu.make_async_copy(wq_hbm, wqkv.at[seq, :, pl.ds(0, 512)], load_sems.at[0]),
        pltpu.make_async_copy(wk_hbm, wqkv.at[seq, :, pl.ds(512, 128)], load_sems.at[1]),
        pltpu.make_async_copy(wv_hbm, wqkv.at[seq, :, pl.ds(640, 128)], load_sems.at[2]),
        pltpu.make_async_copy(hid_hbm, hid, load_sems.at[3]),
        pltpu.make_async_copy(wo_hbm, wout.at[seq], load_sems.at[4]),
        pltpu.make_async_copy(gin_hbm, cot, load_sems.at[5]),
    ]
    for load in loads[:4]:
        load.start()
    saved_load = pltpu.make_async_copy(sav_hbm, src, load_sems.at[6])
    again_load = pltpu.make_async_copy(hid_hbm, src, load_sems.at[6])
    pl.when(jnp.logical_not(is_last))(saved_load.start)
    pl.when(is_last)(again_load.start)
    loads[4].start()
    loads[5].start()

    barrier = pltpu.get_barrier_semaphore()

    def greet(j, carry):
        pl.semaphore_signal(
            barrier, inc=1, device_id=other((seq + j) % SEQ), device_id_type=pl.DeviceIdType.MESH
        )
        return carry

    lax.fori_loop(1, SEQ, greet, 0)
    for step in (1, 3):
        pl.semaphore_signal(
            barrier,
            inc=1,
            device_id={"section": (section + step) % 4},
            device_id_type=pl.DeviceIdType.MESH,
        )
    for load in loads[:3]:
        load.wait()
    pl.semaphore_wait(barrier, SEQ - 1 + 2)

    def qkv_view(o, part, sub):
        if sub is None:
            return wqkv.at[o, pl.ds(part * 128, 128), :]
        return wqkv.at[o, pl.ds(part * 128 + sub * 64, 64), :]

    def out_view(o, part, sub):
        if sub is None:
            return wout.at[o, :, pl.ds(part * 4096, 4096)]
        return wout.at[o, :, pl.ds(part * 4096 + sub * 2048, 2048)]

    qkv_gather = Gather(place, qkv_view, wqkv_send, wqkv_recv)
    out_gather = Gather(place, out_view, wout_send, wout_recv)
    qkv_gather.begin()

    acc[...] = jnp.zeros_like(acc)
    zero[...] = jnp.zeros_like(zero)

    def inverse_rms(buf):
        def body(i, total):
            wide = buf[:, pl.ds(pl.multiple_of(i * 512, 512), 512)].astype(f32)
            wide = wide * wide
            return total + (
                (wide[:, :128] + wide[:, 128:256]) + (wide[:, 256:384] + wide[:, 384:])
            )

        total = lax.fori_loop(0, 16, body, jnp.zeros((ROWS, 128), f32))
        return lax.rsqrt(jnp.sum(total, axis=1, keepdims=True) * (1.0 / D) + EPSILON)

    def normalize(buf, row):
        inv = inverse_rms(buf)

        def body(i, carry):
            at = pl.ds(pl.multiple_of(i * 128, 128), 128)
            xn[i, pl.ds(row, ROWS), :] = (buf[:, at].astype(f32) * inv * gain[:, at]).astype(bf16)
            return carry

        lax.fori_loop(0, 64, body, 0)
        return inv

    loads[3].wait()
    normalize(hid, 0)
    saved_load.wait()
    inv_src = normalize(src, ROWS)
    loads[4].wait()
    loads[5].wait()

    for step, here in enumerate(qkv_gather.steps()):
        for part, o in here:
            acc[...] += nn(xn[o * 2 + part], wqkv[o, part * 128 : part * 128 + 128, :])

    cos, sin = cosine[...], sine[...]
    for t in range(2):
        row = slice(t * ROWS, (t + 1) * ROWS)
        for h in range(QH + 1):
            u = acc[row, h * HD : (h + 1) * HD]
            u = (u * cos + pltpu.roll(u, HD // 2, 1) * sin).astype(bf16)
            if h < QH:
                queries[t, h * HD : (h + 1) * HD, :] = u
            else:
                kv[PBLK + parity, :, t * 256 : t * 256 + 128] = u
        kv[PBLK + parity, :, t * 256 + 128 : t * 256 + 256] = acc[row, 640:768].astype(bf16)

    def keep_own():
        kv[seq] = kv[PBLK + parity]

    pl.when(in_prompt)(keep_own)
    own_kv = kv.at[PBLK + parity]
    pair_copy = pltpu.make_async_remote_copy(
        src_ref=own_kv,
        dst_ref=own_kv,
        send_sem=pair_sems.at[0],
        recv_sem=pair_sems.at[1],
        device_id=other(partner),
        device_id_type=pl.DeviceIdType.MESH,
    )

    def kv_view(o, part, sub):
        if sub is None:
            return kv.at[o, pl.ds(part * 64, 64), :]
        return kv.at[o, pl.ds(part * 64 + sub * 32, 32), :]

    kv_gather = Gather(place, kv_view, kv_send, kv_recv, only=lambda z: z < 2)
    kv_gather.begin()
    pair_copy.start()
    out_gather.begin()
    for _ in kv_gather.steps():
        pass
    pair_copy.wait_send()
    pltpu.make_async_remote_copy(
        src_ref=own_kv,
        dst_ref=kv.at[PBLK + 1 - parity],
        send_sem=pair_sems.at[0],
        recv_sem=pair_sems.at[1],
        device_id=other(partner),
        device_id_type=pl.DeviceIdType.MESH,
    ).wait_recv()
    kv_gather.finish()

    across = lax.broadcasted_iota(jnp.int32, (1, QH * ROWS), 1) % ROWS
    query_pos = scalars[19] + across
    down = lax.broadcasted_iota(jnp.int32, (2 * BLK, 1), 0)

    def allowed(c):
        key_pos = jnp.where(down < BLK, scalars[2 * c] + down, scalars[2 * c + 1] + (down - BLK))
        key_pos = jnp.where(key_pos < scalars[18], key_pos, FAR)
        return key_pos <= query_pos

    def keys_of(c, t):
        return kv[pl.ds(2 * c, 2), :, t * 256 : t * 256 + 128].reshape(2 * BLK, HD)

    def values_of(c, t):
        return kv[pl.ds(2 * c, 2), :, t * 256 + 128 : t * 256 + 256].reshape(2 * BLK, HD)

    out_steps = out_gather.steps()

    def attend(t):
        q = queries[t]

        def chunk(c, carry):
            row_max, total, weighted = carry
            scores = jnp.where(allowed(c), nt(keys_of(c, t), q), NEGATIVE)
            new_max = jnp.maximum(row_max, jnp.max(scores, axis=0, keepdims=True))
            weights = jnp.exp2((scores - new_max) * LOG2)
            factor = jnp.exp2((row_max - new_max) * LOG2)
            total = total * factor + jnp.sum(weights, axis=0, keepdims=True)
            weighted = weighted * factor + tn(values_of(c, t), weights.astype(bf16))
            return new_max, total, weighted

        carry = (
            jnp.full((1, QH * ROWS), NEGATIVE, f32),
            jnp.zeros((1, QH * ROWS), f32),
            jnp.zeros((HD, QH * ROWS), f32),
        )
        for start in (0, 3, 6):
            carry = lax.fori_loop(start, start + 3, chunk, carry)
            next(out_steps)
        row_max, total, weighted = carry
        weighted = weighted / total
        for h in range(QH):
            mixed[t, :, h * HD : (h + 1) * HD] = weighted[:, h * HD : (h + 1) * HD].T.astype(bf16)
        return row_max * LOG2 + jnp.log2(total)

    log_total = attend(1)
    attend(0)
    for _ in out_steps:
        pass

    mixed_now = mixed[0]
    next_copies = []
    squares = jnp.zeros((ROWS, 128), f32)
    products = jnp.zeros((ROWS, 128), f32)
    for c in range(OUT_STEPS):
        at = pl.ds(c * OUT_COLS, OUT_COLS)
        w = wout[:, :, at].reshape(QH * HD, OUT_COLS)
        y = (nn(mixed_now, w) + hid[:, at].astype(f32)).astype(bf16)
        layer_out[:, at] = y
        next_copies.append(
            pltpu.make_async_remote_copy(
                src_ref=layer_out.at[:, at],
                dst_ref=nh_hbm.at[0, :, at],
                send_sem=next_send.at[c],
                recv_sem=next_recv.at[c],
                device_id={"section": (section + 1) % 4},
                device_id_type=pl.DeviceIdType.MESH,
            )
        )
        pl.when(section < 3)(next_copies[-1].start)
        wide = y.astype(f32)
        scored = wide * head[:, at]
        wide = wide * wide
        for part in range(OUT_COLS // 128):
            squares += wide[:, part * 128 : part * 128 + 128]
            products += scored[:, part * 128 : part * 128 + 128]

    zero_next = [
        pltpu.make_async_copy(
            zero, nh_hbm.at[0, :, pl.ds(c * OUT_COLS, OUT_COLS)], zero_sems.at[c]
        )
        for c in range(OUT_STEPS)
    ]
    zero_prev = [
        pltpu.make_async_copy(
            zero, pg_hbm.at[0, :, pl.ds(c * OUT_COLS, OUT_COLS)], zero_sems.at[c]
        )
        for c in range(OUT_STEPS)
    ]

    def clear_next():
        for copy in zero_next:
            copy.start()

    def clear_prev():
        for copy in zero_prev:
            copy.start()

    pl.when(section == 0)(clear_next)
    pl.when(is_last)(clear_prev)

    def reward_rows():
        mean_square = jnp.sum(squares, axis=1, keepdims=True) * (1.0 / D)
        dots = jnp.sum(products, axis=1, keepdims=True)
        inv = lax.rsqrt(mean_square + EPSILON)
        rows = lax.broadcasted_iota(jnp.int32, (ROWS, 1), 0)
        hit = rows == scalars[20]
        reward = jnp.sum(jnp.where(hit, dots * inv, 0.0), axis=0, keepdims=True)
        tile[...] = jnp.broadcast_to(reward, (8, 128))
        me = seq - PBLK
        copies = []
        for j in range(1, PBLK):
            copies.append(
                pltpu.make_async_remote_copy(
                    src_ref=tile,
                    dst_ref=tiles.at[me],
                    send_sem=tile_send.at[j],
                    recv_sem=tile_recv.at[me],
                    device_id=other(PBLK + (me + j) % PBLK),
                    device_id_type=pl.DeviceIdType.MESH,
                )
            )
            copies[-1].start()
        tiles[me] = tile[...]
        for j in range(1, PBLK):
            source = (me + j) % PBLK
            pltpu.make_async_remote_copy(
                src_ref=tile,
                dst_ref=tiles.at[source],
                send_sem=tile_send.at[0],
                recv_sem=tile_recv.at[source],
                device_id=other(partner),
                device_id_type=pl.DeviceIdType.MESH,
            ).wait_recv()
        for copy in copies:
            copy.wait_send()
        mine = tiles[pl.ds(me // 2 * 2, 1), 0:1].reshape(1, 128) + tiles[
            pl.ds(me // 2 * 2 + 1, 1), 0:1
        ].reshape(1, 128)
        pull = jnp.zeros((1, 128), f32)
        for r in range(RESP):
            way = sign[r : r + 1, :]
            reward_r = tiles[2 * r, 0:1] + tiles[2 * r + 1, 0:1]
            pull += way / (1.0 + jnp.exp(way * (reward_r - mine)))
        pull = pull * (LOSS_SCALE / 28.0)
        row_grad = jnp.where(hit, jnp.sum(pull, axis=1, keepdims=True) * (1.0 / 128.0), 0.0)
        by_head = row_grad * inv
        by_out = row_grad * (inv * inv * inv) * (dots * (1.0 / D))

        def body(c, carry):
            at = pl.ds(pl.multiple_of(c * OUT_COLS, OUT_COLS), OUT_COLS)
            cot[:, at] = (by_head * head[:, at] - layer_out[:, at].astype(f32) * by_out).astype(
                bf16
            )
            return carry

        lax.fori_loop(0, OUT_STEPS, body, 0)

    def no_rewards():
        cot[...] = jnp.zeros_like(cot)

    pl.when(jnp.logical_and(is_last, jnp.logical_not(in_prompt)))(reward_rows)
    pl.when(jnp.logical_and(is_last, in_prompt))(no_rewards)

    def mix_back(c, total):
        at = pl.ds(pl.multiple_of(c * OUT_COLS, OUT_COLS), OUT_COLS)
        return total + nt(cot[:, at], wout[:, :, at].reshape(QH * HD, OUT_COLS))

    d_mixed = lax.fori_loop(0, OUT_STEPS, mix_back, jnp.zeros((ROWS, QH * HD), f32)).astype(bf16)
    dots = d_mixed.astype(f32) * mixed[1].astype(f32)
    row_dots = []
    for h in range(QH):
        dheads[h * HD : (h + 1) * HD, :] = d_mixed[:, h * HD : (h + 1) * HD]
        row_dots.append(jnp.sum(dots[:, h * HD : (h + 1) * HD].T, axis=0, keepdims=True))
    row_dots = jnp.concatenate(row_dots, axis=1)

    q = queries[1]
    dh = dheads[...]

    def attend_back(c, d_query):
        keys, values = keys_of(c, 1), values_of(c, 1)
        probs = jnp.exp2(jnp.where(allowed(c), nt(keys, q) * LOG2 - log_total, NEGATIVE))
        d_scores = (probs * (nt(values, dh) - row_dots)).astype(bf16)
        d_key = (nn(d_scores, q) * SCALE).astype(bf16)
        d_value = nn(probs.astype(bf16), dh).astype(bf16)
        dkv[pl.ds(2 * c, 2), :, 0:128] = d_key.reshape(2, BLK, HD)
        dkv[pl.ds(2 * c, 2), :, 128:256] = d_value.reshape(2, BLK, HD)
        return d_query + tn(keys, d_scores)

    def to_owner(owner):
        return pltpu.make_async_remote_copy(
            src_ref=dkv.at[owner],
            dst_ref=landed.at[seq],
            send_sem=rs_send.at[owner],
            recv_sem=rs_recv.at[seq],
            device_id=other(owner),
            device_id_type=pl.DeviceIdType.MESH,
        )

    def back_chunk(i, d_query):
        c = (i + seq) % 8
        d_query = attend_back(c, d_query)
        for half in range(2):
            owner = 2 * c + half
            pl.when(owner != seq)(to_owner(owner).start)
        return d_query

    d_query = attend_back(8, jnp.zeros((HD, QH * ROWS), f32))
    to_partner = pltpu.make_async_remote_copy(
        src_ref=dkv.at[PBLK + 1 - parity],
        dst_ref=landed.at[seq],
        send_sem=rs_send.at[PBLK],
        recv_sem=rs_recv.at[seq],
        device_id=other(partner),
        device_id_type=pl.DeviceIdType.MESH,
    )
    pl.when(jnp.logical_not(in_prompt))(to_partner.start)
    d_query = lax.fori_loop(0, 8, back_chunk, d_query) * SCALE

    for h in range(QH):
        u = d_query[:, h * HD : (h + 1) * HD].T
        back[:, h * HD : (h + 1) * HD] = (u * cos - pltpu.roll(u, HD // 2, 1) * sin).astype(bf16)

    def arrived(source):
        pltpu.make_async_remote_copy(
            src_ref=dkv.at[0],
            dst_ref=landed.at[source],
            send_sem=rs_send.at[0],
            recv_sem=rs_recv.at[source],
            device_id=other(partner),
            device_id_type=pl.DeviceIdType.MESH,
        ).wait_recv()

    def keep(total):
        u = total[:, :HD]
        back[:, 512:640] = (u * cos - pltpu.roll(u, HD // 2, 1) * sin).astype(bf16)
        back[:, 640:768] = total[:, HD:].astype(bf16)

    def sum_prompt():
        def body(j, total):
            source = (seq + j) % SEQ
            arrived(source)
            return total + landed[source].astype(f32)

        keep(lax.fori_loop(1, SEQ, body, dkv[seq].astype(f32)))

    def sum_answer():
        arrived(partner)
        keep(dkv[PBLK + parity].astype(f32) + landed[partner].astype(f32))

    pl.when(in_prompt)(sum_prompt)
    pl.when(jnp.logical_not(in_prompt))(sum_answer)

    back_all = back[...]
    along = jnp.sum(back_all.astype(f32) * acc[ROWS:, :], axis=1, keepdims=True)
    along = along * (inv_src * inv_src) * (1.0 / D)
    prev_copies = []
    for c in range(BACK_STEPS):
        at = pl.ds(c * BACK_COLS, BACK_COLS)
        w = wqkv[2 * c : 2 * c + 2].reshape(BACK_COLS, QKV)
        u = nt(back_all, w) * gain[:, at]
        grad[:, at] = (
            cot[:, at].astype(f32) + inv_src * u - src[:, at].astype(f32) * along
        ).astype(bf16)
        prev_copies.append(
            pltpu.make_async_remote_copy(
                src_ref=grad.at[:, at],
                dst_ref=pg_hbm.at[0, :, at],
                send_sem=prev_send.at[c],
                recv_sem=prev_recv.at[c],
                device_id={"section": (section + 3) % 4},
                device_id_type=pl.DeviceIdType.MESH,
            )
        )
        pl.when(section > 0)(prev_copies[-1].start)

    qkv_gather.finish(wqkv.at[pl.ds(0, SEQ - 1)])
    out_gather.finish(wout.at[pl.ds(0, SEQ - 1)])

    def sent_owner(owner, carry):
        pl.when(owner != seq)(to_owner(owner).wait_send)
        return carry

    lax.fori_loop(0, PBLK, sent_owner, 0)
    pl.when(jnp.logical_not(in_prompt))(to_partner.wait_send)

    def each(copies, what):
        def run():
            for copy in copies:
                getattr(copy, what)()

        return run

    pl.when(section < 3)(each(next_copies, "wait_send"))
    pl.when(section > 0)(each(next_copies, "wait_recv"))
    pl.when(section == 0)(each(zero_next, "wait"))
    pl.when(is_last)(each(zero_prev, "wait"))
    pl.when(section > 0)(each(prev_copies, "wait_send"))
    pl.when(section < 3)(each(prev_copies, "wait_recv"))


def per_device(
    hidden_in,
    saved_hidden,
    grad_in,
    norm_gain,
    w_query,
    w_key,
    w_value,
    w_out,
    head,
    block_table,
    resp_lengths,
    pairs,
):
    seq = lax.axis_index("seq")
    in_prompt = seq < PBLK
    answer = jnp.clip((seq - PBLK) // 2, 0, RESP - 1)
    half = seq % 2
    answers = jnp.arange(RESP, dtype=jnp.int32)
    length = jnp.sum(jnp.where(answers == answer, resp_lengths, 0))
    own_block = jnp.sum(jnp.where(jnp.arange(PBLK, dtype=jnp.int32) == seq, block_table, 0))
    first_pos = jnp.where(in_prompt, own_block * BLK, PROMPT + half * BLK)
    pair_pos = jnp.where(in_prompt, FAR, PROMPT + jnp.arange(2, dtype=jnp.int32) * BLK)
    limit = jnp.where(in_prompt, FAR, PROMPT + length)
    end_row = jnp.where(in_prompt, -1, length - 1 - half * BLK)
    scalars = jnp.concatenate(
        [block_table * BLK, pair_pos, jnp.stack([limit, first_pos, end_row])]
    ).astype(jnp.int32)
    won = jnp.logical_and(pairs[:, 0:1] == answer, pairs[:, 1:2] == answers[None, :])
    lost = jnp.logical_and(pairs[:, 1:2] == answer, pairs[:, 0:1] == answers[None, :])
    sign = jnp.sum(lost.astype(f32) - won.astype(f32), axis=0)
    sign = jnp.broadcast_to(sign[:, None], (RESP, 128))
    frequency = ROPE_BASE ** (-2.0 * jnp.arange(HD // 2, dtype=f32) / HD)
    position = first_pos + jnp.arange(ROWS, dtype=jnp.int32)
    angles = position.astype(f32)[:, None] * frequency[None, :]
    cosine, sine = jnp.cos(angles), jnp.sin(angles)
    cosine = jnp.concatenate([cosine, cosine], axis=1)
    sine = jnp.concatenate([-sine, sine], axis=1)

    any_spec = pl.BlockSpec(memory_space=pl.ANY)
    vmem = pl.BlockSpec(memory_space=pltpu.VMEM)
    dma = pltpu.SemaphoreType.DMA
    out = jax.ShapeDtypeStruct((1, ROWS, D), bf16)
    return pl.pallas_call(
        layer_kernel,
        out_shape=(out, out),
        in_specs=[pl.BlockSpec(memory_space=pltpu.SMEM)] + [any_spec] * 7 + [vmem] * 5,
        out_specs=(any_spec, any_spec),
        scratch_shapes=[
            pltpu.VMEM((ROWS, D), bf16),
            pltpu.VMEM((ROWS, D), bf16),
            pltpu.VMEM((ROWS, D), bf16),
            pltpu.VMEM((64, 2 * ROWS, 128), bf16),
            pltpu.VMEM((SEQ, 256, QKV), bf16),
            pltpu.VMEM((SEQ, 16, D), bf16),
            pltpu.VMEM((2 * ROWS, QKV), f32),
            pltpu.VMEM((2, QH * ROWS, HD), bf16),
            pltpu.VMEM((PBLK + 2, BLK, 512), bf16),
            pltpu.VMEM((2, ROWS, QH * HD), bf16),
            pltpu.VMEM((ROWS, D), bf16),
            pltpu.VMEM((QH * ROWS, HD), bf16),
            pltpu.VMEM((PBLK + 2, BLK, 256), bf16),
            pltpu.VMEM((SEQ, BLK, 256), bf16),
            pltpu.VMEM((8, 128), f32),
            pltpu.VMEM((PBLK, 8, 128), f32),
            pltpu.VMEM((ROWS, QKV), bf16),
            pltpu.VMEM((ROWS, D), bf16),
            pltpu.VMEM((ROWS, OUT_COLS), bf16),
            dma((7,)),
            dma((1,)),
            dma((90,)),
            dma((1,)),
            dma((90,)),
            dma((84,)),
            dma((90,)),
            dma((2,)),
            dma((PBLK + 1,)),
            dma((SEQ,)),
            dma((PBLK,)),
            dma((PBLK,)),
            dma((OUT_STEPS,)),
            dma((OUT_STEPS,)),
            dma((BACK_STEPS,)),
            dma((BACK_STEPS,)),
            dma((OUT_STEPS,)),
        ],
        compiler_params=pltpu.CompilerParams(
            collective_id=0, has_side_effects=True, vmem_limit_bytes=60 * 1024 * 1024
        ),
        cost_estimate=pl.CostEstimate(
            flops=12_000_000_000, bytes_accessed=12_000_000, transcendentals=4_000_000
        ),
    )(
        scalars,
        hidden_in[0],
        saved_hidden[0],
        grad_in[0],
        w_query[0],
        w_key[0],
        w_value[0],
        w_out[0],
        norm_gain,
        head[None, :],
        cosine,
        sine,
        sign,
    )


def solution(mesh):
    rows = P("section", "seq", None)
    return jax.shard_map(
        per_device,
        mesh=mesh,
        in_specs=(rows, rows, rows, P("section", None), rows, rows, rows, rows, P(), P(), P(), P()),
        out_specs=(rows, rows),
        check_vma=False,
    )
```

```python
import math

import jax
import jax.numpy as jnp
import numpy as np
from jax import lax
from jax.experimental import pallas as pl
from jax.experimental.pallas import tpu as pltpu
from jax.sharding import PartitionSpec as P

HD = 128
QH = 4
RESP = 8
PAIRS = 28
SECTIONS = 4
BLK = 128
D = 8192
ROWS = 128
SEQ = 32
PBLK = 16
PROMPT = 2048
QKV = 768
EPSILON = 1e-05
ROPE_BASE = 500000.0
LOSS_SCALE = 1024.0
NEGATIVE = -1e30
FAR = 1 << 30
SCALE = HD**-0.5
LOG2 = SCALE / math.log(2.0)
OUT_COLS = 1024
OUT_STEPS = D // OUT_COLS
BACK_COLS = 512
BACK_STEPS = D // BACK_COLS

f32 = jnp.float32
bf16 = jnp.bfloat16

FIRST = ((0, 0), (1, 0), (0, 1), (0, 3), (1, 1), (1, 3), (0, 2), (1, 2))
LAST = (0, 1, 3, 2)
STEPS = 10
WAYS = ((True, "xz"), (True, "zx"), (False, "xz"), (False, "zx"))


def nt(a, b):
    return lax.dot_general(a, b, (((1,), (1,)), ((), ())), preferred_element_type=f32)


def tn(a, b):
    return lax.dot_general(a, b, (((0,), (0,)), ((), ())), preferred_element_type=f32)


def nn(a, b):
    return jnp.dot(a, b, preferred_element_type=f32)


class Place:
    def __init__(self):
        self.seq = lax.axis_index("seq")
        z, y, x = self.seq // 8, lax.rem(self.seq // 4, 2), lax.rem(self.seq, 4)
        self.zs = [lax.rem(z + d, 4) for d in range(4)]
        self.ys = [lax.rem(y + d, 2) * 4 for d in range(2)]
        self.xs = [lax.rem(x + d, 4) for d in range(4)]
        self.z_rows = [d * 8 for d in self.zs]

    def at(self, dz=0, dy=0, dx=0):
        return self.z_rows[dz % 4] + self.ys[dy % 2] + self.xs[dx % 4]


class Part:
    def __init__(self, place, view, y_first, axes, send_sem, recv_sems, base):
        self.place, self.view, self.y_first, self.axes = place, view, y_first, axes
        self.send_sem, self.recv_sems = send_sem, recv_sems
        self.slots = {}
        for dy in range(2):
            for da in range(4):
                for db in range(4):
                    if y_first:
                        halves = 2 if (da == 2 and db == 0) or db == 2 else 1
                    else:
                        halves = 2 if dy == 0 and ((da == 2 and db == 0) or db == 2) else 1
                    for sub in range(halves):
                        if (dy, da, db) != (0, 0, 0):
                            self.slots[(dy, da, db, sub)] = base + len(self.slots)

    def origin(self, dy, da, db):
        dx, dz = (da, db) if self.axes == "xz" else (db, da)
        return self.place.at(dz, dy, dx)

    def push(self, dy, da, db, axis, step=1, sub=None):
        if axis == "y":
            target, key = self.place.at(0, 1, 0), (1 - dy, da, db, 0)
        else:
            along_x = (axis == "a") == (self.axes == "xz")
            target = self.place.at(0, 0, step) if along_x else self.place.at(step, 0, 0)
            if axis == "a":
                key = (dy, (da - step) % 4, db, sub or 0)
            else:
                key = (dy, da, (db - step) % 4, sub or 0)
        ref = self.view(self.origin(dy, da, db), sub)
        pltpu.make_async_remote_copy(
            src_ref=ref,
            dst_ref=ref,
            send_sem=self.send_sem.at[0],
            recv_sem=self.recv_sems.at[self.slots[key]],
            device_id={"seq": target},
            device_id_type=pl.DeviceIdType.MESH,
        ).start()

    def take(self, dy, da, db, sub=None):
        ref = self.view(self.origin(dy, da, db), sub)
        pltpu.make_async_remote_copy(
            src_ref=ref,
            dst_ref=ref,
            send_sem=self.send_sem.at[0],
            recv_sem=self.recv_sems.at[self.slots[(dy, da, db, sub or 0)]],
            device_id={"seq": self.place.at(0, 1, 0)},
            device_id_type=pl.DeviceIdType.MESH,
        ).wait_recv()

    def both(self, dy, da, db, axis):
        self.push(dy, da, db, axis, 1)
        self.push(dy, da, db, axis, -1)

    def begin(self):
        self.push(0, 0, 0, "y")
        self.both(0, 0, 0, "a")
        self.both(0, 0, 0, "b")

    def from_first_ring(self, dy, da):
        if da == 2:
            self.take(dy, 2, 0, 0)
            self.take(dy, 2, 0, 1)
        elif (dy, da) != (0, 0):
            self.take(dy, da, 0)
            if da == 0:
                self.both(dy, 0, 0, "a")
            else:
                self.push(dy, da, 0, "a", -1 if da == 1 else 1, 1 if da == 1 else 0)
        if (dy, da) != (0, 0):
            self.both(dy, da, 0, "b")
            if not self.y_first:
                self.push(dy, da, 0, "y")

    def from_second_ring(self, dy, da):
        for db in (1, 3):
            self.take(dy, da, db)
            self.push(dy, da, db, "b", -1 if db == 1 else 1, 1 if db == 1 else 0)
            if not self.y_first:
                self.push(dy, da, db, "y")

    def across_second_ring(self, dy, da):
        self.take(dy, da, 2, 0)
        self.take(dy, da, 2, 1)
        if not self.y_first:
            self.push(dy, da, 2, "y")

    def step(self, k):
        order = FIRST if self.y_first else tuple((0, da) for da in LAST)
        here = []
        if k < len(order):
            self.from_first_ring(*order[k])
        if 1 <= k <= len(order):
            dy, da = order[k - 1]
            self.from_second_ring(dy, da)
            here += [self.origin(dy, da, db) for db in (0, 1, 3)]
        if 2 <= k <= len(order) + 1:
            dy, da = order[k - 2]
            self.across_second_ring(dy, da)
            here.append(self.origin(dy, da, 2))
        if not self.y_first and STEPS - 4 <= k:
            da = LAST[k - (STEPS - 4)]
            for db in (0, 1, 3, 2):
                self.take(1, da, db)
                here.append(self.origin(1, da, db))
        return here


class Gather:
    def __init__(self, place, views, send_sem, recv_sems):
        self.send_sem, self.parts, base = send_sem, [], 0
        for view, (y_first, axes) in zip(views, WAYS):
            part = Part(place, view, y_first, axes, send_sem, recv_sems, base)
            base += len(part.slots)
            self.parts.append(part)
        self.place = place

    def begin(self):
        for part in self.parts:
            part.begin()

    def step(self, k):
        return [(i, o) for i, part in enumerate(self.parts) for o in part.step(k)]

    def finish(self, whole):
        pltpu.make_async_remote_copy(
            src_ref=whole,
            dst_ref=whole,
            send_sem=self.send_sem.at[0],
            recv_sem=self.send_sem.at[0],
            device_id={"seq": self.place.at(0, 1, 0)},
            device_id_type=pl.DeviceIdType.MESH,
        ).wait_send()


def layer_kernel(
    block_table,
    lengths,
    pairs,
    hid_hbm,
    sav_hbm,
    gin_hbm,
    wq_hbm,
    wk_hbm,
    wv_hbm,
    wo_hbm,
    gain,
    head,
    cos_in,
    sin_in,
    cos_block,
    sin_block,
    nh_hbm,
    pg_hbm,
    key_pos_of,
    hid,
    src,
    cot,
    xn,
    wqkv,
    wout,
    acc,
    queries,
    kv,
    pair_kv,
    mixed,
    layer_out,
    squares,
    products,
    mixing,
    dheads,
    dkv,
    pair_dkv,
    landed,
    pair_landed,
    column,
    column_landed,
    tiles,
    back,
    grad,
    zero,
    load_sems,
    weight_send,
    g1_recv,
    g2_recv,
    kvz_send,
    kvz_recv,
    kv_send,
    kv_recv,
    pair_sems,
    rs_send,
    rs_recv,
    pair_back_sems,
    column_send,
    column_recv,
    tile_send,
    tile_recv,
    next_send,
    next_recv,
    prev_send,
    prev_recv,
    zero_sems,
):
    place = Place()
    seq, z = place.seq, place.zs[0]
    own = place.ys[0] + place.xs[0]
    section = lax.axis_index("section")
    is_last = section == SECTIONS - 1
    not_last = section < SECTIONS - 1
    parity = seq % 2
    partner = seq + 1 - 2 * parity
    in_prompt = seq < PBLK
    in_answer = seq >= PBLK

    def other(index):
        return {"seq": index}

    def beside(j):
        return lax.rem(own + j, 8)

    loads = [
        pltpu.make_async_copy(wk_hbm.at[0], wqkv.at[seq, 4], load_sems.at[0]),
        pltpu.make_async_copy(wv_hbm.at[0], wqkv.at[seq, 5], load_sems.at[1]),
    ]
    for h in range(QH):
        loads.append(
            pltpu.make_async_copy(
                wq_hbm.at[0, :, pl.ds(h * HD, HD)], wqkv.at[seq, h], load_sems.at[2 + h]
            )
        )
    hid_load = pltpu.make_async_copy(hid_hbm.at[0], hid, load_sems.at[6])
    saved_load = pltpu.make_async_copy(sav_hbm.at[0], src, load_sems.at[7])
    again_load = pltpu.make_async_copy(hid_hbm.at[0], src, load_sems.at[7])
    wout_load = pltpu.make_async_copy(wo_hbm.at[0], wout.at[seq], load_sems.at[8])
    cot_load = pltpu.make_async_copy(gin_hbm.at[0], cot, load_sems.at[9])
    for load in loads:
        load.start()
    hid_load.start()
    pl.when(not_last)(saved_load.start)
    pl.when(is_last)(again_load.start)
    wout_load.start()
    cot_load.start()

    barrier = pltpu.get_barrier_semaphore()

    def greet(index):
        pl.semaphore_signal(
            barrier, inc=1, device_id=other(index), device_id_type=pl.DeviceIdType.MESH
        )

    for j in range(1, 8):
        greet(z * 8 + beside(j))
    for dz in range(1, 4):
        greet(place.at(dz))
    for step in (1, 3):
        pl.semaphore_signal(
            barrier,
            inc=1,
            device_id={"section": (section + step) % 4},
            device_id_type=pl.DeviceIdType.MESH,
        )

    half = seq % 2
    answer = jnp.maximum(seq - PBLK, 0) // 2
    own_block = jnp.where(in_prompt, block_table[seq % PBLK], PBLK + half)
    length = lengths[answer]
    first_pos = own_block * BLK
    limit = jnp.where(in_prompt, FAR, PROMPT + length)
    end_row = jnp.where(in_prompt, -1, length - 1 - half * BLK)
    for b in range(PBLK):
        key_pos_of[b] = block_table[b] * BLK
    for b in range(2):
        key_pos_of[PBLK + b] = jnp.where(in_prompt, FAR, PROMPT + b * BLK)
    cos_b, sin_b = cos_block[own_block], sin_block[own_block]
    cos = cos_in[...] * cos_b - sin_in[...] * sin_b
    sin = sin_in[...] * cos_b + cos_in[...] * sin_b

    for load in loads:
        load.wait()
    pl.semaphore_wait(barrier, 12)

    def qkv_view(first, count):
        def view(o, sub):
            if sub is None:
                return wqkv.at[o, pl.ds(first, count)]
            if count == 2:
                return wqkv.at[o, pl.ds(first + sub, 1)]
            return wqkv.at[o, pl.ds(first, 1), pl.ds(sub * 128, 128), :]

        return view

    def out_view(first, size):
        def view(o, sub):
            if sub is None:
                return wout.at[o, :, pl.ds(first, size)]
            return wout.at[o, :, pl.ds(first + sub * (size // 2), size // 2)]

        return view

    groups = ((0, 2), (2, 2), (4, 1), (5, 1))
    g1 = Gather(place, [qkv_view(*g) for g in groups], weight_send.at[pl.ds(0, 1)], g1_recv)
    columns = ((0, 2816), (2816, 2816), (5632, 1280), (6912, 1280))
    g2 = Gather(place, [out_view(*c) for c in columns], weight_send.at[pl.ds(1, 1)], g2_recv)
    g1.begin()

    acc[...] = jnp.zeros_like(acc)
    zero[...] = jnp.zeros_like(zero)

    def inverse_rms(buf):
        def body(i, total):
            wide = buf[:, pl.ds(pl.multiple_of(i * 512, 512), 512)].astype(f32)
            wide = wide * wide
            return total + (
                (wide[:, :128] + wide[:, 128:256]) + (wide[:, 256:384] + wide[:, 384:])
            )

        total = lax.fori_loop(0, 16, body, jnp.zeros((ROWS, 128), f32))
        return lax.rsqrt(jnp.sum(total, axis=1, keepdims=True) * (1.0 / D) + EPSILON)

    def normalize(buf, row):
        inv = inverse_rms(buf)

        def body(i, carry):
            at = pl.ds(pl.multiple_of(i * 256, 256), 256)
            xn[i, pl.ds(row, ROWS), :] = (buf[:, at].astype(f32) * inv * gain[:, at]).astype(bf16)
            return carry

        lax.fori_loop(0, SEQ, body, 0)
        return inv

    def project(here):
        for i, o in here:
            first, count = groups[i]
            w = jnp.concatenate([wqkv[o, g] for g in range(first, first + count)], axis=1)
            acc[:, first * HD : (first + count) * HD] += nn(xn[o], w)

    hid_load.wait()
    normalize(hid, 0)
    first_here = g1.step(0)
    saved_load.wait()
    inv_src = normalize(src, ROWS)
    wout_load.wait()
    cot_load.wait()
    first_here += g1.step(1)
    project(first_here)
    for k in range(2, STEPS):
        if k == 5:
            g2.begin()
        project(g1.step(k))
        if k >= 7:
            g2.step(k - 7)

    def rotated(t, g):
        u = acc[t * ROWS : (t + 1) * ROWS, g * HD : (g + 1) * HD]
        return (u * cos + pltpu.roll(u, HD // 2, 1) * sin).astype(bf16)

    for t in range(2):
        pair_kv[parity, :, t * 256 : t * 256 + 128] = rotated(t, 4)
        pair_kv[parity, :, t * 256 + 128 : t * 256 + 256] = acc[
            t * ROWS : (t + 1) * ROWS, 640:768
        ].astype(bf16)

    pair_copy = pltpu.make_async_remote_copy(
        src_ref=pair_kv.at[parity],
        dst_ref=pair_kv.at[parity],
        send_sem=pair_sems.at[0],
        recv_sem=pair_sems.at[1],
        device_id=other(partner),
        device_id_type=pl.DeviceIdType.MESH,
    )

    def along_z(dz):
        return pltpu.make_async_remote_copy(
            src_ref=kv.at[z % 2, own],
            dst_ref=kv.at[z % 2, own],
            send_sem=kvz_send.at[dz],
            recv_sem=kvz_recv.at[z % 2],
            device_id=other(place.at(dz)),
            device_id_type=pl.DeviceIdType.MESH,
        )

    def send_along_z():
        kv[z, own] = pair_kv[parity]
        for dz in (1, 3, 2):
            along_z(dz).start()

    pl.when(in_prompt)(send_along_z)
    pair_copy.start()

    kv_sent, kv_slots = [], {}

    def kv_piece(dy, dx, rows):
        return kv.at[:, place.ys[dy % 2] + place.xs[dx % 4], pl.ds(*rows)]

    def kv_slot(dy, dx, rows):
        return kv_slots.setdefault((dy % 2, dx % 4, rows), len(kv_slots))

    def kv_push(dy, dx, rows, to_y, to_x):
        ref = kv_piece(dy, dx, rows)
        copy = pltpu.make_async_remote_copy(
            src_ref=ref,
            dst_ref=ref,
            send_sem=kv_send.at[len(kv_sent)],
            recv_sem=kv_recv.at[kv_slot(dy - to_y, dx - to_x, rows)],
            device_id=other(place.at(0, to_y, to_x)),
            device_id_type=pl.DeviceIdType.MESH,
        )
        kv_sent.append(copy)
        copy.start()

    def kv_take(dy, dx, rows):
        ref = kv_piece(dy, dx, rows)
        pltpu.make_async_remote_copy(
            src_ref=ref,
            dst_ref=ref,
            send_sem=kv_send.at[0],
            recv_sem=kv_recv.at[kv_slot(dy, dx, rows)],
            device_id=other(place.at(0, 1, 0)),
            device_id_type=pl.DeviceIdType.MESH,
        ).wait_recv()

    y_rows, x_rows = (0, 64), (64, 64)

    def halves_of(rows):
        return (rows[0], 32), (rows[0] + 32, 32)

    def kv_ring(dy, rows):
        kv_push(dy, 0, rows, 0, 1)
        kv_push(dy, 0, rows, 0, -1)

    def kv_ring_on(dy, rows):
        low, high = halves_of(rows)
        kv_take(dy, 1, rows)
        kv_push(dy, 1, high, 0, -1)
        kv_take(dy, 3, rows)
        kv_push(dy, 3, low, 0, 1)

    def kv_ring_end(dy, rows):
        for part in halves_of(rows):
            kv_take(dy, 2, part)

    def kv_step(k):
        if k == 0:
            for source in range(2):

                def wait(source=source):
                    pltpu.make_async_remote_copy(
                        src_ref=kv.at[source, own],
                        dst_ref=kv.at[source, own],
                        send_sem=kvz_send.at[0],
                        recv_sem=kvz_recv.at[source],
                        device_id=other(partner),
                        device_id_type=pl.DeviceIdType.MESH,
                    ).wait_recv()

                pl.when(z != source)(wait)
            kv_push(0, 0, y_rows, 1, 0)
            kv_ring(0, x_rows)
            kv_ring(0, y_rows)
            kv_push(0, 0, x_rows, 1, 0)
        elif k == 1:
            kv_take(1, 0, y_rows)
            kv_ring(1, y_rows)
            kv_ring_on(0, x_rows)
            kv_push(0, 1, x_rows, 1, 0)
            kv_push(0, 3, x_rows, 1, 0)
            kv_ring_on(0, y_rows)
        elif k == 2:
            kv_ring_end(0, x_rows)
            kv_push(0, 2, x_rows, 1, 0)
            kv_ring_on(1, y_rows)
        else:
            kv_ring_end(0, y_rows)
            kv_ring_end(1, y_rows)
            for dx in range(4):
                kv_take(1, dx, x_rows)

    g2.step(3)
    kv_step(0)
    for t in range(2):
        for h in range(QH):
            queries[t, h * HD : (h + 1) * HD, :] = rotated(t, h)
    for k in range(1, 4):
        g2.step(3 + k)
        kv_step(k)
    pair_copy.wait_send()
    pltpu.make_async_remote_copy(
        src_ref=pair_kv.at[parity],
        dst_ref=pair_kv.at[1 - parity],
        send_sem=pair_sems.at[0],
        recv_sem=pair_sems.at[1],
        device_id=other(partner),
        device_id_type=pl.DeviceIdType.MESH,
    ).wait_recv()

    across = lax.broadcasted_iota(jnp.int32, (1, QH * ROWS), 1) % ROWS
    query_pos = first_pos + across
    down = lax.broadcasted_iota(jnp.int32, (2 * BLK, 1), 0)

    def allowed(c):
        key_pos = jnp.where(
            down < BLK, key_pos_of[2 * c] + down, key_pos_of[2 * c + 1] + (down - BLK)
        )
        key_pos = jnp.where(key_pos < limit, key_pos, FAR)
        return key_pos <= query_pos

    def block_of(c, at):
        if isinstance(c, int) and c == PBLK // 2:
            return pair_kv[:, :, at].reshape(2 * BLK, HD)
        side, first = c // 4, lax.rem(c, 4) * 2
        return kv[pl.ds(side, 1), pl.ds(first, 2), :, at].reshape(2 * BLK, HD)

    def keys_of(c, t):
        return block_of(c, slice(t * 256, t * 256 + 128))

    def values_of(c, t):
        return block_of(c, slice(t * 256 + 128, t * 256 + 256))

    def attend(t, between):
        q = queries[t]

        def chunk(c, carry):
            row_max, total, weighted = carry
            scores = jnp.where(allowed(c), nt(keys_of(c, t), q), NEGATIVE)
            new_max = jnp.maximum(row_max, jnp.max(scores, axis=0, keepdims=True))
            weights = jnp.exp2((scores - new_max) * LOG2)
            factor = jnp.exp2((row_max - new_max) * LOG2)
            total = total * factor + jnp.sum(weights, axis=0, keepdims=True)
            weighted = weighted * factor + tn(values_of(c, t), weights.astype(bf16))
            return new_max, total, weighted

        carry = (
            jnp.full((1, QH * ROWS), NEGATIVE, f32),
            jnp.zeros((1, QH * ROWS), f32),
            jnp.zeros((HD, QH * ROWS), f32),
        )
        for start, then in zip((0, 4), between):
            carry = lax.fori_loop(start, start + 4, chunk, carry)
            for k in then:
                g2.step(k)
        carry = chunk(PBLK // 2, carry)
        row_max, total, weighted = carry
        weighted = weighted / total
        for h in range(QH):
            mixed[t, :, h * HD : (h + 1) * HD] = weighted[:, h * HD : (h + 1) * HD].T.astype(bf16)
        return row_max * LOG2 + jnp.log2(total)

    log_total = attend(1, ((7,), (8,)))
    attend(0, ((9,), ()))

    next_copies = [
        pltpu.make_async_remote_copy(
            src_ref=layer_out.at[:, pl.ds(c * OUT_COLS, OUT_COLS)],
            dst_ref=nh_hbm.at[0, :, pl.ds(c * OUT_COLS, OUT_COLS)],
            send_sem=next_send.at[c],
            recv_sem=next_recv.at[c],
            device_id={"section": (section + 1) % 4},
            device_id_type=pl.DeviceIdType.MESH,
        )
        for c in range(OUT_STEPS)
    ]

    def output(steps):
        mixed_now = mixed[0]
        for c in steps:
            at = pl.ds(c * OUT_COLS, OUT_COLS)
            w = wout[:, :, at].reshape(QH * HD, OUT_COLS)
            y = (nn(mixed_now, w) + hid[:, at].astype(f32)).astype(bf16)
            layer_out[:, at] = y
            pl.when(not_last)(next_copies[c].start)

    def measure_output():
        def body(i, carry):
            square, product = carry
            wide = layer_out[:, pl.ds(pl.multiple_of(i * 128, 128), 128)].astype(f32)
            return square + wide * wide, product + wide * head[pl.ds(i, 1), :]

        none = jnp.zeros((ROWS, 128), f32)
        squares[...], products[...] = lax.fori_loop(0, D // 128, body, (none, none))

    def mix_back(steps):
        def body(c, total):
            at = pl.ds(pl.multiple_of(c * OUT_COLS, OUT_COLS), OUT_COLS)
            return total + nt(cot[:, at], wout[:, :, at].reshape(QH * HD, OUT_COLS))

        mixing[...] = lax.fori_loop(steps[0], steps[1], body, mixing[...])

    mixing[...] = jnp.zeros_like(mixing)
    pl.when(not_last)(lambda: mix_back((0, OUT_STEPS)))

    zero_next = [
        pltpu.make_async_copy(
            zero, nh_hbm.at[0, :, pl.ds(c * OUT_COLS, OUT_COLS)], zero_sems.at[c]
        )
        for c in range(OUT_STEPS)
    ]
    zero_prev = [
        pltpu.make_async_copy(
            zero, pg_hbm.at[0, :, pl.ds(c * OUT_COLS, OUT_COLS)], zero_sems.at[c]
        )
        for c in range(OUT_STEPS)
    ]

    def each(copies, what):
        def run():
            for copy in copies:
                getattr(copy, what)()

        return run

    pl.when(section == 0)(each(zero_next, "start"))
    pl.when(is_last)(each(zero_prev, "start"))

    def reward_rows():
        output(range(OUT_STEPS))
        measure_output()
        mean_square = jnp.sum(squares[...], axis=1, keepdims=True) * (1.0 / D)
        dots = jnp.sum(products[...], axis=1, keepdims=True)
        inv = lax.rsqrt(mean_square + EPSILON)
        rows = lax.broadcasted_iota(jnp.int32, (ROWS, 1), 0)
        hit = rows == end_row
        reward = jnp.sum(jnp.where(hit, dots * inv, 0.0), axis=0, keepdims=True)
        side = z - 2
        tiles[side, own] = jnp.broadcast_to(reward, (8, 128))
        to_z = pltpu.make_async_remote_copy(
            src_ref=tiles.at[side, own],
            dst_ref=tiles.at[side, own],
            send_sem=tile_send.at[0],
            recv_sem=tile_recv.at[8],
            device_id=other((3 - side) * 8 + own),
            device_id_type=pl.DeviceIdType.MESH,
        )
        to_z.start()
        down8 = lax.broadcasted_iota(jnp.int32, (RESP, 128), 0)
        sign = jnp.zeros((RESP, 128), f32)
        for p in range(PAIRS):
            won, lost = pairs[p, 0], pairs[p, 1]
            sign += jnp.where(lost == answer, (down8 == won).astype(f32), 0.0)
            sign -= jnp.where(won == answer, (down8 == lost).astype(f32), 0.0)
        pltpu.make_async_remote_copy(
            src_ref=tiles.at[1 - side, own],
            dst_ref=tiles.at[1 - side, own],
            send_sem=tile_send.at[0],
            recv_sem=tile_recv.at[8],
            device_id=other(partner),
            device_id_type=pl.DeviceIdType.MESH,
        ).wait_recv()
        copies = [to_z]
        for j in range(1, 8):
            copies.append(
                pltpu.make_async_remote_copy(
                    src_ref=tiles.at[:, own],
                    dst_ref=tiles.at[:, own],
                    send_sem=tile_send.at[j],
                    recv_sem=tile_recv.at[own],
                    device_id=other(z * 8 + beside(j)),
                    device_id_type=pl.DeviceIdType.MESH,
                )
            )
            copies[-1].start()
        for j in range(1, 8):
            pltpu.make_async_remote_copy(
                src_ref=tiles.at[:, own],
                dst_ref=tiles.at[:, beside(j)],
                send_sem=tile_send.at[0],
                recv_sem=tile_recv.at[beside(j)],
                device_id=other(partner),
                device_id_type=pl.DeviceIdType.MESH,
            ).wait_recv()
        for copy in copies:
            copy.wait_send()
        mine = (tiles[side, own] + tiles[side, own + 1 - 2 * parity])[0:1]
        pull = jnp.zeros((1, 128), f32)
        for r in range(RESP):
            way = sign[r : r + 1, :]
            first = 2 * (r % 4)
            reward_r = (tiles[r // 4, first] + tiles[r // 4, first + 1])[0:1]
            pull += way / (1.0 + jnp.exp(way * (reward_r - mine)))
        pull = pull * (LOSS_SCALE / PAIRS)
        row_grad = jnp.where(hit, jnp.sum(pull, axis=1, keepdims=True) * (1.0 / 128.0), 0.0)
        by_head = row_grad * inv
        by_out = row_grad * (inv * inv * inv) * (dots * (1.0 / D))

        def body(i, carry):
            at = pl.ds(pl.multiple_of(i * 128, 128), 128)
            wide = layer_out[:, at].astype(f32)
            cot[:, at] = (by_head * head[pl.ds(i, 1), :] - wide * by_out).astype(bf16)
            return carry

        lax.fori_loop(0, D // 128, body, 0)
        mix_back((0, OUT_STEPS))

    def no_rewards():
        cot[...] = jnp.zeros_like(cot)

    pl.when(jnp.logical_and(is_last, in_answer))(reward_rows)
    pl.when(jnp.logical_and(is_last, in_prompt))(no_rewards)

    d_mixed = mixing[...].astype(bf16)
    dots = d_mixed.astype(f32) * mixed[1].astype(f32)
    row_dots = []
    for h in range(QH):
        dheads[h * HD : (h + 1) * HD, :] = d_mixed[:, h * HD : (h + 1) * HD]
        row_dots.append(jnp.sum(dots[:, h * HD : (h + 1) * HD].T, axis=0, keepdims=True))
    row_dots = jnp.concatenate(row_dots, axis=1)

    q = queries[1]
    dh = dheads[...]

    def attend_back(c, d_query):
        keys, values = keys_of(c, 1), values_of(c, 1)
        probs = jnp.exp2(jnp.where(allowed(c), nt(keys, q) * LOG2 - log_total, NEGATIVE))
        d_scores = (probs * (nt(values, dh) - row_dots)).astype(bf16)
        d_key = (nn(d_scores, q) * SCALE).astype(bf16)
        d_value = nn(probs.astype(bf16), dh).astype(bf16)
        both = jnp.concatenate([d_key, d_value], axis=1)
        if isinstance(c, int):
            pair_dkv[...] = both.reshape(2, BLK, 2 * HD)
        else:
            dkv[pl.ds(c // 4, 1), pl.ds(lax.rem(c, 4) * 2, 2)] = both.reshape(1, 2, BLK, 2 * HD)
        return d_query + tn(keys, d_scores)

    def to_summer(side, there):
        return pltpu.make_async_remote_copy(
            src_ref=dkv.at[side, there],
            dst_ref=landed.at[own, side],
            send_sem=rs_send.at[side * 8 + there],
            recv_sem=rs_recv.at[own * 2 + side],
            device_id=other(z * 8 + there),
            device_id_type=pl.DeviceIdType.MESH,
        )

    def back_chunk(i, d_query):
        side, pair = i // 4, lax.rem(own // 2 + 1 + i, 4)
        d_query = attend_back(side * 4 + pair, d_query)
        for j in range(2):
            there = pair * 2 + j
            pl.when(there != own)(to_summer(side, there).start)
        return d_query

    d_query = lax.fori_loop(0, 8, back_chunk, jnp.zeros((HD, QH * ROWS), f32))
    d_query = attend_back(PBLK // 2, d_query) * SCALE
    to_partner = pltpu.make_async_remote_copy(
        src_ref=pair_dkv.at[1 - parity],
        dst_ref=pair_landed,
        send_sem=pair_back_sems.at[0],
        recv_sem=pair_back_sems.at[1],
        device_id=other(partner),
        device_id_type=pl.DeviceIdType.MESH,
    )
    pl.when(in_answer)(to_partner.start)

    for h in range(QH):
        u = d_query[:, h * HD : (h + 1) * HD].T
        back[:, h * HD : (h + 1) * HD] = (u * cos - pltpu.roll(u, HD // 2, 1) * sin).astype(bf16)

    pl.when(not_last)(lambda: output(range(OUT_STEPS)))

    def column_copy(side):
        return pltpu.make_async_remote_copy(
            src_ref=column.at[side],
            dst_ref=column_landed.at[z],
            send_sem=column_send.at[side],
            recv_sem=column_recv.at[z],
            device_id=other(side * 8 + own),
            device_id_type=pl.DeviceIdType.MESH,
        )

    for side in range(2):

        def add(j, total, side=side):
            there = beside(j)
            pltpu.make_async_remote_copy(
                src_ref=dkv.at[side, there],
                dst_ref=landed.at[there, side],
                send_sem=rs_send.at[0],
                recv_sem=rs_recv.at[there * 2 + side],
                device_id=other(partner),
                device_id_type=pl.DeviceIdType.MESH,
            ).wait_recv()
            return total + landed[there, side].astype(f32)

        column[side] = lax.fori_loop(1, 8, add, dkv[side, own].astype(f32)).astype(bf16)
        pl.when(z != side)(column_copy(side).start)

    def keep(total):
        u = total[:, :HD]
        back[:, 512:640] = (u * cos - pltpu.roll(u, HD // 2, 1) * sin).astype(bf16)
        back[:, 640:768] = total[:, HD:].astype(bf16)

    def sum_prompt():
        def add(j, total):
            there = lax.rem(z + j, 4)
            pltpu.make_async_remote_copy(
                src_ref=column.at[0],
                dst_ref=column_landed.at[there],
                send_sem=column_send.at[0],
                recv_sem=column_recv.at[there],
                device_id=other(partner),
                device_id_type=pl.DeviceIdType.MESH,
            ).wait_recv()
            return total + column_landed[there].astype(f32)

        keep(lax.fori_loop(1, 4, add, column[z].astype(f32)))

    def sum_answer():
        to_partner.wait_recv()
        keep(pair_dkv[parity].astype(f32) + pair_landed[...].astype(f32))

    pl.when(in_prompt)(sum_prompt)
    pl.when(in_answer)(sum_answer)

    back_all = back[...]
    along = jnp.sum(back_all.astype(f32) * acc[ROWS:, :], axis=1, keepdims=True)
    along = along * (inv_src * inv_src) * (1.0 / D)
    prev_copies = []
    for c in range(BACK_STEPS):
        at = pl.ds(c * BACK_COLS, BACK_COLS)
        w = jnp.concatenate(
            [wqkv[2 * c : 2 * c + 2, g].reshape(BACK_COLS, HD) for g in range(QKV // HD)], axis=1
        )
        u = nt(back_all, w) * gain[:, at]
        grad[:, at] = (
            cot[:, at].astype(f32) + inv_src * u - src[:, at].astype(f32) * along
        ).astype(bf16)
        prev_copies.append(
            pltpu.make_async_remote_copy(
                src_ref=grad.at[:, at],
                dst_ref=pg_hbm.at[0, :, at],
                send_sem=prev_send.at[c],
                recv_sem=prev_recv.at[c],
                device_id={"section": (section + 3) % 4},
                device_id_type=pl.DeviceIdType.MESH,
            )
        )
        pl.when(section > 0)(prev_copies[-1].start)

    g1.finish(wqkv.at[pl.ds(0, SEQ - 1)])
    g2.finish(wout.at[pl.ds(0, SEQ - 1)])
    pl.when(in_prompt)(each([along_z(dz) for dz in (1, 3, 2)], "wait_send"))
    for copy in kv_sent:
        copy.wait_send()
    for side in range(2):

        def sent_on(there, carry, side=side):
            pl.when(there != own)(to_summer(side, there).wait_send)
            return carry

        lax.fori_loop(0, 8, sent_on, 0)
        pl.when(z != side)(column_copy(side).wait_send)
    pl.when(in_answer)(to_partner.wait_send)
    pl.when(not_last)(each(next_copies, "wait_send"))
    pl.when(section > 0)(each(next_copies, "wait_recv"))
    pl.when(section == 0)(each(zero_next, "wait"))
    pl.when(is_last)(each(zero_prev, "wait"))
    pl.when(section > 0)(each(prev_copies, "wait_send"))
    pl.when(not_last)(each(prev_copies, "wait_recv"))


def angle_tables():
    frequency = ROPE_BASE ** (-2.0 * np.arange(HD // 2) / HD)

    def table(positions):
        angles = np.asarray(positions, np.float64)[:, None] * frequency[None, :]
        cosine, sine = np.cos(angles), np.sin(angles)
        return (
            np.concatenate([cosine, cosine], axis=1).astype(np.float32),
            np.concatenate([-sine, sine], axis=1).astype(np.float32),
        )

    within = table(np.arange(BLK))
    blocks = [part[:, None, :] for part in table(np.arange(PBLK + 2) * BLK)]
    return (*within, *blocks)


def per_device(
    hidden_in,
    saved_hidden,
    grad_in,
    norm_gain,
    w_query,
    w_key,
    w_value,
    w_out,
    head,
    block_table,
    resp_lengths,
    pairs,
):
    any_spec = pl.BlockSpec(memory_space=pl.ANY)
    vmem = pl.BlockSpec(memory_space=pltpu.VMEM)
    smem = pl.BlockSpec(memory_space=pltpu.SMEM)
    dma = pltpu.SemaphoreType.DMA
    out = jax.ShapeDtypeStruct((1, ROWS, D), bf16)
    return pl.pallas_call(
        layer_kernel,
        out_shape=(out, out),
        in_specs=[smem] * 3 + [any_spec] * 7 + [vmem] * 6,
        out_specs=(any_spec, any_spec),
        scratch_shapes=[
            pltpu.SMEM((PBLK + 2,), jnp.int32),
            pltpu.VMEM((ROWS, D), bf16),
            pltpu.VMEM((ROWS, D), bf16),
            pltpu.VMEM((ROWS, D), bf16),
            pltpu.VMEM((SEQ, 2 * ROWS, 256), bf16),
            pltpu.VMEM((SEQ, QKV // HD, 256, HD), bf16),
            pltpu.VMEM((SEQ, 16, D), bf16),
            pltpu.VMEM((2 * ROWS, QKV), f32),
            pltpu.VMEM((2, QH * ROWS, HD), bf16),
            pltpu.VMEM((2, 8, BLK, 512), bf16),
            pltpu.VMEM((2, BLK, 512), bf16),
            pltpu.VMEM((2, ROWS, QH * HD), bf16),
            pltpu.VMEM((ROWS, D), bf16),
            pltpu.VMEM((ROWS, 128), f32),
            pltpu.VMEM((ROWS, 128), f32),
            pltpu.VMEM((ROWS, QH * HD), f32),
            pltpu.VMEM((QH * ROWS, HD), bf16),
            pltpu.VMEM((2, 8, BLK, 256), bf16),
            pltpu.VMEM((2, BLK, 256), bf16),
            pltpu.VMEM((8, 2, BLK, 256), bf16),
            pltpu.VMEM((BLK, 256), bf16),
            pltpu.VMEM((2, BLK, 256), bf16),
            pltpu.VMEM((4, BLK, 256), bf16),
            pltpu.VMEM((2, 8, 8, 128), f32),
            pltpu.VMEM((ROWS, QKV), bf16),
            pltpu.VMEM((ROWS, D), bf16),
            pltpu.VMEM((ROWS, OUT_COLS), bf16),
            dma((10,)),
            dma((2,)),
            dma((160,)),
            dma((160,)),
            dma((4,)),
            dma((2,)),
            dma((32,)),
            dma((32,)),
            dma((2,)),
            dma((16,)),
            dma((16,)),
            dma((2,)),
            dma((2,)),
            dma((4,)),
            dma((8,)),
            dma((9,)),
            dma((OUT_STEPS,)),
            dma((OUT_STEPS,)),
            dma((BACK_STEPS,)),
            dma((BACK_STEPS,)),
            dma((OUT_STEPS,)),
        ],
        compiler_params=pltpu.CompilerParams(
            collective_id=0, has_side_effects=True, vmem_limit_bytes=60 * 1024 * 1024
        ),
        cost_estimate=pl.CostEstimate(
            flops=12_000_000_000, bytes_accessed=12_000_000, transcendentals=4_000_000
        ),
    )(
        block_table,
        resp_lengths,
        pairs,
        hidden_in,
        saved_hidden,
        grad_in,
        w_query,
        w_key,
        w_value,
        w_out,
        norm_gain,
        head.reshape(D // 128, 128),
        *angle_tables(),
    )


def solution(mesh):
    rows = P("section", "seq", None)
    return jax.shard_map(
        per_device,
        mesh=mesh,
        in_specs=(rows, rows, rows, P("section", None), rows, rows, rows, rows, P(), P(), P(), P()),
        out_specs=(rows, rows),
        check_vma=False,
    )
```

```python
import math

import jax
import jax.numpy as jnp
import numpy as np
from jax import lax
from jax.experimental import pallas as pl
from jax.experimental.pallas import tpu as pltpu
from jax.sharding import PartitionSpec as P

HD = 128
QH = 4
RESP = 8
PAIRS = 28
SECTIONS = 4
BLK = 128
D = 8192
ROWS = 128
SEQ = 32
PBLK = 16
PROMPT = 2048
QKV = 768
EPSILON = 1e-05
ROPE_BASE = 500000.0
LOSS_SCALE = 1024.0
NEGATIVE = -1e30
FAR = 1 << 30
SCALE = HD**-0.5
LOG2 = SCALE / math.log(2.0)
OUT_COLS = 1024
OUT_STEPS = D // OUT_COLS
MIX_COLS = 512
MIX_STEPS = D // MIX_COLS
MIX_FIRST = 2 * 2816 // MIX_COLS
BACK_COLS = 512
BACK_STEPS = D // BACK_COLS
ROUND = (2, 7, 12)

f32 = jnp.float32
bf16 = jnp.bfloat16

FIRST = ((0, 0), (1, 0), (0, 1), (0, 3), (1, 1), (1, 3), (0, 2), (1, 2))
LAST = (0, 1, 3, 2)
LAG_ON, LAG_ACROSS = 2, 4
STEPS = len(FIRST) + LAG_ACROSS
QKV_WAYS = (
    (True, "xz"),
    (True, "zx"),
    (True, "xz"),
    (True, "zx"),
    (False, "xz"),
    (False, "zx"),
)
OUT_WAYS = ((True, "xz"), (True, "zx"), (False, "xz"), (False, "zx"))


def nt(a, b):
    return lax.dot_general(a, b, (((1,), (1,)), ((), ())), preferred_element_type=f32)


def tn(a, b):
    return lax.dot_general(a, b, (((0,), (0,)), ((), ())), preferred_element_type=f32)


def nn(a, b):
    return jnp.dot(a, b, preferred_element_type=f32)


class Place:
    def __init__(self):
        self.seq = lax.axis_index("seq")
        z, y, x = self.seq // 8, lax.rem(self.seq // 4, 2), lax.rem(self.seq, 4)
        self.zs = [lax.rem(z + d, 4) for d in range(4)]
        self.ys = [lax.rem(y + d, 2) * 4 for d in range(2)]
        self.xs = [lax.rem(x + d, 4) for d in range(4)]
        self.z_rows = [d * 8 for d in self.zs]

    def at(self, dz=0, dy=0, dx=0):
        return self.z_rows[dz % 4] + self.ys[dy % 2] + self.xs[dx % 4]


class Part:
    def __init__(self, place, view, y_first, axes, send_sem, recv_sems, base):
        self.place, self.view, self.y_first, self.axes = place, view, y_first, axes
        self.send_sem, self.recv_sems = send_sem, recv_sems
        self.slots = {}
        for dy in range(2):
            for da in range(4):
                for db in range(4):
                    if y_first:
                        halves = 2 if (da == 2 and db == 0) or db == 2 else 1
                    else:
                        halves = 2 if dy == 0 and ((da == 2 and db == 0) or db == 2) else 1
                    for sub in range(halves):
                        if (dy, da, db) != (0, 0, 0):
                            self.slots[(dy, da, db, sub)] = base + len(self.slots)

    def origin(self, dy, da, db):
        dx, dz = (da, db) if self.axes == "xz" else (db, da)
        return self.place.at(dz, dy, dx)

    def push(self, dy, da, db, axis, step=1, sub=None):
        if axis == "y":
            target, key = self.place.at(0, 1, 0), (1 - dy, da, db, 0)
        else:
            along_x = (axis == "a") == (self.axes == "xz")
            target = self.place.at(0, 0, step) if along_x else self.place.at(step, 0, 0)
            if axis == "a":
                key = (dy, (da - step) % 4, db, sub or 0)
            else:
                key = (dy, da, (db - step) % 4, sub or 0)
        ref = self.view(self.origin(dy, da, db), sub)
        pltpu.make_async_remote_copy(
            src_ref=ref,
            dst_ref=ref,
            send_sem=self.send_sem.at[0],
            recv_sem=self.recv_sems.at[self.slots[key]],
            device_id={"seq": target},
            device_id_type=pl.DeviceIdType.MESH,
        ).start()

    def take(self, dy, da, db, sub=None):
        ref = self.view(self.origin(dy, da, db), sub)
        pltpu.make_async_remote_copy(
            src_ref=ref,
            dst_ref=ref,
            send_sem=self.send_sem.at[0],
            recv_sem=self.recv_sems.at[self.slots[(dy, da, db, sub or 0)]],
            device_id={"seq": self.place.at(0, 1, 0)},
            device_id_type=pl.DeviceIdType.MESH,
        ).wait_recv()

    def both(self, dy, da, db, axis):
        self.push(dy, da, db, axis, 1)
        self.push(dy, da, db, axis, -1)

    def begin(self):
        self.push(0, 0, 0, "y")
        self.both(0, 0, 0, "a")
        self.both(0, 0, 0, "b")

    def from_first_ring(self, dy, da):
        if da == 2:
            self.take(dy, 2, 0, 0)
            self.take(dy, 2, 0, 1)
        elif (dy, da) != (0, 0):
            self.take(dy, da, 0)
            if da == 0:
                self.both(dy, 0, 0, "a")
            else:
                self.push(dy, da, 0, "a", -1 if da == 1 else 1, 1 if da == 1 else 0)
        if (dy, da) != (0, 0):
            self.both(dy, da, 0, "b")
            if not self.y_first:
                self.push(dy, da, 0, "y")

    def from_second_ring(self, dy, da):
        for db in (1, 3):
            self.take(dy, da, db)
            self.push(dy, da, db, "b", -1 if db == 1 else 1, 1 if db == 1 else 0)
            if not self.y_first:
                self.push(dy, da, db, "y")

    def across_second_ring(self, dy, da):
        self.take(dy, da, 2, 0)
        self.take(dy, da, 2, 1)
        if not self.y_first:
            self.push(dy, da, 2, "y")

    def step(self, k):
        order = FIRST if self.y_first else tuple((0, da) for da in LAST)
        here = []
        if k < len(order):
            self.from_first_ring(*order[k])
        if 0 <= k - LAG_ON < len(order):
            dy, da = order[k - LAG_ON]
            self.from_second_ring(dy, da)
            here += [self.origin(dy, da, db) for db in (0, 1, 3)]
        if 0 <= k - LAG_ACROSS < len(order):
            dy, da = order[k - LAG_ACROSS]
            self.across_second_ring(dy, da)
            here.append(self.origin(dy, da, 2))
        if not self.y_first and STEPS - 4 <= k:
            da = LAST[k - (STEPS - 4)]
            for db in (0, 1, 3, 2):
                self.take(1, da, db)
                here.append(self.origin(1, da, db))
        return here


class Gather:
    def __init__(self, place, views, ways, send_sem, recv_sems):
        self.send_sem, self.parts, base = send_sem, [], 0
        for view, (y_first, axes) in zip(views, ways):
            part = Part(place, view, y_first, axes, send_sem, recv_sems, base)
            base += len(part.slots)
            self.parts.append(part)
        self.place = place

    def begin(self):
        for part in self.parts:
            part.begin()

    def step(self, *steps):
        if len(steps) == 1 and isinstance(steps[0], int):
            steps = [(i, steps[0]) for i in range(len(self.parts))]
        return [(i, o) for i, k in steps if 0 <= k < STEPS for o in self.parts[i].step(k)]

    def finish(self, whole):
        pltpu.make_async_remote_copy(
            src_ref=whole,
            dst_ref=whole,
            send_sem=self.send_sem.at[0],
            recv_sem=self.send_sem.at[0],
            device_id={"seq": self.place.at(0, 1, 0)},
            device_id_type=pl.DeviceIdType.MESH,
        ).wait_send()


def layer_kernel(
    block_table,
    lengths,
    pairs,
    hid_hbm,
    sav_hbm,
    gin_hbm,
    wq_hbm,
    wk_hbm,
    wv_hbm,
    wo_hbm,
    gain,
    head,
    cos_in,
    sin_in,
    cos_block,
    sin_block,
    nh_hbm,
    pg_hbm,
    key_pos_of,
    hid,
    src,
    cot,
    xn,
    wqkv,
    wout,
    acc,
    queries,
    kv,
    pair_kv,
    mixed,
    layer_out,
    squares,
    products,
    mixing,
    dheads,
    dkv,
    pair_dkv,
    landed,
    pair_landed,
    column,
    column_landed,
    tiles,
    back,
    grad,
    relay,
    zero,
    load_sems,
    weight_send,
    g1_recv,
    g2_recv,
    kvz_send,
    kvz_recv,
    kv_send,
    kv_recv,
    pair_sems,
    rs_send,
    rs_recv,
    pair_back_sems,
    column_send,
    column_recv,
    tile_send,
    tile_recv,
    next_send,
    next_recv,
    prev_send,
    prev_recv,
    relay_send,
    relay_recv,
    zero_sems,
):
    place = Place()
    seq, z = place.seq, place.zs[0]
    own = place.ys[0] + place.xs[0]
    section = lax.axis_index("section")
    is_last = section == SECTIONS - 1
    not_last = section < SECTIONS - 1
    parity = seq % 2
    partner = seq + 1 - 2 * parity
    in_prompt = seq < PBLK
    in_answer = seq >= PBLK
    has_back = section > 0
    from_grad = jnp.logical_and(has_back, not_last)
    sends_keys = jnp.logical_and(has_back, jnp.logical_or(not_last, in_answer))
    last_prompt = jnp.logical_and(is_last, in_prompt)
    across_y = place.at(0, 1, 0)

    def other(index):
        return {"seq": index}

    def beside(j):
        return lax.rem(own + j, 8)

    loads = [
        pltpu.make_async_copy(wk_hbm.at[0], wqkv.at[seq, 4], load_sems.at[0]),
        pltpu.make_async_copy(wv_hbm.at[0], wqkv.at[seq, 5], load_sems.at[1]),
    ]
    for h in range(QH):
        loads.append(
            pltpu.make_async_copy(
                wq_hbm.at[0, :, pl.ds(h * HD, HD)], wqkv.at[seq, h], load_sems.at[2 + h]
            )
        )
    hid_load = pltpu.make_async_copy(hid_hbm.at[0], hid, load_sems.at[6])
    saved_load = pltpu.make_async_copy(sav_hbm.at[0], src, load_sems.at[7])
    again_load = pltpu.make_async_copy(hid_hbm.at[0], src, load_sems.at[7])
    wout_load = pltpu.make_async_copy(wo_hbm.at[0], wout.at[seq], load_sems.at[8])
    cot_load = pltpu.make_async_copy(gin_hbm.at[0], cot, load_sems.at[9])
    for load in loads:
        load.start()
    hid_load.start()
    pl.when(not_last)(saved_load.start)
    pl.when(is_last)(again_load.start)
    wout_load.start()
    cot_load.start()

    barrier = pltpu.get_barrier_semaphore()

    def greet(index):
        pl.semaphore_signal(
            barrier, inc=1, device_id=other(index), device_id_type=pl.DeviceIdType.MESH
        )

    for j in range(1, 8):
        greet(z * 8 + beside(j))
    for dz in range(1, 4):
        greet(place.at(dz))
    for step in (1, 3):
        pl.semaphore_signal(
            barrier,
            inc=1,
            device_id={"section": (section + step) % 4},
            device_id_type=pl.DeviceIdType.MESH,
        )

    half = seq % 2
    answer = jnp.maximum(seq - PBLK, 0) // 2
    own_block = jnp.where(in_prompt, block_table[seq % PBLK], PBLK + half)
    length = lengths[answer]
    first_pos = own_block * BLK
    limit = jnp.where(in_prompt, FAR, PROMPT + length)
    end_row = jnp.where(in_prompt, -1, length - 1 - half * BLK)
    for b in range(PBLK):
        key_pos_of[b] = block_table[b] * BLK
    for b in range(2):
        key_pos_of[PBLK + b] = jnp.where(in_prompt, FAR, PROMPT + b * BLK)
    cos_b, sin_b = cos_block[own_block], sin_block[own_block]
    cos = cos_in[...] * cos_b - sin_in[...] * sin_b
    sin = sin_in[...] * cos_b + cos_in[...] * sin_b

    pl.semaphore_signal(
        barrier,
        inc=1,
        device_id={"section": (section + 2) % 4, "seq": across_y},
        device_id_type=pl.DeviceIdType.MESH,
    )
    for load in loads:
        load.wait()
    pl.semaphore_wait(barrier, 13)

    def qkv_view(group):
        def view(o, sub):
            if sub is None:
                return wqkv.at[o, group]
            return wqkv.at[o, group, pl.ds(sub * 128, 128), :]

        return view

    def out_view(first, size):
        def view(o, sub):
            if sub is None:
                return wout.at[o, :, pl.ds(first, size)]
            return wout.at[o, :, pl.ds(first + sub * (size // 2), size // 2)]

        return view

    groups = (4, 5, 0, 1, 2, 3)
    g1 = Gather(
        place, [qkv_view(g) for g in groups], QKV_WAYS, weight_send.at[pl.ds(0, 1)], g1_recv
    )
    columns = ((0, 2816), (2816, 2816), (5632, 1280), (6912, 1280))
    g2 = Gather(
        place, [out_view(*c) for c in columns], OUT_WAYS, weight_send.at[pl.ds(1, 1)], g2_recv
    )
    g1.begin()

    acc[...] = jnp.zeros_like(acc)
    zero[...] = jnp.zeros_like(zero)

    def inverse_rms(buf):
        def body(i, total):
            wide = buf[:, pl.ds(pl.multiple_of(i * 512, 512), 512)].astype(f32)
            wide = wide * wide
            return total + (
                (wide[:, :128] + wide[:, 128:256]) + (wide[:, 256:384] + wide[:, 384:])
            )

        total = lax.fori_loop(0, 16, body, jnp.zeros((ROWS, 128), f32))
        return lax.rsqrt(jnp.sum(total, axis=1, keepdims=True) * (1.0 / D) + EPSILON)

    def normalize(buf, row):
        inv = inverse_rms(buf)

        def body(i, carry):
            at = pl.ds(pl.multiple_of(i * 256, 256), 256)
            xn[i, pl.ds(row, ROWS), :] = (buf[:, at].astype(f32) * inv * gain[:, at]).astype(bf16)
            return carry

        lax.fori_loop(0, SEQ, body, 0)
        return inv

    def project(here):
        for i, o in here:
            g = groups[i]
            acc[:, g * HD : (g + 1) * HD] += nn(xn[o], wqkv[o, g])

    def qkv_step(t):
        return g1.step((0, t), (1, t), (5, t - 1), (4, t - 2), (2, t - 3), (3, t - 3))

    hid_load.wait()
    normalize(hid, 0)
    first_here = qkv_step(0)
    saved_load.wait()
    inv_src = normalize(src, ROWS)
    wout_load.wait()
    cot_load.wait()
    first_here += qkv_step(1)
    project(first_here)
    for t in range(2, STEPS):
        if t == STEPS - 4:
            g2.begin()
        project(qkv_step(t))
    g2.step(0)

    def rotated(t, g):
        u = acc[t * ROWS : (t + 1) * ROWS, g * HD : (g + 1) * HD]
        return (u * cos + pltpu.roll(u, HD // 2, 1) * sin).astype(bf16)

    for t in range(2):
        pair_kv[parity, :, t * 256 : t * 256 + 128] = rotated(t, 4)
        pair_kv[parity, :, t * 256 + 128 : t * 256 + 256] = acc[
            t * ROWS : (t + 1) * ROWS, 640:768
        ].astype(bf16)

    pair_copy = pltpu.make_async_remote_copy(
        src_ref=pair_kv.at[parity],
        dst_ref=pair_kv.at[parity],
        send_sem=pair_sems.at[0],
        recv_sem=pair_sems.at[1],
        device_id=other(partner),
        device_id_type=pl.DeviceIdType.MESH,
    )

    def along_z(dz):
        return pltpu.make_async_remote_copy(
            src_ref=kv.at[z % 2, own],
            dst_ref=kv.at[z % 2, own],
            send_sem=kvz_send.at[dz],
            recv_sem=kvz_recv.at[z % 2],
            device_id=other(place.at(dz)),
            device_id_type=pl.DeviceIdType.MESH,
        )

    def send_along_z():
        kv[z, own] = pair_kv[parity]
        for dz in (1, 3, 2):
            along_z(dz).start()

    pl.when(in_prompt)(send_along_z)
    pair_copy.start()

    kv_sent, kv_slots = [], {}

    def kv_piece(dy, dx, rows):
        return kv.at[:, place.ys[dy % 2] + place.xs[dx % 4], pl.ds(*rows)]

    def kv_slot(dy, dx, rows):
        return kv_slots.setdefault((dy % 2, dx % 4, rows), len(kv_slots))

    def kv_push(dy, dx, rows, to_y, to_x):
        ref = kv_piece(dy, dx, rows)
        copy = pltpu.make_async_remote_copy(
            src_ref=ref,
            dst_ref=ref,
            send_sem=kv_send.at[len(kv_sent)],
            recv_sem=kv_recv.at[kv_slot(dy - to_y, dx - to_x, rows)],
            device_id=other(place.at(0, to_y, to_x)),
            device_id_type=pl.DeviceIdType.MESH,
        )
        kv_sent.append(copy)
        copy.start()

    def kv_take(dy, dx, rows):
        ref = kv_piece(dy, dx, rows)
        pltpu.make_async_remote_copy(
            src_ref=ref,
            dst_ref=ref,
            send_sem=kv_send.at[0],
            recv_sem=kv_recv.at[kv_slot(dy, dx, rows)],
            device_id=other(place.at(0, 1, 0)),
            device_id_type=pl.DeviceIdType.MESH,
        ).wait_recv()

    y_rows, x_rows = (0, 64), (64, 64)

    def halves_of(rows):
        return (rows[0], 32), (rows[0] + 32, 32)

    def kv_ring(dy, rows):
        kv_push(dy, 0, rows, 0, 1)
        kv_push(dy, 0, rows, 0, -1)

    def kv_ring_on(dy, rows):
        low, high = halves_of(rows)
        kv_take(dy, 1, rows)
        kv_push(dy, 1, high, 0, -1)
        kv_take(dy, 3, rows)
        kv_push(dy, 3, low, 0, 1)

    def kv_ring_end(dy, rows):
        for part in halves_of(rows):
            kv_take(dy, 2, part)

    def kv_step(k):
        if k == 0:
            for source in range(2):

                def wait(source=source):
                    pltpu.make_async_remote_copy(
                        src_ref=kv.at[source, own],
                        dst_ref=kv.at[source, own],
                        send_sem=kvz_send.at[0],
                        recv_sem=kvz_recv.at[source],
                        device_id=other(partner),
                        device_id_type=pl.DeviceIdType.MESH,
                    ).wait_recv()

                pl.when(z != source)(wait)
            kv_push(0, 0, y_rows, 1, 0)
            kv_ring(0, x_rows)
            kv_ring(0, y_rows)
            kv_push(0, 0, x_rows, 1, 0)
        elif k == 1:
            kv_take(1, 0, y_rows)
            kv_ring(1, y_rows)
            kv_ring_on(0, x_rows)
            kv_push(0, 1, x_rows, 1, 0)
            kv_push(0, 3, x_rows, 1, 0)
            kv_ring_on(0, y_rows)
        elif k == 2:
            kv_ring_end(0, x_rows)
            kv_push(0, 2, x_rows, 1, 0)
            kv_ring_on(1, y_rows)
        else:
            kv_ring_end(0, y_rows)
            kv_ring_end(1, y_rows)
            for dx in range(4):
                kv_take(1, dx, x_rows)

    project(qkv_step(STEPS))
    g2.step(1)
    kv_step(0)
    project(qkv_step(STEPS + 1))
    g2.step(2)
    project(qkv_step(STEPS + 2))
    kv_step(1)
    for t in range(2):
        for h in range(QH):
            queries[t, h * HD : (h + 1) * HD, :] = rotated(t, h)
    g2.step(3)
    kv_step(2)
    g2.step(4)
    g2.step(5)
    kv_step(3)
    g2.step(6)
    pair_copy.wait_send()
    pltpu.make_async_remote_copy(
        src_ref=pair_kv.at[parity],
        dst_ref=pair_kv.at[1 - parity],
        send_sem=pair_sems.at[0],
        recv_sem=pair_sems.at[1],
        device_id=other(partner),
        device_id_type=pl.DeviceIdType.MESH,
    ).wait_recv()

    across = lax.broadcasted_iota(jnp.int32, (1, QH * ROWS), 1) % ROWS
    query_pos = first_pos + across
    down = lax.broadcasted_iota(jnp.int32, (2 * BLK, 1), 0)

    def allowed(c):
        key_pos = jnp.where(
            down < BLK, key_pos_of[2 * c] + down, key_pos_of[2 * c + 1] + (down - BLK)
        )
        key_pos = jnp.where(key_pos < limit, key_pos, FAR)
        return key_pos <= query_pos

    def block_of(c, at):
        if isinstance(c, int) and c == PBLK // 2:
            return pair_kv[:, :, at].reshape(2 * BLK, HD)
        side, first = c // 4, lax.rem(c, 4) * 2
        return kv[pl.ds(side, 1), pl.ds(first, 2), :, at].reshape(2 * BLK, HD)

    def keys_of(c, t):
        return block_of(c, slice(t * 256, t * 256 + 128))

    def values_of(c, t):
        return block_of(c, slice(t * 256 + 128, t * 256 + 256))

    def attend(t, between):
        q = queries[t]

        def chunk(c, carry):
            row_max, total, weighted = carry
            scores = jnp.where(allowed(c), nt(keys_of(c, t), q), NEGATIVE)
            new_max = jnp.maximum(row_max, jnp.max(scores, axis=0, keepdims=True))
            weights = jnp.exp2((scores - new_max) * LOG2)
            factor = jnp.exp2((row_max - new_max) * LOG2)
            total = total * factor + jnp.sum(weights, axis=0, keepdims=True)
            weighted = weighted * factor + tn(values_of(c, t), weights.astype(bf16))
            return new_max, total, weighted

        carry = (
            jnp.full((1, QH * ROWS), NEGATIVE, f32),
            jnp.zeros((1, QH * ROWS), f32),
            jnp.zeros((HD, QH * ROWS), f32),
        )
        for start, then in zip((0, 4), between):
            carry = lax.fori_loop(start, start + 4, chunk, carry)
            for k in then:
                g2.step(k)
        carry = chunk(PBLK // 2, carry)
        row_max, total, weighted = carry
        weighted = weighted / total
        for h in range(QH):
            mixed[t, :, h * HD : (h + 1) * HD] = weighted[:, h * HD : (h + 1) * HD].T.astype(bf16)
        return row_max * LOG2 + jnp.log2(total)

    log_total = attend(1, ((7,), (8,)))

    def attend_early():
        attend(0, ((), ()))

    early = section == 0
    pl.when(early)(attend_early)

    for k in range(9, STEPS):
        g2.step((0, k), (1, k))
    g2.step((2, 9), (3, 9))

    next_copies = [
        pltpu.make_async_remote_copy(
            src_ref=layer_out.at[:, pl.ds(c * OUT_COLS, OUT_COLS)],
            dst_ref=nh_hbm.at[0, :, pl.ds(c * OUT_COLS, OUT_COLS)],
            send_sem=next_send.at[c],
            recv_sem=next_recv.at[c],
            device_id={"section": (section + 1) % 4},
            device_id_type=pl.DeviceIdType.MESH,
        )
        for c in range(OUT_STEPS)
    ]

    def output(steps):
        mixed_now = mixed[0]
        for c in steps:
            at = pl.ds(c * OUT_COLS, OUT_COLS)
            w = wout[:, :, at].reshape(QH * HD, OUT_COLS)
            y = (nn(mixed_now, w) + hid[:, at].astype(f32)).astype(bf16)
            layer_out[:, at] = y
            pl.when(not_last)(next_copies[c].start)

    def measure_output():
        def body(i, carry):
            square, product = carry
            wide = layer_out[:, pl.ds(pl.multiple_of(i * 128, 128), 128)].astype(f32)
            return square + wide * wide, product + wide * head[pl.ds(i, 1), :]

        none = jnp.zeros((ROWS, 128), f32)
        squares[...], products[...] = lax.fori_loop(0, D // 128, body, (none, none))

    def mix_back(steps):
        def body(c, total):
            at = pl.ds(pl.multiple_of(c * MIX_COLS, MIX_COLS), MIX_COLS)
            return total + nt(wout[:, :, at].reshape(QH * HD, MIX_COLS), cot[:, at])

        mixing[...] = lax.fori_loop(steps[0], steps[1], body, mixing[...])

    mixing[...] = jnp.zeros_like(mixing)
    pl.when(from_grad)(lambda: mix_back((0, MIX_FIRST)))
    for k in range(10, STEPS):
        g2.step((2, k), (3, k))
    pl.when(early)(lambda: output(range(OUT_STEPS)))
    pl.when(from_grad)(lambda: mix_back((MIX_FIRST, MIX_STEPS)))

    zero_next = [
        pltpu.make_async_copy(
            zero, nh_hbm.at[0, :, pl.ds(c * OUT_COLS, OUT_COLS)], zero_sems.at[c]
        )
        for c in range(OUT_STEPS)
    ]
    zero_prev = [
        pltpu.make_async_copy(
            zero, pg_hbm.at[0, :, pl.ds(c * OUT_COLS, OUT_COLS)], zero_sems.at[c]
        )
        for c in range(OUT_STEPS)
    ]

    def each(copies, what):
        def run():
            for copy in copies:
                getattr(copy, what)()

        return run

    pl.when(section == 0)(each(zero_next, "start"))
    pl.when(is_last)(each(zero_prev, "start"))

    def reward_rows():
        mixed[0] = mixed[1]
        output(range(OUT_STEPS))
        measure_output()
        mean_square = jnp.sum(squares[...], axis=1, keepdims=True) * (1.0 / D)
        dots = jnp.sum(products[...], axis=1, keepdims=True)
        inv = lax.rsqrt(mean_square + EPSILON)
        rows = lax.broadcasted_iota(jnp.int32, (ROWS, 1), 0)
        hit = rows == end_row
        reward = jnp.sum(jnp.where(hit, dots * inv, 0.0), axis=0, keepdims=True)
        side = z - 2
        tiles[side, own] = jnp.broadcast_to(reward, (8, 128))
        to_z = pltpu.make_async_remote_copy(
            src_ref=tiles.at[side, own],
            dst_ref=tiles.at[side, own],
            send_sem=tile_send.at[0],
            recv_sem=tile_recv.at[8],
            device_id=other((3 - side) * 8 + own),
            device_id_type=pl.DeviceIdType.MESH,
        )
        to_z.start()
        down8 = lax.broadcasted_iota(jnp.int32, (RESP, 128), 0)
        sign = jnp.zeros((RESP, 128), f32)
        for p in range(PAIRS):
            won, lost = pairs[0, p], pairs[1, p]
            sign += jnp.where(lost == answer, (down8 == won).astype(f32), 0.0)
            sign -= jnp.where(won == answer, (down8 == lost).astype(f32), 0.0)
        pltpu.make_async_remote_copy(
            src_ref=tiles.at[1 - side, own],
            dst_ref=tiles.at[1 - side, own],
            send_sem=tile_send.at[0],
            recv_sem=tile_recv.at[8],
            device_id=other(partner),
            device_id_type=pl.DeviceIdType.MESH,
        ).wait_recv()
        copies = [to_z]
        for j in range(1, 8):
            copies.append(
                pltpu.make_async_remote_copy(
                    src_ref=tiles.at[:, own],
                    dst_ref=tiles.at[:, own],
                    send_sem=tile_send.at[j],
                    recv_sem=tile_recv.at[own],
                    device_id=other(z * 8 + beside(j)),
                    device_id_type=pl.DeviceIdType.MESH,
                )
            )
            copies[-1].start()
        for j in range(1, 8):
            pltpu.make_async_remote_copy(
                src_ref=tiles.at[:, own],
                dst_ref=tiles.at[:, beside(j)],
                send_sem=tile_send.at[0],
                recv_sem=tile_recv.at[beside(j)],
                device_id=other(partner),
                device_id_type=pl.DeviceIdType.MESH,
            ).wait_recv()
        for copy in copies:
            copy.wait_send()
        mine = (tiles[side, own] + tiles[side, own + 1 - 2 * parity])[0:1]
        pull = jnp.zeros((1, 128), f32)
        for r in range(RESP):
            way = sign[r : r + 1, :]
            first = 2 * (r % 4)
            reward_r = (tiles[r // 4, first] + tiles[r // 4, first + 1])[0:1]
            pull += way / (1.0 + jnp.exp(way * (reward_r - mine)))
        pull = pull * (LOSS_SCALE / PAIRS)
        row_grad = jnp.where(hit, jnp.sum(pull, axis=1, keepdims=True) * (1.0 / 128.0), 0.0)
        by_head = row_grad * inv
        by_out = row_grad * (inv * inv * inv) * (dots * (1.0 / D))

        def body(i, carry):
            at = pl.ds(pl.multiple_of(i * 128, 128), 128)
            wide = layer_out[:, at].astype(f32)
            cot[:, at] = (by_head * head[pl.ds(i, 1), :] - wide * by_out).astype(bf16)
            return carry

        lax.fori_loop(0, D // 128, body, 0)
        mix_back((0, MIX_STEPS))

    def no_rewards():
        cot[...] = jnp.zeros_like(cot)

    pl.when(jnp.logical_and(is_last, in_answer))(reward_rows)
    pl.when(last_prompt)(no_rewards)

    row_dots = []
    for h in range(QH):
        at = slice(h * HD, (h + 1) * HD)
        d_head = mixing[at, :].T.astype(bf16)
        dheads[at, :] = d_head
        dots = d_head.astype(f32) * mixed[1, :, at].astype(f32)
        row_dots.append(jnp.sum(dots.T, axis=0, keepdims=True))
    row_dots = jnp.concatenate(row_dots, axis=1)

    q = queries[1]
    dh = dheads[...]

    def attend_back(c, d_query):
        keys, values = keys_of(c, 1), values_of(c, 1)
        probs = jnp.exp2(jnp.where(allowed(c), nt(keys, q) * LOG2 - log_total, NEGATIVE))
        d_scores = (probs * (nt(values, dh) - row_dots)).astype(bf16)
        d_key = (nn(d_scores, q) * SCALE).astype(bf16)
        d_value = nn(probs.astype(bf16), dh).astype(bf16)
        both = jnp.concatenate([d_key, d_value], axis=1)
        if isinstance(c, int):
            pair_dkv[...] = both.reshape(2, BLK, 2 * HD)
        else:
            dkv[pl.ds(c // 4, 1), pl.ds(lax.rem(c, 4) * 2, 2)] = both.reshape(1, 2, BLK, 2 * HD)
        return d_query + tn(keys, d_scores)

    def to_summer(side, there):
        return pltpu.make_async_remote_copy(
            src_ref=dkv.at[side, there],
            dst_ref=landed.at[own, side],
            send_sem=rs_send.at[side * 8 + there],
            recv_sem=rs_recv.at[own * 2 + side],
            device_id=other(z * 8 + there),
            device_id_type=pl.DeviceIdType.MESH,
        )

    def back_chunk(i, d_query):
        side, pair = i // 4, lax.rem(own // 2 + 1 + i, 4)
        d_query = attend_back(side * 4 + pair, d_query)
        for j in range(2):
            there = pair * 2 + j
            pl.when(there != own)(to_summer(side, there).start)
        return d_query

    to_partner = pltpu.make_async_remote_copy(
        src_ref=pair_dkv.at[1 - parity],
        dst_ref=pair_landed,
        send_sem=pair_back_sems.at[0],
        recv_sem=pair_back_sems.at[1],
        device_id=other(partner),
        device_id_type=pl.DeviceIdType.MESH,
    )

    def back_through_keys():
        d_query = lax.fori_loop(0, 8, back_chunk, jnp.zeros((HD, QH * ROWS), f32))
        d_query = attend_back(PBLK // 2, d_query) * SCALE
        pl.when(in_answer)(to_partner.start)
        for h in range(QH):
            u = d_query[:, h * HD : (h + 1) * HD].T
            u = u * cos - pltpu.roll(u, HD // 2, 1) * sin
            back[:, h * HD : (h + 1) * HD] = u.astype(bf16)

    def no_query():
        back[:, 0:512] = jnp.zeros((ROWS, QH * HD), bf16)

    pl.when(sends_keys)(back_through_keys)
    pl.when(last_prompt)(no_query)

    def output_late():
        attend(0, ((), ()))
        output(range(OUT_STEPS))

    pl.when(section == 1)(output_late)

    def column_copy(side):
        return pltpu.make_async_remote_copy(
            src_ref=column.at[side],
            dst_ref=column_landed.at[z],
            send_sem=column_send.at[side],
            recv_sem=column_recv.at[z],
            device_id=other(side * 8 + own),
            device_id_type=pl.DeviceIdType.MESH,
        )

    def sum_plane():
        for side in range(2):

            def add(j, total, side=side):
                there = beside(j)
                pltpu.make_async_remote_copy(
                    src_ref=dkv.at[side, there],
                    dst_ref=landed.at[there, side],
                    send_sem=rs_send.at[0],
                    recv_sem=rs_recv.at[there * 2 + side],
                    device_id=other(partner),
                    device_id_type=pl.DeviceIdType.MESH,
                ).wait_recv()
                return total + landed[there, side].astype(f32)

            column[side] = lax.fori_loop(1, 8, add, dkv[side, own].astype(f32)).astype(bf16)
            pl.when(z != side)(column_copy(side).start)

    pl.when(sends_keys)(sum_plane)

    def keep(total):
        u = total[:, :HD]
        back[:, 512:640] = (u * cos - pltpu.roll(u, HD // 2, 1) * sin).astype(bf16)
        back[:, 640:768] = total[:, HD:].astype(bf16)

    def add_column(there, total):
        pltpu.make_async_remote_copy(
            src_ref=column.at[0],
            dst_ref=column_landed.at[there],
            send_sem=column_send.at[0],
            recv_sem=column_recv.at[there],
            device_id=other(partner),
            device_id_type=pl.DeviceIdType.MESH,
        ).wait_recv()
        return total + column_landed[there].astype(f32)

    def sum_prompt():
        def add(j, total):
            return add_column(lax.rem(z + j, 4), total)

        keep(lax.fori_loop(1, 4, add, column[z].astype(f32)))

    def sum_last_prompt():
        keep(lax.fori_loop(2, 4, add_column, jnp.zeros((BLK, 2 * HD), f32)))

    def sum_answer():
        to_partner.wait_recv()
        keep(pair_dkv[parity].astype(f32) + pair_landed[...].astype(f32))

    pl.when(jnp.logical_and(from_grad, in_prompt))(sum_prompt)
    pl.when(last_prompt)(sum_last_prompt)
    pl.when(jnp.logical_and(has_back, in_answer))(sum_answer)

    def columns_at(c):
        return pl.ds(c * BACK_COLS, BACK_COLS)

    def grad_copy(c, target, send_sem):
        return pltpu.make_async_remote_copy(
            src_ref=grad.at[:, columns_at(c)],
            dst_ref=pg_hbm.at[0, :, columns_at(c)],
            send_sem=send_sem,
            recv_sem=prev_recv.at[c],
            device_id=target,
            device_id_type=pl.DeviceIdType.MESH,
        )

    prev_copies = [
        grad_copy(c, {"section": (section + 3) % 4}, prev_send.at[c]) for c in range(BACK_STEPS)
    ]
    first_relay, second_relay, third_relay = [], [], []
    for i, c in enumerate(ROUND):
        at = columns_at(c)
        first_relay.append(
            pltpu.make_async_remote_copy(
                src_ref=grad.at[:, at],
                dst_ref=grad.at[:, at],
                send_sem=prev_send.at[c],
                recv_sem=relay_recv.at[i],
                device_id={"section": (section + 2) % 4, "seq": across_y},
                device_id_type=pl.DeviceIdType.MESH,
            )
        )
        second_relay.append(
            pltpu.make_async_remote_copy(
                src_ref=grad.at[:, at],
                dst_ref=relay.at[i],
                send_sem=prev_send.at[c],
                recv_sem=relay_recv.at[i],
                device_id={"section": (section + 3) % 4},
                device_id_type=pl.DeviceIdType.MESH,
            )
        )
        third_relay.append(
            pltpu.make_async_remote_copy(
                src_ref=relay.at[i],
                dst_ref=pg_hbm.at[0, :, at],
                send_sem=relay_send.at[i],
                recv_sem=prev_recv.at[c],
                device_id={"section": (section + 2) % 4, "seq": across_y},
                device_id_type=pl.DeviceIdType.MESH,
            )
        )

    def back_through_norm():
        back_all = back[...]
        along = jnp.sum(back_all.astype(f32) * acc[ROWS:, :], axis=1, keepdims=True)
        along = along * (inv_src * inv_src) * (1.0 / D)
        for c in range(BACK_STEPS):
            at = columns_at(c)
            w = jnp.concatenate(
                [wqkv[2 * c : 2 * c + 2, g].reshape(BACK_COLS, HD) for g in range(QKV // HD)],
                axis=1,
            )
            u = nt(back_all, w) * gain[:, at]
            grad[:, at] = (
                cot[:, at].astype(f32) + inv_src * u - src[:, at].astype(f32) * along
            ).astype(bf16)
            if c in ROUND:
                pl.when(section == 2)(first_relay[ROUND.index(c)].start)
                pl.when(section != 2)(prev_copies[c].start)
            else:
                prev_copies[c].start()

    def pass_on():
        for arriving, leaving in zip(first_relay, second_relay):
            arriving.wait_recv()
            leaving.start()

    def pass_on_last():
        for arriving, leaving in zip(second_relay, third_relay):
            arriving.wait_recv()
            leaving.start()

    pl.when(has_back)(back_through_norm)
    pl.when(section == 2)(output_late)
    pl.when(section == 0)(pass_on)
    pl.when(is_last)(pass_on_last)

    g1.finish(wqkv.at[pl.ds(0, SEQ - 1)])
    g2.finish(wout.at[pl.ds(0, SEQ - 1)])
    pl.when(in_prompt)(each([along_z(dz) for dz in (1, 3, 2)], "wait_send"))
    for copy in kv_sent:
        copy.wait_send()
    def keys_sent():
        for side in range(2):

            def sent_on(there, carry, side=side):
                pl.when(there != own)(to_summer(side, there).wait_send)
                return carry

            lax.fori_loop(0, 8, sent_on, 0)
            pl.when(z != side)(column_copy(side).wait_send)
        pl.when(in_answer)(to_partner.wait_send)

    pl.when(sends_keys)(keys_sent)
    pl.when(not_last)(each(next_copies, "wait_send"))
    pl.when(section > 0)(each(next_copies, "wait_recv"))
    pl.when(section == 0)(each(zero_next, "wait"))
    pl.when(is_last)(each(zero_prev, "wait"))
    straight = [prev_copies[c] for c in range(BACK_STEPS) if c not in ROUND]
    around = [prev_copies[c] for c in ROUND]
    pl.when(has_back)(each(straight, "wait_send"))
    pl.when(jnp.logical_and(has_back, section != 2))(each(around, "wait_send"))
    pl.when(section == 2)(each(first_relay, "wait_send"))
    pl.when(section == 0)(each(second_relay, "wait_send"))
    pl.when(is_last)(each(third_relay, "wait_send"))
    pl.when(not_last)(each(prev_copies, "wait_recv"))


def angle_tables():
    frequency = ROPE_BASE ** (-2.0 * np.arange(HD // 2) / HD)

    def table(positions):
        angles = np.asarray(positions, np.float64)[:, None] * frequency[None, :]
        cosine, sine = np.cos(angles), np.sin(angles)
        return (
            np.concatenate([cosine, cosine], axis=1).astype(np.float32),
            np.concatenate([-sine, sine], axis=1).astype(np.float32),
        )

    within = table(np.arange(BLK))
    blocks = [part[:, None, :] for part in table(np.arange(PBLK + 2) * BLK)]
    return (*within, *blocks)


def per_device(
    hidden_in,
    saved_hidden,
    grad_in,
    norm_gain,
    w_query,
    w_key,
    w_value,
    w_out,
    head,
    block_table,
    resp_lengths,
    pairs,
):
    any_spec = pl.BlockSpec(memory_space=pl.ANY)
    vmem = pl.BlockSpec(memory_space=pltpu.VMEM)
    smem = pl.BlockSpec(memory_space=pltpu.SMEM)
    dma = pltpu.SemaphoreType.DMA
    out = jax.ShapeDtypeStruct((1, ROWS, D), bf16)
    return pl.pallas_call(
        layer_kernel,
        out_shape=(out, out),
        in_specs=[smem] * 3 + [any_spec] * 7 + [vmem] * 6,
        out_specs=(any_spec, any_spec),
        scratch_shapes=[
            pltpu.SMEM((PBLK + 2,), jnp.int32),
            pltpu.VMEM((ROWS, D), bf16),
            pltpu.VMEM((ROWS, D), bf16),
            pltpu.VMEM((ROWS, D), bf16),
            pltpu.VMEM((SEQ, 2 * ROWS, 256), bf16),
            pltpu.VMEM((SEQ, QKV // HD, 256, HD), bf16),
            pltpu.VMEM((SEQ, 16, D), bf16),
            pltpu.VMEM((2 * ROWS, QKV), f32),
            pltpu.VMEM((2, QH * ROWS, HD), bf16),
            pltpu.VMEM((2, 8, BLK, 512), bf16),
            pltpu.VMEM((2, BLK, 512), bf16),
            pltpu.VMEM((2, ROWS, QH * HD), bf16),
            pltpu.VMEM((ROWS, D), bf16),
            pltpu.VMEM((ROWS, 128), f32),
            pltpu.VMEM((ROWS, 128), f32),
            pltpu.VMEM((QH * HD, ROWS), f32),
            pltpu.VMEM((QH * ROWS, HD), bf16),
            pltpu.VMEM((2, 8, BLK, 256), bf16),
            pltpu.VMEM((2, BLK, 256), bf16),
            pltpu.VMEM((8, 2, BLK, 256), bf16),
            pltpu.VMEM((BLK, 256), bf16),
            pltpu.VMEM((2, BLK, 256), bf16),
            pltpu.VMEM((4, BLK, 256), bf16),
            pltpu.VMEM((2, 8, 8, 128), f32),
            pltpu.VMEM((ROWS, QKV), bf16),
            pltpu.VMEM((ROWS, D), bf16),
            pltpu.VMEM((len(ROUND), ROWS, BACK_COLS), bf16),
            pltpu.VMEM((ROWS, OUT_COLS), bf16),
            dma((10,)),
            dma((2,)),
            dma((240,)),
            dma((160,)),
            dma((4,)),
            dma((2,)),
            dma((32,)),
            dma((32,)),
            dma((2,)),
            dma((16,)),
            dma((16,)),
            dma((2,)),
            dma((2,)),
            dma((4,)),
            dma((8,)),
            dma((9,)),
            dma((OUT_STEPS,)),
            dma((OUT_STEPS,)),
            dma((BACK_STEPS,)),
            dma((BACK_STEPS,)),
            dma((len(ROUND),)),
            dma((len(ROUND),)),
            dma((OUT_STEPS,)),
        ],
        compiler_params=pltpu.CompilerParams(
            collective_id=0, has_side_effects=True, vmem_limit_bytes=60 * 1024 * 1024
        ),
        cost_estimate=pl.CostEstimate(
            flops=12_000_000_000, bytes_accessed=12_000_000, transcendentals=4_000_000
        ),
    )(
        block_table,
        resp_lengths,
        pairs.T,
        hidden_in,
        saved_hidden,
        grad_in,
        w_query,
        w_key,
        w_value,
        w_out,
        norm_gain,
        head.reshape(D // 128, 128),
        *angle_tables(),
    )


def solution(mesh):
    rows = P("section", "seq", None)
    return jax.shard_map(
        per_device,
        mesh=mesh,
        in_specs=(rows, rows, rows, P("section", None), rows, rows, rows, rows, P(), P(), P(), P()),
        out_specs=(rows, rows),
        check_vma=False,
    )
```

```python
import math

import jax
import jax.numpy as jnp
import numpy as np
from jax import lax
from jax.experimental import pallas as pl
from jax.experimental.pallas import tpu as pltpu
from jax.sharding import PartitionSpec as P

HD = 128
QH = 4
RESP = 8
PAIRS = 28
SECTIONS = 4
BLK = 128
D = 8192
ROWS = 128
SEQ = 32
PBLK = 16
PROMPT = 2048
QKV = 768
EPSILON = 1e-05
ROPE_BASE = 500000.0
LOSS_SCALE = 1024.0
NEGATIVE = -1e30
FAR = 1 << 30
SCALE = HD**-0.5
LOG2 = SCALE / math.log(2.0)
OUT_COLS = 1024
OUT_STEPS = D // OUT_COLS
MIX_COLS = 512
MIX_STEPS = D // MIX_COLS
MIX_FIRST = 2 * 2816 // MIX_COLS
BACK_COLS = 512
BACK_STEPS = D // BACK_COLS
ROUND = (2, 7, 12)

f32 = jnp.float32
bf16 = jnp.bfloat16

FIRST = ((0, 0), (1, 0), (0, 1), (0, 3), (1, 1), (1, 3), (0, 2), (1, 2))
LAST = (0, 1, 3, 2)
LAG_ON, LAG_ACROSS = 2, 4
STEPS = len(FIRST) + LAG_ACROSS
QKV_WAYS = (
    (True, "xz"),
    (True, "zx"),
    (True, "xz"),
    (True, "zx"),
    (False, "xz"),
    (False, "zx"),
)
OUT_WAYS = ((True, "xz"), (True, "zx"), (False, "xz"), (False, "zx"))


def nt(a, b):
    return lax.dot_general(a, b, (((1,), (1,)), ((), ())), preferred_element_type=f32)


def tn(a, b):
    return lax.dot_general(a, b, (((0,), (0,)), ((), ())), preferred_element_type=f32)


def nn(a, b):
    return jnp.dot(a, b, preferred_element_type=f32)


class Place:
    def __init__(self):
        self.seq = lax.axis_index("seq")
        z, y, x = self.seq // 8, lax.rem(self.seq // 4, 2), lax.rem(self.seq, 4)
        self.zs = [lax.rem(z + d, 4) for d in range(4)]
        self.ys = [lax.rem(y + d, 2) * 4 for d in range(2)]
        self.xs = [lax.rem(x + d, 4) for d in range(4)]
        self.z_rows = [d * 8 for d in self.zs]

    def at(self, dz=0, dy=0, dx=0):
        return self.z_rows[dz % 4] + self.ys[dy % 2] + self.xs[dx % 4]


class Part:
    def __init__(self, place, view, y_first, axes, send_sem, recv_sems, base):
        self.place, self.view, self.y_first, self.axes = place, view, y_first, axes
        self.send_sem, self.recv_sems = send_sem, recv_sems
        self.slots = {}
        for dy in range(2):
            for da in range(4):
                for db in range(4):
                    if y_first:
                        halves = 2 if (da == 2 and db == 0) or db == 2 else 1
                    else:
                        halves = 2 if dy == 0 and ((da == 2 and db == 0) or db == 2) else 1
                    for sub in range(halves):
                        if (dy, da, db) != (0, 0, 0):
                            self.slots[(dy, da, db, sub)] = base + len(self.slots)

    def origin(self, dy, da, db):
        dx, dz = (da, db) if self.axes == "xz" else (db, da)
        return self.place.at(dz, dy, dx)

    def push(self, dy, da, db, axis, step=1, sub=None):
        if axis == "y":
            target, key = self.place.at(0, 1, 0), (1 - dy, da, db, 0)
        else:
            along_x = (axis == "a") == (self.axes == "xz")
            target = self.place.at(0, 0, step) if along_x else self.place.at(step, 0, 0)
            if axis == "a":
                key = (dy, (da - step) % 4, db, sub or 0)
            else:
                key = (dy, da, (db - step) % 4, sub or 0)
        ref = self.view(self.origin(dy, da, db), sub)
        pltpu.make_async_remote_copy(
            src_ref=ref,
            dst_ref=ref,
            send_sem=self.send_sem.at[0],
            recv_sem=self.recv_sems.at[self.slots[key]],
            device_id={"seq": target},
            device_id_type=pl.DeviceIdType.MESH,
        ).start()

    def take(self, dy, da, db, sub=None):
        ref = self.view(self.origin(dy, da, db), sub)
        pltpu.make_async_remote_copy(
            src_ref=ref,
            dst_ref=ref,
            send_sem=self.send_sem.at[0],
            recv_sem=self.recv_sems.at[self.slots[(dy, da, db, sub or 0)]],
            device_id={"seq": self.place.at(0, 1, 0)},
            device_id_type=pl.DeviceIdType.MESH,
        ).wait_recv()

    def both(self, dy, da, db, axis):
        self.push(dy, da, db, axis, 1)
        self.push(dy, da, db, axis, -1)

    def begin(self):
        self.push(0, 0, 0, "y")
        self.both(0, 0, 0, "a")
        self.both(0, 0, 0, "b")

    def from_first_ring(self, dy, da):
        if da == 2:
            self.take(dy, 2, 0, 0)
            self.take(dy, 2, 0, 1)
        elif (dy, da) != (0, 0):
            self.take(dy, da, 0)
            if da == 0:
                self.both(dy, 0, 0, "a")
            else:
                self.push(dy, da, 0, "a", -1 if da == 1 else 1, 1 if da == 1 else 0)
        if (dy, da) != (0, 0):
            self.both(dy, da, 0, "b")
            if not self.y_first:
                self.push(dy, da, 0, "y")

    def from_second_ring(self, dy, da):
        for db in (1, 3):
            self.take(dy, da, db)
            self.push(dy, da, db, "b", -1 if db == 1 else 1, 1 if db == 1 else 0)
            if not self.y_first:
                self.push(dy, da, db, "y")

    def across_second_ring(self, dy, da):
        self.take(dy, da, 2, 0)
        self.take(dy, da, 2, 1)
        if not self.y_first:
            self.push(dy, da, 2, "y")

    def step(self, k):
        order = FIRST if self.y_first else tuple((0, da) for da in LAST)
        here = []
        if k < len(order):
            self.from_first_ring(*order[k])
        if 0 <= k - LAG_ON < len(order):
            dy, da = order[k - LAG_ON]
            self.from_second_ring(dy, da)
            here += [self.origin(dy, da, db) for db in (0, 1, 3)]
        if 0 <= k - LAG_ACROSS < len(order):
            dy, da = order[k - LAG_ACROSS]
            self.across_second_ring(dy, da)
            here.append(self.origin(dy, da, 2))
        if not self.y_first and STEPS - 4 <= k:
            da = LAST[k - (STEPS - 4)]
            for db in (0, 1, 3, 2):
                self.take(1, da, db)
                here.append(self.origin(1, da, db))
        return here


class Gather:
    def __init__(self, place, views, ways, send_sem, recv_sems):
        self.send_sem, self.parts, base = send_sem, [], 0
        for view, (y_first, axes) in zip(views, ways):
            part = Part(place, view, y_first, axes, send_sem, recv_sems, base)
            base += len(part.slots)
            self.parts.append(part)
        self.place = place

    def begin(self):
        for part in self.parts:
            part.begin()

    def step(self, *steps):
        if len(steps) == 1 and isinstance(steps[0], int):
            steps = [(i, steps[0]) for i in range(len(self.parts))]
        return [(i, o) for i, k in steps if 0 <= k < STEPS for o in self.parts[i].step(k)]

    def finish(self, whole):
        pltpu.make_async_remote_copy(
            src_ref=whole,
            dst_ref=whole,
            send_sem=self.send_sem.at[0],
            recv_sem=self.send_sem.at[0],
            device_id={"seq": self.place.at(0, 1, 0)},
            device_id_type=pl.DeviceIdType.MESH,
        ).wait_send()


def layer_kernel(
    block_table,
    lengths,
    pairs,
    hid_hbm,
    sav_hbm,
    gin_hbm,
    wq_hbm,
    wk_hbm,
    wv_hbm,
    wo_hbm,
    gain,
    head,
    cos_in,
    sin_in,
    cos_block,
    sin_block,
    nh_hbm,
    pg_hbm,
    key_pos_of,
    hid,
    src,
    cot,
    xn,
    wqkv,
    wout,
    acc,
    queries,
    kv,
    pair_kv,
    mixed,
    layer_out,
    squares,
    products,
    mixing,
    dheads,
    dkv,
    pair_dkv,
    landed,
    pair_landed,
    column,
    column_landed,
    tiles,
    back,
    grad,
    relay,
    load_sems,
    weight_send,
    g1_recv,
    g2_recv,
    kvz_send,
    kvz_recv,
    kv_send,
    kv_recv,
    pair_sems,
    rs_send,
    rs_recv,
    pair_back_sems,
    column_send,
    column_recv,
    tile_send,
    tile_recv,
    next_send,
    next_recv,
    prev_send,
    prev_recv,
    relay_send,
    relay_recv,
):
    place = Place()
    seq, z = place.seq, place.zs[0]
    own = place.ys[0] + place.xs[0]
    section = lax.axis_index("section")
    is_last = section == SECTIONS - 1
    not_last = section < SECTIONS - 1
    parity = seq % 2
    partner = seq + 1 - 2 * parity
    in_prompt = seq < PBLK
    in_answer = seq >= PBLK
    has_back = section > 0
    from_grad = jnp.logical_and(has_back, not_last)
    sends_keys = jnp.logical_and(has_back, jnp.logical_or(not_last, in_answer))
    last_prompt = jnp.logical_and(is_last, in_prompt)
    across_y = place.at(0, 1, 0)

    def other(index):
        return {"seq": index}

    def beside(j):
        return lax.rem(own + j, 8)

    loads = [
        pltpu.make_async_copy(wk_hbm.at[0], wqkv.at[seq, 4], load_sems.at[0]),
        pltpu.make_async_copy(wv_hbm.at[0], wqkv.at[seq, 5], load_sems.at[1]),
    ]
    for h in range(QH):
        loads.append(
            pltpu.make_async_copy(
                wq_hbm.at[0, :, pl.ds(h * HD, HD)], wqkv.at[seq, h], load_sems.at[2 + h]
            )
        )
    hid_load = pltpu.make_async_copy(hid_hbm.at[0], hid, load_sems.at[6])
    saved_load = pltpu.make_async_copy(sav_hbm.at[0], src, load_sems.at[7])
    again_load = pltpu.make_async_copy(hid_hbm.at[0], src, load_sems.at[7])
    wout_load = pltpu.make_async_copy(wo_hbm.at[0], wout.at[seq], load_sems.at[8])
    cot_load = pltpu.make_async_copy(gin_hbm.at[0], cot, load_sems.at[9])
    for load in loads:
        load.start()
    barrier = pltpu.get_barrier_semaphore()

    def greet(index):
        pl.semaphore_signal(
            barrier, inc=1, device_id=other(index), device_id_type=pl.DeviceIdType.MESH
        )

    for j in range(1, 8):
        greet(z * 8 + beside(j))
    for dz in range(1, 4):
        greet(place.at(dz))
    for step in (1, 3):
        pl.semaphore_signal(
            barrier,
            inc=1,
            device_id={"section": (section + step) % 4},
            device_id_type=pl.DeviceIdType.MESH,
        )

    half = seq % 2
    answer = jnp.maximum(seq - PBLK, 0) // 2
    own_block = jnp.where(in_prompt, block_table[seq % PBLK], PBLK + half)
    length = lengths[answer]
    first_pos = own_block * BLK
    limit = jnp.where(in_prompt, FAR, PROMPT + length)
    end_row = jnp.where(in_prompt, -1, length - 1 - half * BLK)
    for b in range(PBLK):
        key_pos_of[b] = block_table[b] * BLK
    for b in range(2):
        key_pos_of[PBLK + b] = jnp.where(in_prompt, FAR, PROMPT + b * BLK)
    cos_b, sin_b = cos_block[own_block], sin_block[own_block]
    cos = cos_in[...] * cos_b - sin_in[...] * sin_b
    sin = sin_in[...] * cos_b + cos_in[...] * sin_b

    pl.semaphore_signal(
        barrier,
        inc=1,
        device_id={"section": (section + 2) % 4, "seq": across_y},
        device_id_type=pl.DeviceIdType.MESH,
    )
    for load in loads:
        load.wait()
    hid_load.start()
    pl.when(not_last)(saved_load.start)
    pl.when(is_last)(again_load.start)
    wout_load.start()
    cot_load.start()
    pl.semaphore_wait(barrier, 13)

    def qkv_view(group):
        def view(o, sub):
            if sub is None:
                return wqkv.at[o, group]
            return wqkv.at[o, group, pl.ds(sub * 128, 128), :]

        return view

    def out_view(first, size):
        def view(o, sub):
            if sub is None:
                return wout.at[o, :, pl.ds(first, size)]
            return wout.at[o, :, pl.ds(first + sub * (size // 2), size // 2)]

        return view

    groups = (4, 5, 0, 1, 2, 3)
    g1 = Gather(
        place, [qkv_view(g) for g in groups], QKV_WAYS, weight_send.at[pl.ds(0, 1)], g1_recv
    )
    columns = ((0, 2816), (2816, 2816), (5632, 1280), (6912, 1280))
    g2 = Gather(
        place, [out_view(*c) for c in columns], OUT_WAYS, weight_send.at[pl.ds(1, 1)], g2_recv
    )
    g1.begin()

    acc[...] = jnp.zeros_like(acc)

    def inverse_rms(buf):
        def body(i, total):
            wide = buf[:, pl.ds(pl.multiple_of(i * 512, 512), 512)].astype(f32)
            wide = wide * wide
            return total + (
                (wide[:, :128] + wide[:, 128:256]) + (wide[:, 256:384] + wide[:, 384:])
            )

        total = lax.fori_loop(0, 16, body, jnp.zeros((ROWS, 128), f32))
        return lax.rsqrt(jnp.sum(total, axis=1, keepdims=True) * (1.0 / D) + EPSILON)

    def normalize(buf, row):
        inv = inverse_rms(buf)

        def body(i, carry):
            at = pl.ds(pl.multiple_of(i * 256, 256), 256)
            xn[i, pl.ds(row, ROWS), :] = (buf[:, at].astype(f32) * inv * gain[:, at]).astype(bf16)
            return carry

        lax.fori_loop(0, SEQ, body, 0)
        return inv

    def project(here):
        for i, o in here:
            g = groups[i]
            acc[:, g * HD : (g + 1) * HD] += nn(xn[o], wqkv[o, g])

    def qkv_step(t):
        return g1.step((0, t), (1, t), (5, t - 1), (4, t - 2), (2, t - 3), (3, t - 3))

    hid_load.wait()
    normalize(hid, 0)
    first_here = qkv_step(0)
    saved_load.wait()
    inv_src = normalize(src, ROWS)
    wout_load.wait()
    cot_load.wait()
    first_here += qkv_step(1)
    project(first_here)
    for t in range(2, STEPS):
        if t == STEPS - 4:
            g2.begin()
        project(qkv_step(t))
    g2.step(0)

    def rotated(t, g):
        u = acc[t * ROWS : (t + 1) * ROWS, g * HD : (g + 1) * HD]
        return (u * cos + pltpu.roll(u, HD // 2, 1) * sin).astype(bf16)

    for t in range(2):
        pair_kv[parity, :, t * 256 : t * 256 + 128] = rotated(t, 4)
        pair_kv[parity, :, t * 256 + 128 : t * 256 + 256] = acc[
            t * ROWS : (t + 1) * ROWS, 640:768
        ].astype(bf16)

    pair_copy = pltpu.make_async_remote_copy(
        src_ref=pair_kv.at[parity],
        dst_ref=pair_kv.at[parity],
        send_sem=pair_sems.at[0],
        recv_sem=pair_sems.at[1],
        device_id=other(partner),
        device_id_type=pl.DeviceIdType.MESH,
    )

    def along_z(dz):
        return pltpu.make_async_remote_copy(
            src_ref=kv.at[z % 2, own],
            dst_ref=kv.at[z % 2, own],
            send_sem=kvz_send.at[dz],
            recv_sem=kvz_recv.at[z % 2],
            device_id=other(place.at(dz)),
            device_id_type=pl.DeviceIdType.MESH,
        )

    def send_along_z():
        kv[z, own] = pair_kv[parity]
        for dz in (1, 3, 2):
            along_z(dz).start()

    pl.when(in_prompt)(send_along_z)
    pair_copy.start()

    kv_sent, kv_slots = [], {}

    def kv_piece(dy, dx, rows):
        return kv.at[:, place.ys[dy % 2] + place.xs[dx % 4], pl.ds(*rows)]

    def kv_slot(dy, dx, rows):
        return kv_slots.setdefault((dy % 2, dx % 4, rows), len(kv_slots))

    def kv_push(dy, dx, rows, to_y, to_x):
        ref = kv_piece(dy, dx, rows)
        copy = pltpu.make_async_remote_copy(
            src_ref=ref,
            dst_ref=ref,
            send_sem=kv_send.at[len(kv_sent)],
            recv_sem=kv_recv.at[kv_slot(dy - to_y, dx - to_x, rows)],
            device_id=other(place.at(0, to_y, to_x)),
            device_id_type=pl.DeviceIdType.MESH,
        )
        kv_sent.append(copy)
        copy.start()

    def kv_take(dy, dx, rows):
        ref = kv_piece(dy, dx, rows)
        pltpu.make_async_remote_copy(
            src_ref=ref,
            dst_ref=ref,
            send_sem=kv_send.at[0],
            recv_sem=kv_recv.at[kv_slot(dy, dx, rows)],
            device_id=other(place.at(0, 1, 0)),
            device_id_type=pl.DeviceIdType.MESH,
        ).wait_recv()

    y_rows, x_rows = (0, 64), (64, 64)

    def halves_of(rows):
        return (rows[0], 32), (rows[0] + 32, 32)

    def kv_ring(dy, rows):
        kv_push(dy, 0, rows, 0, 1)
        kv_push(dy, 0, rows, 0, -1)

    def kv_ring_on(dy, rows):
        low, high = halves_of(rows)
        kv_take(dy, 1, rows)
        kv_push(dy, 1, high, 0, -1)
        kv_take(dy, 3, rows)
        kv_push(dy, 3, low, 0, 1)

    def kv_ring_end(dy, rows):
        for part in halves_of(rows):
            kv_take(dy, 2, part)

    def kv_step(k):
        if k == 0:
            for source in range(2):

                def wait(source=source):
                    pltpu.make_async_remote_copy(
                        src_ref=kv.at[source, own],
                        dst_ref=kv.at[source, own],
                        send_sem=kvz_send.at[0],
                        recv_sem=kvz_recv.at[source],
                        device_id=other(partner),
                        device_id_type=pl.DeviceIdType.MESH,
                    ).wait_recv()

                pl.when(z != source)(wait)
            kv_push(0, 0, y_rows, 1, 0)
            kv_ring(0, x_rows)
            kv_ring(0, y_rows)
            kv_push(0, 0, x_rows, 1, 0)
        elif k == 1:
            kv_take(1, 0, y_rows)
            kv_ring(1, y_rows)
            kv_ring_on(0, x_rows)
            kv_push(0, 1, x_rows, 1, 0)
            kv_push(0, 3, x_rows, 1, 0)
            kv_ring_on(0, y_rows)
        elif k == 2:
            kv_ring_end(0, x_rows)
            kv_push(0, 2, x_rows, 1, 0)
            kv_ring_on(1, y_rows)
        else:
            kv_ring_end(0, y_rows)
            kv_ring_end(1, y_rows)
            for dx in range(4):
                kv_take(1, dx, x_rows)

    project(qkv_step(STEPS))
    g2.step(1)
    kv_step(0)
    project(qkv_step(STEPS + 1))
    g2.step(2)
    project(qkv_step(STEPS + 2))
    kv_step(1)
    for t in range(2):
        for h in range(QH):
            queries[t, h * HD : (h + 1) * HD, :] = rotated(t, h)
    g2.step(3)
    kv_step(2)
    g2.step(4)
    g2.step(5)
    kv_step(3)
    g2.step(6)
    pair_copy.wait_send()
    pltpu.make_async_remote_copy(
        src_ref=pair_kv.at[parity],
        dst_ref=pair_kv.at[1 - parity],
        send_sem=pair_sems.at[0],
        recv_sem=pair_sems.at[1],
        device_id=other(partner),
        device_id_type=pl.DeviceIdType.MESH,
    ).wait_recv()

    across = lax.broadcasted_iota(jnp.int32, (1, QH * ROWS), 1) % ROWS
    query_pos = first_pos + across
    down = lax.broadcasted_iota(jnp.int32, (2 * BLK, 1), 0)

    def allowed(c):
        key_pos = jnp.where(
            down < BLK, key_pos_of[2 * c] + down, key_pos_of[2 * c + 1] + (down - BLK)
        )
        key_pos = jnp.where(key_pos < limit, key_pos, FAR)
        return key_pos <= query_pos

    def block_of(c, at):
        if isinstance(c, int) and c == PBLK // 2:
            return pair_kv[:, :, at].reshape(2 * BLK, HD)
        side, first = c // 4, lax.rem(c, 4) * 2
        return kv[pl.ds(side, 1), pl.ds(first, 2), :, at].reshape(2 * BLK, HD)

    def keys_of(c, t):
        return block_of(c, slice(t * 256, t * 256 + 128))

    def values_of(c, t):
        return block_of(c, slice(t * 256 + 128, t * 256 + 256))

    def attend(t, between):
        q = queries[t]

        def chunk(c, carry):
            row_max, total, weighted = carry
            scores = jnp.where(allowed(c), nt(keys_of(c, t), q), NEGATIVE)
            new_max = jnp.maximum(row_max, jnp.max(scores, axis=0, keepdims=True))
            weights = jnp.exp2((scores - new_max) * LOG2)
            factor = jnp.exp2((row_max - new_max) * LOG2)
            total = total * factor + jnp.sum(weights, axis=0, keepdims=True)
            weighted = weighted * factor + tn(values_of(c, t), weights.astype(bf16))
            return new_max, total, weighted

        carry = (
            jnp.full((1, QH * ROWS), NEGATIVE, f32),
            jnp.zeros((1, QH * ROWS), f32),
            jnp.zeros((HD, QH * ROWS), f32),
        )
        for start, then in zip((0, 4), between):
            carry = lax.fori_loop(start, start + 4, chunk, carry)
            for k in then:
                g2.step(k)
        carry = chunk(PBLK // 2, carry)
        row_max, total, weighted = carry
        weighted = weighted / total
        for h in range(QH):
            mixed[t, :, h * HD : (h + 1) * HD] = weighted[:, h * HD : (h + 1) * HD].T.astype(bf16)
        return row_max * LOG2 + jnp.log2(total)

    log_total = attend(1, ((7,), (8,)))

    def attend_early():
        attend(0, ((), ()))

    early = section == 0
    pl.when(early)(attend_early)

    for k in range(9, STEPS):
        g2.step((0, k), (1, k))
    g2.step((2, 9), (3, 9))

    next_copies = [
        pltpu.make_async_remote_copy(
            src_ref=layer_out.at[:, pl.ds(c * OUT_COLS, OUT_COLS)],
            dst_ref=nh_hbm.at[0, :, pl.ds(c * OUT_COLS, OUT_COLS)],
            send_sem=next_send.at[c],
            recv_sem=next_recv.at[c],
            device_id={"section": (section + 1) % 4},
            device_id_type=pl.DeviceIdType.MESH,
        )
        for c in range(OUT_STEPS)
    ]

    def output(steps):
        mixed_now = mixed[0]
        for c in steps:
            at = pl.ds(c * OUT_COLS, OUT_COLS)
            w = wout[:, :, at].reshape(QH * HD, OUT_COLS)
            y = (nn(mixed_now, w) + hid[:, at].astype(f32)).astype(bf16)
            layer_out[:, at] = y
            pl.when(not_last)(next_copies[c].start)

    def measure_output():
        def body(i, carry):
            square, product = carry
            wide = layer_out[:, pl.ds(pl.multiple_of(i * 128, 128), 128)].astype(f32)
            return square + wide * wide, product + wide * head[pl.ds(i, 1), :]

        none = jnp.zeros((ROWS, 128), f32)
        squares[...], products[...] = lax.fori_loop(0, D // 128, body, (none, none))

    def mix_back(steps):
        def body(c, total):
            at = pl.ds(pl.multiple_of(c * MIX_COLS, MIX_COLS), MIX_COLS)
            return total + nt(wout[:, :, at].reshape(QH * HD, MIX_COLS), cot[:, at])

        mixing[...] = lax.fori_loop(steps[0], steps[1], body, mixing[...])

    mixing[...] = jnp.zeros_like(mixing)
    pl.when(from_grad)(lambda: mix_back((0, MIX_FIRST)))
    for k in range(10, STEPS):
        g2.step((2, k), (3, k))
    pl.when(early)(lambda: output(range(OUT_STEPS)))
    pl.when(from_grad)(lambda: mix_back((MIX_FIRST, MIX_STEPS)))

    def each(copies, what):
        def run():
            for copy in copies:
                getattr(copy, what)()

        return run

    def reward_rows():
        mixed[0] = mixed[1]
        output(range(OUT_STEPS))
        measure_output()
        mean_square = jnp.sum(squares[...], axis=1, keepdims=True) * (1.0 / D)
        dots = jnp.sum(products[...], axis=1, keepdims=True)
        inv = lax.rsqrt(mean_square + EPSILON)
        rows = lax.broadcasted_iota(jnp.int32, (ROWS, 1), 0)
        hit = rows == end_row
        reward = jnp.sum(jnp.where(hit, dots * inv, 0.0), axis=0, keepdims=True)
        side = z - 2
        tiles[side, own] = jnp.broadcast_to(reward, (8, 128))
        to_z = pltpu.make_async_remote_copy(
            src_ref=tiles.at[side, own],
            dst_ref=tiles.at[side, own],
            send_sem=tile_send.at[0],
            recv_sem=tile_recv.at[8],
            device_id=other((3 - side) * 8 + own),
            device_id_type=pl.DeviceIdType.MESH,
        )
        to_z.start()
        down8 = lax.broadcasted_iota(jnp.int32, (RESP, 128), 0)
        sign = jnp.zeros((RESP, 128), f32)
        for p in range(PAIRS):
            won, lost = pairs[0, p], pairs[1, p]
            sign += jnp.where(lost == answer, (down8 == won).astype(f32), 0.0)
            sign -= jnp.where(won == answer, (down8 == lost).astype(f32), 0.0)
        pltpu.make_async_remote_copy(
            src_ref=tiles.at[1 - side, own],
            dst_ref=tiles.at[1 - side, own],
            send_sem=tile_send.at[0],
            recv_sem=tile_recv.at[8],
            device_id=other(partner),
            device_id_type=pl.DeviceIdType.MESH,
        ).wait_recv()
        copies = [to_z]
        for j in range(1, 8):
            copies.append(
                pltpu.make_async_remote_copy(
                    src_ref=tiles.at[:, own],
                    dst_ref=tiles.at[:, own],
                    send_sem=tile_send.at[j],
                    recv_sem=tile_recv.at[own],
                    device_id=other(z * 8 + beside(j)),
                    device_id_type=pl.DeviceIdType.MESH,
                )
            )
            copies[-1].start()
        for j in range(1, 8):
            pltpu.make_async_remote_copy(
                src_ref=tiles.at[:, own],
                dst_ref=tiles.at[:, beside(j)],
                send_sem=tile_send.at[0],
                recv_sem=tile_recv.at[beside(j)],
                device_id=other(partner),
                device_id_type=pl.DeviceIdType.MESH,
            ).wait_recv()
        for copy in copies:
            copy.wait_send()
        mine = (tiles[side, own] + tiles[side, own + 1 - 2 * parity])[0:1]
        pull = jnp.zeros((1, 128), f32)
        for r in range(RESP):
            way = sign[r : r + 1, :]
            first = 2 * (r % 4)
            reward_r = (tiles[r // 4, first] + tiles[r // 4, first + 1])[0:1]
            pull += way / (1.0 + jnp.exp(way * (reward_r - mine)))
        pull = pull * (LOSS_SCALE / PAIRS)
        row_grad = jnp.where(hit, jnp.sum(pull, axis=1, keepdims=True) * (1.0 / 128.0), 0.0)
        by_head = row_grad * inv
        by_out = row_grad * (inv * inv * inv) * (dots * (1.0 / D))

        def body(i, carry):
            at = pl.ds(pl.multiple_of(i * 128, 128), 128)
            wide = layer_out[:, at].astype(f32)
            cot[:, at] = (by_head * head[pl.ds(i, 1), :] - wide * by_out).astype(bf16)
            return carry

        lax.fori_loop(0, D // 128, body, 0)
        mix_back((0, MIX_STEPS))

    def no_rewards():
        cot[...] = jnp.zeros_like(cot)

    pl.when(jnp.logical_and(is_last, in_answer))(reward_rows)
    pl.when(last_prompt)(no_rewards)

    row_dots = []
    for h in range(QH):
        at = slice(h * HD, (h + 1) * HD)
        d_head = mixing[at, :].T.astype(bf16)
        dheads[at, :] = d_head
        dots = d_head.astype(f32) * mixed[1, :, at].astype(f32)
        row_dots.append(jnp.sum(dots.T, axis=0, keepdims=True))
    row_dots = jnp.concatenate(row_dots, axis=1)

    q = queries[1]
    dh = dheads[...]

    def attend_back(c, d_query):
        keys, values = keys_of(c, 1), values_of(c, 1)
        probs = jnp.exp2(jnp.where(allowed(c), nt(keys, q) * LOG2 - log_total, NEGATIVE))
        d_scores = (probs * (nt(values, dh) - row_dots)).astype(bf16)
        d_key = (nn(d_scores, q) * SCALE).astype(bf16)
        d_value = nn(probs.astype(bf16), dh).astype(bf16)
        both = jnp.concatenate([d_key, d_value], axis=1)
        if isinstance(c, int):
            pair_dkv[...] = both.reshape(2, BLK, 2 * HD)
        else:
            dkv[pl.ds(c // 4, 1), pl.ds(lax.rem(c, 4) * 2, 2)] = both.reshape(1, 2, BLK, 2 * HD)
        return d_query + tn(keys, d_scores)

    def to_summer(side, there):
        return pltpu.make_async_remote_copy(
            src_ref=dkv.at[side, there],
            dst_ref=landed.at[own, side],
            send_sem=rs_send.at[side * 8 + there],
            recv_sem=rs_recv.at[own * 2 + side],
            device_id=other(z * 8 + there),
            device_id_type=pl.DeviceIdType.MESH,
        )

    def back_chunk(i, d_query):
        side, pair = i // 4, lax.rem(own // 2 + 1 + i, 4)
        d_query = attend_back(side * 4 + pair, d_query)
        for j in range(2):
            there = pair * 2 + j
            pl.when(there != own)(to_summer(side, there).start)
        return d_query

    to_partner = pltpu.make_async_remote_copy(
        src_ref=pair_dkv.at[1 - parity],
        dst_ref=pair_landed,
        send_sem=pair_back_sems.at[0],
        recv_sem=pair_back_sems.at[1],
        device_id=other(partner),
        device_id_type=pl.DeviceIdType.MESH,
    )

    def back_through_keys():
        d_query = lax.fori_loop(0, 8, back_chunk, jnp.zeros((HD, QH * ROWS), f32), unroll=2)
        d_query = attend_back(PBLK // 2, d_query) * SCALE
        pl.when(in_answer)(to_partner.start)
        for h in range(QH):
            u = d_query[:, h * HD : (h + 1) * HD].T
            u = u * cos - pltpu.roll(u, HD // 2, 1) * sin
            back[:, h * HD : (h + 1) * HD] = u.astype(bf16)

    def no_query():
        back[:, 0:512] = jnp.zeros((ROWS, QH * HD), bf16)

    pl.when(sends_keys)(back_through_keys)
    pl.when(last_prompt)(no_query)

    def output_late():
        attend(0, ((), ()))
        output(range(OUT_STEPS))

    pl.when(section == 1)(output_late)

    def column_copy(side):
        return pltpu.make_async_remote_copy(
            src_ref=column.at[side],
            dst_ref=column_landed.at[z],
            send_sem=column_send.at[side],
            recv_sem=column_recv.at[z],
            device_id=other(side * 8 + own),
            device_id_type=pl.DeviceIdType.MESH,
        )

    def sum_plane():
        for side in range(2):

            def add(j, total, side=side):
                there = beside(j)
                pltpu.make_async_remote_copy(
                    src_ref=dkv.at[side, there],
                    dst_ref=landed.at[there, side],
                    send_sem=rs_send.at[0],
                    recv_sem=rs_recv.at[there * 2 + side],
                    device_id=other(partner),
                    device_id_type=pl.DeviceIdType.MESH,
                ).wait_recv()
                return total + landed[there, side].astype(f32)

            column[side] = lax.fori_loop(1, 8, add, dkv[side, own].astype(f32)).astype(bf16)
            pl.when(z != side)(column_copy(side).start)

    pl.when(sends_keys)(sum_plane)

    def keep(total):
        u = total[:, :HD]
        back[:, 512:640] = (u * cos - pltpu.roll(u, HD // 2, 1) * sin).astype(bf16)
        back[:, 640:768] = total[:, HD:].astype(bf16)

    def add_column(there, total):
        pltpu.make_async_remote_copy(
            src_ref=column.at[0],
            dst_ref=column_landed.at[there],
            send_sem=column_send.at[0],
            recv_sem=column_recv.at[there],
            device_id=other(partner),
            device_id_type=pl.DeviceIdType.MESH,
        ).wait_recv()
        return total + column_landed[there].astype(f32)

    def sum_prompt():
        def add(j, total):
            return add_column(lax.rem(z + j, 4), total)

        keep(lax.fori_loop(1, 4, add, column[z].astype(f32)))

    def sum_last_prompt():
        keep(lax.fori_loop(2, 4, add_column, jnp.zeros((BLK, 2 * HD), f32)))

    def sum_answer():
        to_partner.wait_recv()
        keep(pair_dkv[parity].astype(f32) + pair_landed[...].astype(f32))

    pl.when(jnp.logical_and(from_grad, in_prompt))(sum_prompt)
    pl.when(last_prompt)(sum_last_prompt)
    pl.when(jnp.logical_and(has_back, in_answer))(sum_answer)

    def columns_at(c):
        return pl.ds(c * BACK_COLS, BACK_COLS)

    def grad_copy(c, target, send_sem):
        return pltpu.make_async_remote_copy(
            src_ref=grad.at[:, columns_at(c)],
            dst_ref=pg_hbm.at[0, :, columns_at(c)],
            send_sem=send_sem,
            recv_sem=prev_recv.at[c],
            device_id=target,
            device_id_type=pl.DeviceIdType.MESH,
        )

    prev_copies = [
        grad_copy(c, {"section": (section + 3) % 4}, prev_send.at[c]) for c in range(BACK_STEPS)
    ]
    first_relay, second_relay, third_relay = [], [], []
    for i, c in enumerate(ROUND):
        at = columns_at(c)
        first_relay.append(
            pltpu.make_async_remote_copy(
                src_ref=grad.at[:, at],
                dst_ref=grad.at[:, at],
                send_sem=prev_send.at[c],
                recv_sem=relay_recv.at[i],
                device_id={"section": (section + 2) % 4, "seq": across_y},
                device_id_type=pl.DeviceIdType.MESH,
            )
        )
        second_relay.append(
            pltpu.make_async_remote_copy(
                src_ref=grad.at[:, at],
                dst_ref=relay.at[i],
                send_sem=prev_send.at[c],
                recv_sem=relay_recv.at[i],
                device_id={"section": (section + 3) % 4},
                device_id_type=pl.DeviceIdType.MESH,
            )
        )
        third_relay.append(
            pltpu.make_async_remote_copy(
                src_ref=relay.at[i],
                dst_ref=pg_hbm.at[0, :, at],
                send_sem=relay_send.at[i],
                recv_sem=prev_recv.at[c],
                device_id={"section": (section + 2) % 4, "seq": across_y},
                device_id_type=pl.DeviceIdType.MESH,
            )
        )

    def back_through_norm():
        back_all = back[...]
        along = jnp.sum(back_all.astype(f32) * acc[ROWS:, :], axis=1, keepdims=True)
        along = along * (inv_src * inv_src) * (1.0 / D)
        for c in range(BACK_STEPS):
            at = columns_at(c)
            w = jnp.concatenate(
                [wqkv[2 * c : 2 * c + 2, g].reshape(BACK_COLS, HD) for g in range(QKV // HD)],
                axis=1,
            )
            u = nt(back_all, w) * gain[:, at]
            grad[:, at] = (
                cot[:, at].astype(f32) + inv_src * u - src[:, at].astype(f32) * along
            ).astype(bf16)
            if c in ROUND:
                pl.when(section == 2)(first_relay[ROUND.index(c)].start)
                pl.when(section != 2)(prev_copies[c].start)
            else:
                prev_copies[c].start()

    def pass_on():
        for arriving, leaving in zip(first_relay, second_relay):
            arriving.wait_recv()
            leaving.start()

    def pass_on_last():
        for arriving, leaving in zip(second_relay, third_relay):
            arriving.wait_recv()
            leaving.start()

    pl.when(has_back)(back_through_norm)
    pl.when(section == 2)(output_late)
    pl.when(section == 0)(pass_on)
    pl.when(is_last)(pass_on_last)

    g1.finish(wqkv.at[pl.ds(0, SEQ - 1)])
    g2.finish(wout.at[pl.ds(0, SEQ - 1)])
    pl.when(in_prompt)(each([along_z(dz) for dz in (1, 3, 2)], "wait_send"))
    for copy in kv_sent:
        copy.wait_send()
    def keys_sent():
        for side in range(2):

            def sent_on(there, carry, side=side):
                pl.when(there != own)(to_summer(side, there).wait_send)
                return carry

            lax.fori_loop(0, 8, sent_on, 0)
            pl.when(z != side)(column_copy(side).wait_send)
        pl.when(in_answer)(to_partner.wait_send)

    pl.when(sends_keys)(keys_sent)
    pl.when(not_last)(each(next_copies, "wait_send"))
    pl.when(section > 0)(each(next_copies, "wait_recv"))
    straight = [prev_copies[c] for c in range(BACK_STEPS) if c not in ROUND]
    around = [prev_copies[c] for c in ROUND]
    pl.when(has_back)(each(straight, "wait_send"))
    pl.when(jnp.logical_and(has_back, section != 2))(each(around, "wait_send"))
    pl.when(section == 2)(each(first_relay, "wait_send"))
    pl.when(section == 0)(each(second_relay, "wait_send"))
    pl.when(is_last)(each(third_relay, "wait_send"))
    pl.when(not_last)(each(prev_copies, "wait_recv"))


def angle_tables():
    frequency = ROPE_BASE ** (-2.0 * np.arange(HD // 2) / HD)

    def table(positions):
        angles = np.asarray(positions, np.float64)[:, None] * frequency[None, :]
        cosine, sine = np.cos(angles), np.sin(angles)
        return (
            np.concatenate([cosine, cosine], axis=1).astype(np.float32),
            np.concatenate([-sine, sine], axis=1).astype(np.float32),
        )

    within = table(np.arange(BLK))
    blocks = [part[:, None, :] for part in table(np.arange(PBLK + 2) * BLK)]
    return (*within, *blocks)


def per_device(
    hidden_in,
    saved_hidden,
    grad_in,
    norm_gain,
    w_query,
    w_key,
    w_value,
    w_out,
    head,
    block_table,
    resp_lengths,
    pairs,
):
    any_spec = pl.BlockSpec(memory_space=pl.ANY)
    vmem = pl.BlockSpec(memory_space=pltpu.VMEM)
    smem = pl.BlockSpec(memory_space=pltpu.SMEM)
    dma = pltpu.SemaphoreType.DMA
    out = jax.ShapeDtypeStruct((1, ROWS, D), bf16)
    next_hidden, prev_grad = pl.pallas_call(
        layer_kernel,
        out_shape=(out, out),
        in_specs=[smem] * 3 + [any_spec] * 7 + [vmem] * 6,
        out_specs=(any_spec, any_spec),
        scratch_shapes=[
            pltpu.SMEM((PBLK + 2,), jnp.int32),
            pltpu.VMEM((ROWS, D), bf16),
            pltpu.VMEM((ROWS, D), bf16),
            pltpu.VMEM((ROWS, D), bf16),
            pltpu.VMEM((SEQ, 2 * ROWS, 256), bf16),
            pltpu.VMEM((SEQ, QKV // HD, 256, HD), bf16),
            pltpu.VMEM((SEQ, 16, D), bf16),
            pltpu.VMEM((2 * ROWS, QKV), f32),
            pltpu.VMEM((2, QH * ROWS, HD), bf16),
            pltpu.VMEM((2, 8, BLK, 512), bf16),
            pltpu.VMEM((2, BLK, 512), bf16),
            pltpu.VMEM((2, ROWS, QH * HD), bf16),
            pltpu.VMEM((ROWS, D), bf16),
            pltpu.VMEM((ROWS, 128), f32),
            pltpu.VMEM((ROWS, 128), f32),
            pltpu.VMEM((QH * HD, ROWS), f32),
            pltpu.VMEM((QH * ROWS, HD), bf16),
            pltpu.VMEM((2, 8, BLK, 256), bf16),
            pltpu.VMEM((2, BLK, 256), bf16),
            pltpu.VMEM((8, 2, BLK, 256), bf16),
            pltpu.VMEM((BLK, 256), bf16),
            pltpu.VMEM((2, BLK, 256), bf16),
            pltpu.VMEM((4, BLK, 256), bf16),
            pltpu.VMEM((2, 8, 8, 128), f32),
            pltpu.VMEM((ROWS, QKV), bf16),
            pltpu.VMEM((ROWS, D), bf16),
            pltpu.VMEM((len(ROUND), ROWS, BACK_COLS), bf16),
            dma((10,)),
            dma((2,)),
            dma((240,)),
            dma((160,)),
            dma((4,)),
            dma((2,)),
            dma((32,)),
            dma((32,)),
            dma((2,)),
            dma((16,)),
            dma((16,)),
            dma((2,)),
            dma((2,)),
            dma((4,)),
            dma((8,)),
            dma((9,)),
            dma((OUT_STEPS,)),
            dma((OUT_STEPS,)),
            dma((BACK_STEPS,)),
            dma((BACK_STEPS,)),
            dma((len(ROUND),)),
            dma((len(ROUND),)),
        ],
        compiler_params=pltpu.CompilerParams(
            collective_id=0, has_side_effects=True, vmem_limit_bytes=60 * 1024 * 1024
        ),
        cost_estimate=pl.CostEstimate(
            flops=12_000_000_000, bytes_accessed=12_000_000, transcendentals=4_000_000
        ),
    )(
        block_table,
        resp_lengths,
        pairs.T,
        hidden_in,
        saved_hidden,
        grad_in,
        w_query,
        w_key,
        w_value,
        w_out,
        norm_gain,
        head.reshape(D // 128, 128),
        *angle_tables(),
    )
    section = lax.axis_index("section")
    nothing = jnp.zeros((), bf16)
    return (
        jnp.where(section == 0, nothing, next_hidden),
        jnp.where(section == SECTIONS - 1, nothing, prev_grad),
    )


def solution(mesh):
    rows = P("section", "seq", None)
    return jax.shard_map(
        per_device,
        mesh=mesh,
        in_specs=(rows, rows, rows, P("section", None), rows, rows, rows, rows, P(), P(), P(), P()),
        out_specs=(rows, rows),
        check_vma=False,
    )
```

```python
import math

import jax
import jax.numpy as jnp
import numpy as np
from jax import lax
from jax.experimental import pallas as pl
from jax.experimental.pallas import tpu as pltpu
from jax.sharding import PartitionSpec as P

HD = 128
QH = 4
RESP = 8
PAIRS = 28
SECTIONS = 4
BLK = 128
D = 8192
ROWS = 128
SEQ = 32
PBLK = 16
PROMPT = 2048
QKV = 768
EPSILON = 1e-05
ROPE_BASE = 500000.0
LOSS_SCALE = 1024.0
NEGATIVE = -1e30
FAR = 1 << 30
SCALE = HD**-0.5
LOG2 = SCALE / math.log(2.0)
OUT_COLS = 1024
OUT_STEPS = D // OUT_COLS
MIX_COLS = 512
MIX_STEPS = D // MIX_COLS
MIX_FIRST = 2 * 2816 // MIX_COLS
BACK_COLS = 512
BACK_STEPS = D // BACK_COLS
ROUND = (2, 7, 12)

f32 = jnp.float32
bf16 = jnp.bfloat16

FIRST = ((0, 0), (1, 0), (0, 1), (0, 3), (1, 1), (1, 3), (0, 2), (1, 2))
LAST = (0, 1, 3, 2)
LAG_ON, LAG_ACROSS = 2, 4
STEPS = len(FIRST) + LAG_ACROSS
QKV_WAYS = (
    (True, "xz"),
    (True, "zx"),
    (True, "xz"),
    (True, "zx"),
    (False, "xz"),
    (False, "zx"),
)
OUT_WAYS = ((True, "xz"), (True, "zx"), (False, "xz"), (False, "zx"))


def nt(a, b):
    return lax.dot_general(a, b, (((1,), (1,)), ((), ())), preferred_element_type=f32)


def tn(a, b):
    return lax.dot_general(a, b, (((0,), (0,)), ((), ())), preferred_element_type=f32)


def nn(a, b):
    return jnp.dot(a, b, preferred_element_type=f32)


class Place:
    def __init__(self):
        self.seq = lax.axis_index("seq")
        z, y, x = self.seq // 8, lax.rem(self.seq // 4, 2), lax.rem(self.seq, 4)
        self.zs = [lax.rem(z + d, 4) for d in range(4)]
        self.ys = [lax.rem(y + d, 2) * 4 for d in range(2)]
        self.xs = [lax.rem(x + d, 4) for d in range(4)]
        self.z_rows = [d * 8 for d in self.zs]

    def at(self, dz=0, dy=0, dx=0):
        return self.z_rows[dz % 4] + self.ys[dy % 2] + self.xs[dx % 4]


class Part:
    def __init__(self, place, view, y_first, axes, send_sem, recv_sems, base):
        self.place, self.view, self.y_first, self.axes = place, view, y_first, axes
        self.send_sem, self.recv_sems = send_sem, recv_sems
        self.slots = {}
        for dy in range(2):
            for da in range(4):
                for db in range(4):
                    if y_first:
                        halves = 2 if (da == 2 and db == 0) or db == 2 else 1
                    else:
                        halves = 2 if dy == 0 and ((da == 2 and db == 0) or db == 2) else 1
                    for sub in range(halves):
                        if (dy, da, db) != (0, 0, 0):
                            self.slots[(dy, da, db, sub)] = base + len(self.slots)

    def origin(self, dy, da, db):
        dx, dz = (da, db) if self.axes == "xz" else (db, da)
        return self.place.at(dz, dy, dx)

    def push(self, dy, da, db, axis, step=1, sub=None):
        if axis == "y":
            target, key = self.place.at(0, 1, 0), (1 - dy, da, db, 0)
        else:
            along_x = (axis == "a") == (self.axes == "xz")
            target = self.place.at(0, 0, step) if along_x else self.place.at(step, 0, 0)
            if axis == "a":
                key = (dy, (da - step) % 4, db, sub or 0)
            else:
                key = (dy, da, (db - step) % 4, sub or 0)
        ref = self.view(self.origin(dy, da, db), sub)
        pltpu.make_async_remote_copy(
            src_ref=ref,
            dst_ref=ref,
            send_sem=self.send_sem.at[0],
            recv_sem=self.recv_sems.at[self.slots[key]],
            device_id={"seq": target},
            device_id_type=pl.DeviceIdType.MESH,
        ).start()

    def take(self, dy, da, db, sub=None):
        ref = self.view(self.origin(dy, da, db), sub)
        pltpu.make_async_remote_copy(
            src_ref=ref,
            dst_ref=ref,
            send_sem=self.send_sem.at[0],
            recv_sem=self.recv_sems.at[self.slots[(dy, da, db, sub or 0)]],
            device_id={"seq": self.place.at(0, 1, 0)},
            device_id_type=pl.DeviceIdType.MESH,
        ).wait_recv()

    def both(self, dy, da, db, axis):
        self.push(dy, da, db, axis, 1)
        self.push(dy, da, db, axis, -1)

    def begin(self):
        self.push(0, 0, 0, "y")
        self.both(0, 0, 0, "a")
        self.both(0, 0, 0, "b")

    def from_first_ring(self, dy, da):
        if da == 2:
            self.take(dy, 2, 0, 0)
            self.take(dy, 2, 0, 1)
        elif (dy, da) != (0, 0):
            self.take(dy, da, 0)
            if da == 0:
                self.both(dy, 0, 0, "a")
            else:
                self.push(dy, da, 0, "a", -1 if da == 1 else 1, 1 if da == 1 else 0)
        if (dy, da) != (0, 0):
            self.both(dy, da, 0, "b")
            if not self.y_first:
                self.push(dy, da, 0, "y")

    def from_second_ring(self, dy, da):
        for db in (1, 3):
            self.take(dy, da, db)
            self.push(dy, da, db, "b", -1 if db == 1 else 1, 1 if db == 1 else 0)
            if not self.y_first:
                self.push(dy, da, db, "y")

    def across_second_ring(self, dy, da):
        self.take(dy, da, 2, 0)
        self.take(dy, da, 2, 1)
        if not self.y_first:
            self.push(dy, da, 2, "y")

    def step(self, k):
        order = FIRST if self.y_first else tuple((0, da) for da in LAST)
        here = []
        if k < len(order):
            self.from_first_ring(*order[k])
        if 0 <= k - LAG_ON < len(order):
            dy, da = order[k - LAG_ON]
            self.from_second_ring(dy, da)
            here += [self.origin(dy, da, db) for db in (0, 1, 3)]
        if 0 <= k - LAG_ACROSS < len(order):
            dy, da = order[k - LAG_ACROSS]
            self.across_second_ring(dy, da)
            here.append(self.origin(dy, da, 2))
        if not self.y_first and STEPS - 4 <= k:
            da = LAST[k - (STEPS - 4)]
            for db in (0, 1, 3, 2):
                self.take(1, da, db)
                here.append(self.origin(1, da, db))
        return here


class Gather:
    def __init__(self, place, views, ways, send_sem, recv_sems):
        self.send_sem, self.parts, base = send_sem, [], 0
        for view, (y_first, axes) in zip(views, ways):
            part = Part(place, view, y_first, axes, send_sem, recv_sems, base)
            base += len(part.slots)
            self.parts.append(part)
        self.place = place

    def begin(self):
        for part in self.parts:
            part.begin()

    def step(self, *steps):
        if len(steps) == 1 and isinstance(steps[0], int):
            steps = [(i, steps[0]) for i in range(len(self.parts))]
        return [(i, o) for i, k in steps if 0 <= k < STEPS for o in self.parts[i].step(k)]

    def finish(self, whole):
        pltpu.make_async_remote_copy(
            src_ref=whole,
            dst_ref=whole,
            send_sem=self.send_sem.at[0],
            recv_sem=self.send_sem.at[0],
            device_id={"seq": self.place.at(0, 1, 0)},
            device_id_type=pl.DeviceIdType.MESH,
        ).wait_send()


def layer_kernel(
    block_table,
    lengths,
    pairs,
    hid_hbm,
    sav_hbm,
    gin_hbm,
    wq_hbm,
    wk_hbm,
    wv_hbm,
    wo_hbm,
    gain,
    head,
    cos_in,
    sin_in,
    cos_block,
    sin_block,
    nh_hbm,
    pg_hbm,
    key_pos_of,
    hid,
    src,
    cot,
    xn,
    wqkv,
    wout,
    acc,
    queries,
    kv,
    pair_kv,
    mixed,
    layer_out,
    squares,
    products,
    mixing,
    dheads,
    dkv,
    pair_dkv,
    landed,
    pair_landed,
    column,
    column_landed,
    tiles,
    back,
    grad,
    relay,
    load_sems,
    weight_send,
    g1_recv,
    g2_recv,
    kvz_send,
    kvz_recv,
    kv_send,
    kv_recv,
    pair_sems,
    rs_send,
    rs_recv,
    pair_back_sems,
    column_send,
    column_recv,
    tile_send,
    tile_recv,
    next_send,
    next_recv,
    prev_send,
    prev_recv,
    relay_send,
    relay_recv,
):
    place = Place()
    seq, z = place.seq, place.zs[0]
    own = place.ys[0] + place.xs[0]
    section = lax.axis_index("section")
    is_last = section == SECTIONS - 1
    not_last = section < SECTIONS - 1
    parity = seq % 2
    partner = seq + 1 - 2 * parity
    in_prompt = seq < PBLK
    in_answer = seq >= PBLK
    has_back = section > 0
    from_grad = jnp.logical_and(has_back, not_last)
    sends_keys = jnp.logical_and(has_back, jnp.logical_or(not_last, in_answer))
    last_prompt = jnp.logical_and(is_last, in_prompt)
    across_y = place.at(0, 1, 0)

    def other(index):
        return {"seq": index}

    def beside(j):
        return lax.rem(own + j, 8)

    loads = [
        pltpu.make_async_copy(wk_hbm.at[0], wqkv.at[seq, 4], load_sems.at[0]),
        pltpu.make_async_copy(wv_hbm.at[0], wqkv.at[seq, 5], load_sems.at[1]),
    ]
    for h in range(QH):
        loads.append(
            pltpu.make_async_copy(
                wq_hbm.at[0, :, pl.ds(h * HD, HD)], wqkv.at[seq, h], load_sems.at[2 + h]
            )
        )
    hid_load = pltpu.make_async_copy(hid_hbm.at[0], hid, load_sems.at[6])
    saved_load = pltpu.make_async_copy(sav_hbm.at[0], src, load_sems.at[7])
    again_load = pltpu.make_async_copy(hid_hbm.at[0], src, load_sems.at[7])
    wout_load = pltpu.make_async_copy(wo_hbm.at[0], wout.at[seq], load_sems.at[8])
    cot_load = pltpu.make_async_copy(gin_hbm.at[0], cot, load_sems.at[9])
    for load in loads:
        load.start()
    barrier = pltpu.get_barrier_semaphore()

    def greet(index):
        pl.semaphore_signal(
            barrier, inc=1, device_id=other(index), device_id_type=pl.DeviceIdType.MESH
        )

    for j in range(1, 8):
        greet(z * 8 + beside(j))
    for dz in range(1, 4):
        greet(place.at(dz))
    for step in (1, 3):
        pl.semaphore_signal(
            barrier,
            inc=1,
            device_id={"section": (section + step) % 4},
            device_id_type=pl.DeviceIdType.MESH,
        )

    half = seq % 2
    answer = jnp.maximum(seq - PBLK, 0) // 2
    own_block = jnp.where(in_prompt, block_table[seq % PBLK], PBLK + half)
    length = lengths[answer]
    first_pos = own_block * BLK
    limit = jnp.where(in_prompt, FAR, PROMPT + length)
    end_row = jnp.where(in_prompt, -1, length - 1 - half * BLK)
    for b in range(PBLK):
        key_pos_of[b] = block_table[b] * BLK
    for b in range(2):
        key_pos_of[PBLK + b] = jnp.where(in_prompt, FAR, PROMPT + b * BLK)
    cos_b, sin_b = cos_block[own_block], sin_block[own_block]
    cos = cos_in[...] * cos_b - sin_in[...] * sin_b
    sin = sin_in[...] * cos_b + cos_in[...] * sin_b

    pl.semaphore_signal(
        barrier,
        inc=1,
        device_id={"section": (section + 2) % 4, "seq": across_y},
        device_id_type=pl.DeviceIdType.MESH,
    )
    for load in loads:
        load.wait()
    hid_load.start()
    pl.when(not_last)(saved_load.start)
    pl.when(is_last)(again_load.start)
    wout_load.start()
    cot_load.start()
    pl.semaphore_wait(barrier, 13)

    def qkv_view(group):
        def view(o, sub):
            if sub is None:
                return wqkv.at[o, group]
            return wqkv.at[o, group, pl.ds(sub * 128, 128), :]

        return view

    def out_view(first, size):
        def view(o, sub):
            if sub is None:
                return wout.at[o, :, pl.ds(first, size)]
            return wout.at[o, :, pl.ds(first + sub * (size // 2), size // 2)]

        return view

    groups = (4, 5, 0, 1, 2, 3)
    g1 = Gather(
        place, [qkv_view(g) for g in groups], QKV_WAYS, weight_send.at[pl.ds(0, 1)], g1_recv
    )
    columns = ((0, 2816), (2816, 2816), (5632, 1280), (6912, 1280))
    g2 = Gather(
        place, [out_view(*c) for c in columns], OUT_WAYS, weight_send.at[pl.ds(1, 1)], g2_recv
    )
    g1.begin()

    acc[...] = jnp.zeros_like(acc)

    def inverse_rms(buf):
        def body(i, total):
            wide = buf[:, pl.ds(pl.multiple_of(i * 512, 512), 512)].astype(f32)
            wide = wide * wide
            return total + (
                (wide[:, :128] + wide[:, 128:256]) + (wide[:, 256:384] + wide[:, 384:])
            )

        total = lax.fori_loop(0, 16, body, jnp.zeros((ROWS, 128), f32))
        return lax.rsqrt(jnp.sum(total, axis=1, keepdims=True) * (1.0 / D) + EPSILON)

    def normalize(buf, row):
        inv = inverse_rms(buf)

        def body(i, carry):
            at = pl.ds(pl.multiple_of(i * 256, 256), 256)
            xn[i, pl.ds(row, ROWS), :] = (buf[:, at].astype(f32) * inv * gain[:, at]).astype(bf16)
            return carry

        lax.fori_loop(0, SEQ, body, 0)
        return inv

    def project(here):
        for i, o in here:
            g = groups[i]
            acc[:, g * HD : (g + 1) * HD] += nn(xn[o], wqkv[o, g])

    def qkv_step(t):
        return g1.step((0, t), (1, t), (5, t - 1), (4, t - 2), (2, t - 3), (3, t - 3))

    hid_load.wait()
    normalize(hid, 0)
    first_here = qkv_step(0)
    saved_load.wait()
    inv_src = normalize(src, ROWS)
    wout_load.wait()
    cot_load.wait()
    first_here += qkv_step(1)
    project(first_here)
    for t in range(2, STEPS):
        if t == STEPS - 4:
            g2.begin()
        project(qkv_step(t))
    g2.step(0)

    def rotated(t, g):
        u = acc[t * ROWS : (t + 1) * ROWS, g * HD : (g + 1) * HD]
        return (u * cos + pltpu.roll(u, HD // 2, 1) * sin).astype(bf16)

    for t in range(2):
        pair_kv[parity, :, t * 256 : t * 256 + 128] = rotated(t, 4)
        pair_kv[parity, :, t * 256 + 128 : t * 256 + 256] = acc[
            t * ROWS : (t + 1) * ROWS, 640:768
        ].astype(bf16)

    pair_copy = pltpu.make_async_remote_copy(
        src_ref=pair_kv.at[parity],
        dst_ref=pair_kv.at[parity],
        send_sem=pair_sems.at[0],
        recv_sem=pair_sems.at[1],
        device_id=other(partner),
        device_id_type=pl.DeviceIdType.MESH,
    )

    def along_z(dz):
        return pltpu.make_async_remote_copy(
            src_ref=kv.at[z % 2, own],
            dst_ref=kv.at[z % 2, own],
            send_sem=kvz_send.at[dz],
            recv_sem=kvz_recv.at[z % 2],
            device_id=other(place.at(dz)),
            device_id_type=pl.DeviceIdType.MESH,
        )

    def send_along_z():
        kv[z, own] = pair_kv[parity]
        for dz in (1, 3, 2):
            along_z(dz).start()

    pl.when(in_prompt)(send_along_z)
    pair_copy.start()

    kv_sent, kv_slots = [], {}

    def kv_piece(dy, dx, rows):
        return kv.at[:, place.ys[dy % 2] + place.xs[dx % 4], pl.ds(*rows)]

    def kv_slot(dy, dx, rows):
        return kv_slots.setdefault((dy % 2, dx % 4, rows), len(kv_slots))

    def kv_push(dy, dx, rows, to_y, to_x):
        ref = kv_piece(dy, dx, rows)
        copy = pltpu.make_async_remote_copy(
            src_ref=ref,
            dst_ref=ref,
            send_sem=kv_send.at[len(kv_sent)],
            recv_sem=kv_recv.at[kv_slot(dy - to_y, dx - to_x, rows)],
            device_id=other(place.at(0, to_y, to_x)),
            device_id_type=pl.DeviceIdType.MESH,
        )
        kv_sent.append(copy)
        copy.start()

    def kv_take(dy, dx, rows):
        ref = kv_piece(dy, dx, rows)
        pltpu.make_async_remote_copy(
            src_ref=ref,
            dst_ref=ref,
            send_sem=kv_send.at[0],
            recv_sem=kv_recv.at[kv_slot(dy, dx, rows)],
            device_id=other(place.at(0, 1, 0)),
            device_id_type=pl.DeviceIdType.MESH,
        ).wait_recv()

    y_rows, x_rows = (0, 64), (64, 64)

    def halves_of(rows):
        return (rows[0], 32), (rows[0] + 32, 32)

    def kv_ring(dy, rows):
        kv_push(dy, 0, rows, 0, 1)
        kv_push(dy, 0, rows, 0, -1)

    def kv_ring_on(dy, rows):
        low, high = halves_of(rows)
        kv_take(dy, 1, rows)
        kv_push(dy, 1, high, 0, -1)
        kv_take(dy, 3, rows)
        kv_push(dy, 3, low, 0, 1)

    def kv_ring_end(dy, rows):
        for part in halves_of(rows):
            kv_take(dy, 2, part)

    def kv_step(k):
        if k == 0:
            for source in range(2):

                def wait(source=source):
                    pltpu.make_async_remote_copy(
                        src_ref=kv.at[source, own],
                        dst_ref=kv.at[source, own],
                        send_sem=kvz_send.at[0],
                        recv_sem=kvz_recv.at[source],
                        device_id=other(partner),
                        device_id_type=pl.DeviceIdType.MESH,
                    ).wait_recv()

                pl.when(z != source)(wait)
            kv_push(0, 0, y_rows, 1, 0)
            kv_ring(0, x_rows)
            kv_ring(0, y_rows)
            kv_push(0, 0, x_rows, 1, 0)
        elif k == 1:
            kv_take(1, 0, y_rows)
            kv_ring(1, y_rows)
            kv_ring_on(0, x_rows)
            kv_push(0, 1, x_rows, 1, 0)
            kv_push(0, 3, x_rows, 1, 0)
            kv_ring_on(0, y_rows)
        elif k == 2:
            kv_ring_end(0, x_rows)
            kv_push(0, 2, x_rows, 1, 0)
            kv_ring_on(1, y_rows)
        else:
            kv_ring_end(0, y_rows)
            kv_ring_end(1, y_rows)
            for dx in range(4):
                kv_take(1, dx, x_rows)

    project(qkv_step(STEPS))
    g2.step(1)
    kv_step(0)
    project(qkv_step(STEPS + 1))
    g2.step(2)
    project(qkv_step(STEPS + 2))
    kv_step(1)
    for t in range(2):
        for h in range(QH):
            queries[t, h * HD : (h + 1) * HD, :] = rotated(t, h)
    g2.step(3)
    kv_step(2)
    g2.step(4)
    g2.step(5)
    kv_step(3)
    g2.step(6)
    pair_copy.wait_send()
    pltpu.make_async_remote_copy(
        src_ref=pair_kv.at[parity],
        dst_ref=pair_kv.at[1 - parity],
        send_sem=pair_sems.at[0],
        recv_sem=pair_sems.at[1],
        device_id=other(partner),
        device_id_type=pl.DeviceIdType.MESH,
    ).wait_recv()

    across = lax.broadcasted_iota(jnp.int32, (1, QH * ROWS), 1) % ROWS
    query_pos = first_pos + across
    down = lax.broadcasted_iota(jnp.int32, (2 * BLK, 1), 0)

    def allowed(c):
        key_pos = jnp.where(
            down < BLK, key_pos_of[2 * c] + down, key_pos_of[2 * c + 1] + (down - BLK)
        )
        key_pos = jnp.where(key_pos < limit, key_pos, FAR)
        return key_pos <= query_pos

    def block_of(c, at):
        if isinstance(c, int) and c == PBLK // 2:
            return pair_kv[:, :, at].reshape(2 * BLK, HD)
        side, first = c // 4, lax.rem(c, 4) * 2
        return kv[pl.ds(side, 1), pl.ds(first, 2), :, at].reshape(2 * BLK, HD)

    def keys_of(c, t):
        return block_of(c, slice(t * 256, t * 256 + 128))

    def values_of(c, t):
        return block_of(c, slice(t * 256 + 128, t * 256 + 256))

    def attend(t, between):
        q = queries[t]

        def chunk(c, carry):
            row_max, total, weighted = carry
            scores = jnp.where(allowed(c), nt(keys_of(c, t), q), NEGATIVE)
            new_max = jnp.maximum(row_max, jnp.max(scores, axis=0, keepdims=True))
            weights = jnp.exp2((scores - new_max) * LOG2)
            factor = jnp.exp2((row_max - new_max) * LOG2)
            total = total * factor + jnp.sum(weights, axis=0, keepdims=True)
            weighted = weighted * factor + tn(values_of(c, t), weights.astype(bf16))
            return new_max, total, weighted

        carry = (
            jnp.full((1, QH * ROWS), NEGATIVE, f32),
            jnp.zeros((1, QH * ROWS), f32),
            jnp.zeros((HD, QH * ROWS), f32),
        )
        for start, then in zip((0, 4), between):
            carry = lax.fori_loop(start, start + 4, chunk, carry, unroll=2)
            for k in then:
                g2.step(k)
        carry = chunk(PBLK // 2, carry)
        row_max, total, weighted = carry
        weighted = weighted / total
        for h in range(QH):
            mixed[t, :, h * HD : (h + 1) * HD] = weighted[:, h * HD : (h + 1) * HD].T.astype(bf16)
        return row_max * LOG2 + jnp.log2(total)

    log_total = attend(1, ((7,), (8,)))

    def attend_early():
        attend(0, ((), ()))

    early = section == 0
    pl.when(early)(attend_early)

    for k in range(9, STEPS):
        g2.step((0, k), (1, k))
    g2.step((2, 9), (3, 9))

    next_copies = [
        pltpu.make_async_remote_copy(
            src_ref=layer_out.at[:, pl.ds(c * OUT_COLS, OUT_COLS)],
            dst_ref=nh_hbm.at[0, :, pl.ds(c * OUT_COLS, OUT_COLS)],
            send_sem=next_send.at[c],
            recv_sem=next_recv.at[c],
            device_id={"section": (section + 1) % 4},
            device_id_type=pl.DeviceIdType.MESH,
        )
        for c in range(OUT_STEPS)
    ]

    def output(steps):
        mixed_now = mixed[0]
        for c in steps:
            at = pl.ds(c * OUT_COLS, OUT_COLS)
            w = wout[:, :, at].reshape(QH * HD, OUT_COLS)
            y = (nn(mixed_now, w) + hid[:, at].astype(f32)).astype(bf16)
            layer_out[:, at] = y
            pl.when(not_last)(next_copies[c].start)

    def measure_output():
        def body(i, carry):
            square, product = carry
            wide = layer_out[:, pl.ds(pl.multiple_of(i * 128, 128), 128)].astype(f32)
            return square + wide * wide, product + wide * head[pl.ds(i, 1), :]

        none = jnp.zeros((ROWS, 128), f32)
        squares[...], products[...] = lax.fori_loop(0, D // 128, body, (none, none))

    def mix_back(steps):
        def body(c, total):
            at = pl.ds(pl.multiple_of(c * MIX_COLS, MIX_COLS), MIX_COLS)
            return total + nt(wout[:, :, at].reshape(QH * HD, MIX_COLS), cot[:, at])

        mixing[...] = lax.fori_loop(steps[0], steps[1], body, mixing[...], unroll=True)

    mixing[...] = jnp.zeros_like(mixing)
    pl.when(from_grad)(lambda: mix_back((0, MIX_FIRST)))
    for k in range(10, STEPS):
        g2.step((2, k), (3, k))
    pl.when(early)(lambda: output(range(OUT_STEPS)))
    pl.when(from_grad)(lambda: mix_back((MIX_FIRST, MIX_STEPS)))

    def each(copies, what):
        def run():
            for copy in copies:
                getattr(copy, what)()

        return run

    def reward_rows():
        mixed[0] = mixed[1]
        output(range(OUT_STEPS))
        measure_output()
        mean_square = jnp.sum(squares[...], axis=1, keepdims=True) * (1.0 / D)
        dots = jnp.sum(products[...], axis=1, keepdims=True)
        inv = lax.rsqrt(mean_square + EPSILON)
        rows = lax.broadcasted_iota(jnp.int32, (ROWS, 1), 0)
        hit = rows == end_row
        reward = jnp.sum(jnp.where(hit, dots * inv, 0.0), axis=0, keepdims=True)
        side = z - 2
        tiles[side, own] = jnp.broadcast_to(reward, (8, 128))
        to_z = pltpu.make_async_remote_copy(
            src_ref=tiles.at[side, own],
            dst_ref=tiles.at[side, own],
            send_sem=tile_send.at[0],
            recv_sem=tile_recv.at[8],
            device_id=other((3 - side) * 8 + own),
            device_id_type=pl.DeviceIdType.MESH,
        )
        to_z.start()
        down8 = lax.broadcasted_iota(jnp.int32, (RESP, 128), 0)
        sign = jnp.zeros((RESP, 128), f32)
        for p in range(PAIRS):
            won, lost = pairs[0, p], pairs[1, p]
            sign += jnp.where(lost == answer, (down8 == won).astype(f32), 0.0)
            sign -= jnp.where(won == answer, (down8 == lost).astype(f32), 0.0)
        pltpu.make_async_remote_copy(
            src_ref=tiles.at[1 - side, own],
            dst_ref=tiles.at[1 - side, own],
            send_sem=tile_send.at[0],
            recv_sem=tile_recv.at[8],
            device_id=other(partner),
            device_id_type=pl.DeviceIdType.MESH,
        ).wait_recv()
        copies = [to_z]
        for j in range(1, 8):
            copies.append(
                pltpu.make_async_remote_copy(
                    src_ref=tiles.at[:, own],
                    dst_ref=tiles.at[:, own],
                    send_sem=tile_send.at[j],
                    recv_sem=tile_recv.at[own],
                    device_id=other(z * 8 + beside(j)),
                    device_id_type=pl.DeviceIdType.MESH,
                )
            )
            copies[-1].start()
        for j in range(1, 8):
            pltpu.make_async_remote_copy(
                src_ref=tiles.at[:, own],
                dst_ref=tiles.at[:, beside(j)],
                send_sem=tile_send.at[0],
                recv_sem=tile_recv.at[beside(j)],
                device_id=other(partner),
                device_id_type=pl.DeviceIdType.MESH,
            ).wait_recv()
        for copy in copies:
            copy.wait_send()
        mine = (tiles[side, own] + tiles[side, own + 1 - 2 * parity])[0:1]
        pull = jnp.zeros((1, 128), f32)
        for r in range(RESP):
            way = sign[r : r + 1, :]
            first = 2 * (r % 4)
            reward_r = (tiles[r // 4, first] + tiles[r // 4, first + 1])[0:1]
            pull += way / (1.0 + jnp.exp(way * (reward_r - mine)))
        pull = pull * (LOSS_SCALE / PAIRS)
        row_grad = jnp.where(hit, jnp.sum(pull, axis=1, keepdims=True) * (1.0 / 128.0), 0.0)
        by_head = row_grad * inv
        by_out = row_grad * (inv * inv * inv) * (dots * (1.0 / D))

        def body(i, carry):
            at = pl.ds(pl.multiple_of(i * 128, 128), 128)
            wide = layer_out[:, at].astype(f32)
            cot[:, at] = (by_head * head[pl.ds(i, 1), :] - wide * by_out).astype(bf16)
            return carry

        lax.fori_loop(0, D // 128, body, 0)
        mix_back((0, MIX_STEPS))

    def no_rewards():
        cot[...] = jnp.zeros_like(cot)

    pl.when(jnp.logical_and(is_last, in_answer))(reward_rows)
    pl.when(last_prompt)(no_rewards)

    row_dots = []
    for h in range(QH):
        at = slice(h * HD, (h + 1) * HD)
        d_head = mixing[at, :].T.astype(bf16)
        dheads[at, :] = d_head
        dots = d_head.astype(f32) * mixed[1, :, at].astype(f32)
        row_dots.append(jnp.sum(dots.T, axis=0, keepdims=True))
    row_dots = jnp.concatenate(row_dots, axis=1)

    q = queries[1]
    dh = dheads[...]

    def attend_back(c, d_query):
        keys, values = keys_of(c, 1), values_of(c, 1)
        probs = jnp.exp2(jnp.where(allowed(c), nt(keys, q) * LOG2 - log_total, NEGATIVE))
        d_scores = (probs * (nt(values, dh) - row_dots)).astype(bf16)
        d_key = (nn(d_scores, q) * SCALE).astype(bf16)
        d_value = nn(probs.astype(bf16), dh).astype(bf16)
        both = jnp.concatenate([d_key, d_value], axis=1)
        if isinstance(c, int):
            pair_dkv[...] = both.reshape(2, BLK, 2 * HD)
        else:
            dkv[pl.ds(c // 4, 1), pl.ds(lax.rem(c, 4) * 2, 2)] = both.reshape(1, 2, BLK, 2 * HD)
        return d_query + tn(keys, d_scores)

    def to_summer(side, there):
        return pltpu.make_async_remote_copy(
            src_ref=dkv.at[side, there],
            dst_ref=landed.at[own, side],
            send_sem=rs_send.at[side * 8 + there],
            recv_sem=rs_recv.at[own * 2 + side],
            device_id=other(z * 8 + there),
            device_id_type=pl.DeviceIdType.MESH,
        )

    def back_chunk(i, d_query):
        side, pair = i // 4, lax.rem(own // 2 + 1 + i, 4)
        d_query = attend_back(side * 4 + pair, d_query)
        for j in range(2):
            there = pair * 2 + j
            pl.when(there != own)(to_summer(side, there).start)
        return d_query

    to_partner = pltpu.make_async_remote_copy(
        src_ref=pair_dkv.at[1 - parity],
        dst_ref=pair_landed,
        send_sem=pair_back_sems.at[0],
        recv_sem=pair_back_sems.at[1],
        device_id=other(partner),
        device_id_type=pl.DeviceIdType.MESH,
    )

    def back_through_keys():
        d_query = lax.fori_loop(0, 8, back_chunk, jnp.zeros((HD, QH * ROWS), f32), unroll=2)
        d_query = attend_back(PBLK // 2, d_query) * SCALE
        pl.when(in_answer)(to_partner.start)
        for h in range(QH):
            u = d_query[:, h * HD : (h + 1) * HD].T
            u = u * cos - pltpu.roll(u, HD // 2, 1) * sin
            back[:, h * HD : (h + 1) * HD] = u.astype(bf16)

    def no_query():
        back[:, 0:512] = jnp.zeros((ROWS, QH * HD), bf16)

    pl.when(sends_keys)(back_through_keys)
    pl.when(last_prompt)(no_query)

    def output_late():
        attend(0, ((), ()))
        output(range(OUT_STEPS))

    pl.when(section == 1)(output_late)

    def column_copy(side):
        return pltpu.make_async_remote_copy(
            src_ref=column.at[side],
            dst_ref=column_landed.at[z],
            send_sem=column_send.at[side],
            recv_sem=column_recv.at[z],
            device_id=other(side * 8 + own),
            device_id_type=pl.DeviceIdType.MESH,
        )

    def sum_plane():
        for side in range(2):

            def add(j, total, side=side):
                there = beside(j)
                pltpu.make_async_remote_copy(
                    src_ref=dkv.at[side, there],
                    dst_ref=landed.at[there, side],
                    send_sem=rs_send.at[0],
                    recv_sem=rs_recv.at[there * 2 + side],
                    device_id=other(partner),
                    device_id_type=pl.DeviceIdType.MESH,
                ).wait_recv()
                return total + landed[there, side].astype(f32)

            column[side] = lax.fori_loop(1, 8, add, dkv[side, own].astype(f32)).astype(bf16)
            pl.when(z != side)(column_copy(side).start)

    pl.when(sends_keys)(sum_plane)

    def keep(total):
        u = total[:, :HD]
        back[:, 512:640] = (u * cos - pltpu.roll(u, HD // 2, 1) * sin).astype(bf16)
        back[:, 640:768] = total[:, HD:].astype(bf16)

    def add_column(there, total):
        pltpu.make_async_remote_copy(
            src_ref=column.at[0],
            dst_ref=column_landed.at[there],
            send_sem=column_send.at[0],
            recv_sem=column_recv.at[there],
            device_id=other(partner),
            device_id_type=pl.DeviceIdType.MESH,
        ).wait_recv()
        return total + column_landed[there].astype(f32)

    def sum_prompt():
        def add(j, total):
            return add_column(lax.rem(z + j, 4), total)

        keep(lax.fori_loop(1, 4, add, column[z].astype(f32)))

    def sum_last_prompt():
        keep(lax.fori_loop(2, 4, add_column, jnp.zeros((BLK, 2 * HD), f32)))

    def sum_answer():
        to_partner.wait_recv()
        keep(pair_dkv[parity].astype(f32) + pair_landed[...].astype(f32))

    pl.when(jnp.logical_and(from_grad, in_prompt))(sum_prompt)
    pl.when(last_prompt)(sum_last_prompt)
    pl.when(jnp.logical_and(has_back, in_answer))(sum_answer)

    def columns_at(c):
        return pl.ds(c * BACK_COLS, BACK_COLS)

    def grad_copy(c, target, send_sem):
        return pltpu.make_async_remote_copy(
            src_ref=grad.at[:, columns_at(c)],
            dst_ref=pg_hbm.at[0, :, columns_at(c)],
            send_sem=send_sem,
            recv_sem=prev_recv.at[c],
            device_id=target,
            device_id_type=pl.DeviceIdType.MESH,
        )

    prev_copies = [
        grad_copy(c, {"section": (section + 3) % 4}, prev_send.at[c]) for c in range(BACK_STEPS)
    ]
    first_relay, second_relay, third_relay = [], [], []
    for i, c in enumerate(ROUND):
        at = columns_at(c)
        first_relay.append(
            pltpu.make_async_remote_copy(
                src_ref=grad.at[:, at],
                dst_ref=grad.at[:, at],
                send_sem=prev_send.at[c],
                recv_sem=relay_recv.at[i],
                device_id={"section": (section + 2) % 4, "seq": across_y},
                device_id_type=pl.DeviceIdType.MESH,
            )
        )
        second_relay.append(
            pltpu.make_async_remote_copy(
                src_ref=grad.at[:, at],
                dst_ref=relay.at[i],
                send_sem=prev_send.at[c],
                recv_sem=relay_recv.at[i],
                device_id={"section": (section + 3) % 4},
                device_id_type=pl.DeviceIdType.MESH,
            )
        )
        third_relay.append(
            pltpu.make_async_remote_copy(
                src_ref=relay.at[i],
                dst_ref=pg_hbm.at[0, :, at],
                send_sem=relay_send.at[i],
                recv_sem=prev_recv.at[c],
                device_id={"section": (section + 2) % 4, "seq": across_y},
                device_id_type=pl.DeviceIdType.MESH,
            )
        )

    def back_through_norm():
        back_all = back[...]
        along = jnp.sum(back_all.astype(f32) * acc[ROWS:, :], axis=1, keepdims=True)
        along = along * (inv_src * inv_src) * (1.0 / D)
        for c in range(BACK_STEPS):
            at = columns_at(c)
            w = jnp.concatenate(
                [wqkv[2 * c : 2 * c + 2, g].reshape(BACK_COLS, HD) for g in range(QKV // HD)],
                axis=1,
            )
            u = nt(back_all, w) * gain[:, at]
            grad[:, at] = (
                cot[:, at].astype(f32) + inv_src * u - src[:, at].astype(f32) * along
            ).astype(bf16)
            if c in ROUND:
                pl.when(section == 2)(first_relay[ROUND.index(c)].start)
                pl.when(section != 2)(prev_copies[c].start)
            else:
                prev_copies[c].start()

    def pass_on():
        for arriving, leaving in zip(first_relay, second_relay):
            arriving.wait_recv()
            leaving.start()

    def pass_on_last():
        for arriving, leaving in zip(second_relay, third_relay):
            arriving.wait_recv()
            leaving.start()

    pl.when(has_back)(back_through_norm)
    pl.when(section == 2)(output_late)
    pl.when(section == 0)(pass_on)
    pl.when(is_last)(pass_on_last)

    g1.finish(wqkv.at[pl.ds(0, SEQ - 1)])
    g2.finish(wout.at[pl.ds(0, SEQ - 1)])
    pl.when(in_prompt)(each([along_z(dz) for dz in (1, 3, 2)], "wait_send"))
    for copy in kv_sent:
        copy.wait_send()
    def keys_sent():
        for side in range(2):

            def sent_on(there, carry, side=side):
                pl.when(there != own)(to_summer(side, there).wait_send)
                return carry

            lax.fori_loop(0, 8, sent_on, 0)
            pl.when(z != side)(column_copy(side).wait_send)
        pl.when(in_answer)(to_partner.wait_send)

    pl.when(sends_keys)(keys_sent)
    pl.when(not_last)(each(next_copies, "wait_send"))
    pl.when(section > 0)(each(next_copies, "wait_recv"))
    straight = [prev_copies[c] for c in range(BACK_STEPS) if c not in ROUND]
    around = [prev_copies[c] for c in ROUND]
    pl.when(has_back)(each(straight, "wait_send"))
    pl.when(jnp.logical_and(has_back, section != 2))(each(around, "wait_send"))
    pl.when(section == 2)(each(first_relay, "wait_send"))
    pl.when(section == 0)(each(second_relay, "wait_send"))
    pl.when(is_last)(each(third_relay, "wait_send"))
    pl.when(not_last)(each(prev_copies, "wait_recv"))


def angle_tables():
    frequency = ROPE_BASE ** (-2.0 * np.arange(HD // 2) / HD)

    def table(positions):
        angles = np.asarray(positions, np.float64)[:, None] * frequency[None, :]
        cosine, sine = np.cos(angles), np.sin(angles)
        return (
            np.concatenate([cosine, cosine], axis=1).astype(np.float32),
            np.concatenate([-sine, sine], axis=1).astype(np.float32),
        )

    within = table(np.arange(BLK))
    blocks = [part[:, None, :] for part in table(np.arange(PBLK + 2) * BLK)]
    return (*within, *blocks)


def per_device(
    hidden_in,
    saved_hidden,
    grad_in,
    norm_gain,
    w_query,
    w_key,
    w_value,
    w_out,
    head,
    block_table,
    resp_lengths,
    pairs,
):
    any_spec = pl.BlockSpec(memory_space=pl.ANY)
    vmem = pl.BlockSpec(memory_space=pltpu.VMEM)
    smem = pl.BlockSpec(memory_space=pltpu.SMEM)
    dma = pltpu.SemaphoreType.DMA
    out = jax.ShapeDtypeStruct((1, ROWS, D), bf16)
    next_hidden, prev_grad = pl.pallas_call(
        layer_kernel,
        out_shape=(out, out),
        in_specs=[smem] * 3 + [any_spec] * 7 + [vmem] * 6,
        out_specs=(any_spec, any_spec),
        scratch_shapes=[
            pltpu.SMEM((PBLK + 2,), jnp.int32),
            pltpu.VMEM((ROWS, D), bf16),
            pltpu.VMEM((ROWS, D), bf16),
            pltpu.VMEM((ROWS, D), bf16),
            pltpu.VMEM((SEQ, 2 * ROWS, 256), bf16),
            pltpu.VMEM((SEQ, QKV // HD, 256, HD), bf16),
            pltpu.VMEM((SEQ, 16, D), bf16),
            pltpu.VMEM((2 * ROWS, QKV), f32),
            pltpu.VMEM((2, QH * ROWS, HD), bf16),
            pltpu.VMEM((2, 8, BLK, 512), bf16),
            pltpu.VMEM((2, BLK, 512), bf16),
            pltpu.VMEM((2, ROWS, QH * HD), bf16),
            pltpu.VMEM((ROWS, D), bf16),
            pltpu.VMEM((ROWS, 128), f32),
            pltpu.VMEM((ROWS, 128), f32),
            pltpu.VMEM((QH * HD, ROWS), f32),
            pltpu.VMEM((QH * ROWS, HD), bf16),
            pltpu.VMEM((2, 8, BLK, 256), bf16),
            pltpu.VMEM((2, BLK, 256), bf16),
            pltpu.VMEM((8, 2, BLK, 256), bf16),
            pltpu.VMEM((BLK, 256), bf16),
            pltpu.VMEM((2, BLK, 256), bf16),
            pltpu.VMEM((4, BLK, 256), bf16),
            pltpu.VMEM((2, 8, 8, 128), f32),
            pltpu.VMEM((ROWS, QKV), bf16),
            pltpu.VMEM((ROWS, D), bf16),
            pltpu.VMEM((len(ROUND), ROWS, BACK_COLS), bf16),
            dma((10,)),
            dma((2,)),
            dma((240,)),
            dma((160,)),
            dma((4,)),
            dma((2,)),
            dma((32,)),
            dma((32,)),
            dma((2,)),
            dma((16,)),
            dma((16,)),
            dma((2,)),
            dma((2,)),
            dma((4,)),
            dma((8,)),
            dma((9,)),
            dma((OUT_STEPS,)),
            dma((OUT_STEPS,)),
            dma((BACK_STEPS,)),
            dma((BACK_STEPS,)),
            dma((len(ROUND),)),
            dma((len(ROUND),)),
        ],
        compiler_params=pltpu.CompilerParams(
            collective_id=0, has_side_effects=True, vmem_limit_bytes=60 * 1024 * 1024
        ),
        cost_estimate=pl.CostEstimate(
            flops=12_000_000_000, bytes_accessed=12_000_000, transcendentals=4_000_000
        ),
    )(
        block_table,
        resp_lengths,
        pairs.T,
        hidden_in,
        saved_hidden,
        grad_in,
        w_query,
        w_key,
        w_value,
        w_out,
        norm_gain,
        head.reshape(D // 128, 128),
        *angle_tables(),
    )
    section = lax.axis_index("section")
    nothing = jnp.zeros((), bf16)
    return (
        jnp.where(section == 0, nothing, next_hidden),
        jnp.where(section == SECTIONS - 1, nothing, prev_grad),
    )


def solution(mesh):
    rows = P("section", "seq", None)
    return jax.shard_map(
        per_device,
        mesh=mesh,
        in_specs=(rows, rows, rows, P("section", None), rows, rows, rows, rows, P(), P(), P(), P()),
        out_specs=(rows, rows),
        check_vma=False,
    )
```
